256 devices in a mesh: group: 32 (over z, y), row: 8 (over x, core).
Axes of the slice: x: 4, y: 4, z: 8, core: 2. Of those that a mesh axis runs over, the one named last changes fastest.
Arguments:
- frames: bfloat16 [192, 32, 32, 384], P('group', 'row'), may hold values from -30 to 30
- clip_lengths: int32 [3], replicated, may hold values from 8 to 44, as said below
- group_start: int32 [32], P('group'), may hold values from 0 to 94, as said below
- group_count: int32 [32], P('group'), may hold values from 2 to 6, as said below
- kernel_one: bfloat16 [3, 3, 3, 384, 384], P(None, None, None, 'group'), may hold values from -0.0625 to 0.0625
- kernel_two: bfloat16 [3, 3, 3, 384, 384], P(None, None, None, 'group'), may hold values from -0.0625 to 0.0625
- gain_one: float32 [384], replicated, may hold values from 0.1 to 1.9
- gain_two: float32 [384], replicated, may hold values from 0.1 to 1.9
Outputs:
- decoded: bfloat16 [192, 32, 32, 384], P('group', 'row')
The draws below stay inside these ranges and needn't reach their ends.
Inputs may be any that keep to these rules, and one draw needn't show every extreme that they name: group_start is the exclusive prefix sum of group_count over the devices. `group_count`: a quarter of the devices, never the last one, hold 6 frames, the others 2; the counts sum to 96. `clip_lengths`: one clip has exactly 44 frames; the three sum to 96.
All inputs are finite; a program needn't handle non-finite values.
Results may differ from the reference program's by a relative error of at most 0.0029.
Values may be sent and summed in bfloat16 or wider, within the bound.
No kernel may reach another device: no remote copies, remote signals or barrier semaphores. Data moves between devices by JAX's collectives and lax.ppermute only.
A program may use at most 128 MiB of HBM per device.

```python
import math
import jax
import jax.numpy as jnp
from jax import lax

C = 384
COLS = 32
CAP = 6
H = 32
SLOTS = 192
TOTAL_FRAMES = 96
CLIP_MOST = 44
N_GROUP = 32


def group_layout(key):
    order = jax.random.permutation(key, N_GROUP - 1)
    pattern = jnp.where(jnp.arange(N_GROUP - 1) < N_GROUP // 4, CAP, 2).astype(jnp.int32)
    counts = jnp.concatenate([jnp.take(pattern, order), jnp.full((1,), 2, jnp.int32)]).astype(jnp.int32)
    starts = (jnp.cumsum(counts) - counts).astype(jnp.int32)
    return (counts, starts)


def draw_group_count(key, part):
    return group_layout(key)[0]


def draw_group_start(key, part):
    return group_layout(key)[1]


def draw_clip_lengths(key, part):
    key = jax.random.fold_in(key, 13)
    pick_key, order_key = jax.random.split(key)
    remain = TOTAL_FRAMES - CLIP_MOST
    first = jax.random.randint(pick_key, (), remain - CLIP_MOST, CLIP_MOST + 1).astype(jnp.int32)
    lengths = jnp.stack([jnp.full((), CLIP_MOST, jnp.int32), first, (remain - first).astype(jnp.int32)])
    order = jax.random.permutation(order_key, 3)
    return jnp.take(lengths, order).astype(jnp.int32)


def draw_frames(key, part):
    key = jax.random.fold_in(key, 7)
    base_key, rough_key, channel_key = jax.random.split(key, 3)
    dims = (SLOTS, H, COLS, C)
    row_pos = jnp.arange(H).astype(jnp.float32) / (H - 1)
    rising = jnp.exp(row_pos * math.log(3.0))
    roughness = jnp.exp(jax.random.uniform(rough_key, (SLOTS, H, 1, 1), jnp.float32, 0.0, math.log(3.2)))
    channel_scale = jnp.exp(jax.random.uniform(channel_key, (C,), jnp.float32, math.log(0.1), 0.0))
    base = jnp.clip(jax.random.normal(base_key, dims, jnp.float32), -3.0, 3.0)
    values = base * rising[None, :, None, None] * roughness * channel_scale
    return values.astype(jnp.bfloat16)


def levels(own_key, shape, pieces, smallest, largest):
    loudness = 1.0
    for dim, parts in pieces:
        heights = jax.random.uniform(jax.random.fold_in(jax.random.fold_in(own_key, 6), dim), (parts,), jnp.float32, smallest / len(pieces), largest / len(pieces))
        loudness = loudness * jnp.repeat(jnp.exp(heights), shape[dim] // parts).reshape((-1,) + (1,) * (len(shape) - 1 - dim))
    return loudness


def scatter_about(key, shape, width, most, pieces=(), held_as=jnp.bfloat16):
    drawn = width * jax.random.normal(key, shape, jnp.float32)
    if pieces:
        drawn = drawn * levels(key, shape, pieces, -0.22, 0.18)
    return jnp.clip(drawn, -most, most).astype(held_as)


def setup_inputs(seed: int = 0) -> dict:
    keys = jax.random.split(jax.random.key(seed), 9)
    return {
        "frames": draw_frames(jax.random.fold_in(keys[8], 71), 0),
        "clip_lengths": draw_clip_lengths(jax.random.fold_in(keys[8], 71), 0),
        "group_start": draw_group_start(jax.random.fold_in(keys[8], 71), 0),
        "group_count": draw_group_count(jax.random.fold_in(keys[8], 71), 0),
        "kernel_one": scatter_about(keys[4], (3, 3, 3, C, C), (27 * C) ** -0.5, 0.0625, ((3, 32),)),
        "kernel_two": scatter_about(keys[5], (3, 3, 3, C, C), (27 * C) ** -0.5, 0.0625, ((3, 32),)),
        "gain_one": jnp.clip(1.0 + 0.18 * jax.random.normal(keys[6], (C,), jnp.float32), 0.1, 1.9),
        "gain_two": jnp.clip(1.0 + 0.18 * jax.random.normal(keys[7], (C,), jnp.float32), 0.1, 1.9),
    }


def norm_act(values, gain):
    data = values.astype(jnp.float32)
    mean_square = lax.optimization_barrier(jnp.mean(data * data, axis=-1, keepdims=True))
    scaled = data * lax.rsqrt(mean_square + 1e-06)
    return jax.nn.silu(scaled * gain).astype(jnp.bfloat16)

def causal_conv(acts, kernel, position):
    data = acts.astype(jnp.float32)
    frames_n = data.shape[0]
    summed = jnp.zeros(data.shape, jnp.float32)
    for lag_index in range(3):
        lag = 2 - lag_index
        if lag > 0:
            shifted = jnp.concatenate([jnp.zeros((lag,) + data.shape[1:], jnp.float32), data[:frames_n - lag]], 0)
        else:
            shifted = data
        contrib = lax.conv_general_dilated(shifted, kernel[lag_index].astype(jnp.float32), (1, 1), ((1, 1), (1, 1)), dimension_numbers=('NHWC', 'HWIO', 'NHWC'))
        keep_frame = (position >= lag).astype(jnp.float32)
        summed = summed + keep_frame[:, None, None, None] * contrib
    return summed

def reference(frames, clip_lengths, group_start, group_count, kernel_one, kernel_two, gain_one, gain_two):
    frame_index = jnp.arange(TOTAL_FRAMES, dtype=jnp.int32)
    owner = lax.optimization_barrier(jnp.sum((group_start[None, :] <= frame_index[:, None]).astype(jnp.int32), axis=1)) - 1
    slot_ids = (owner * CAP + frame_index - jnp.take(group_start, owner)).astype(jnp.int32)
    seq = jnp.take(frames, slot_ids, axis=0)
    ends = jnp.cumsum(clip_lengths).astype(jnp.int32)
    begins = lax.optimization_barrier(jnp.max(jnp.where(ends[None, :] <= frame_index[:, None], ends[None, :], 0), axis=1)).astype(jnp.int32)
    position = frame_index - begins
    act_one = norm_act(seq, gain_one)
    middle = causal_conv(act_one, kernel_one, position)
    act_two = norm_act(middle, gain_two)
    result = seq.astype(jnp.float32) + causal_conv(act_two, kernel_two, position)
    slot_all = jnp.arange(SLOTS, dtype=jnp.int32)
    device_of = (slot_all // CAP).astype(jnp.int32)
    within = slot_all - device_of * CAP
    live_slot = within < jnp.take(group_count, device_of)
    source = jnp.minimum(jnp.take(group_start, device_of) + within, TOTAL_FRAMES - 1).astype(jnp.int32)
    picked = jnp.take(result, source, axis=0)
    return jnp.where(live_slot[:, None, None, None], picked, 0.0).astype(jnp.bfloat16)
```

```python
import jax
import jax.numpy as jnp
import numpy as np
from jax import lax
from jax.experimental import pallas as pl
from jax.experimental.pallas import tpu as pltpu
from jax.sharding import Mesh
from jax.sharding import PartitionSpec as P

NZ, NY, NX, NC = 8, 4, 4, 2
AXES = ("z", "y", "x", "c")
C = 384
SHARD = 12
HALF = 14
BUNDLE = 96
ROUND = (0, 1, -1, 2)

FETCH = np.array(
    [
        [[4, 0], [1, 3], [-1, -3], [2, -2]],
        [[4, 0], [-1, -3], [1, 3], [-2, 2]],
    ]
)


def number(z, y, x, c):
    return ((z % NZ * NY + y % NY) * NX + x % NX) * NC + c


def fetch(array, source_of):
    pairs = []
    for z in range(NZ):
        for y in range(NY):
            for x in range(NX):
                for c in range(NC):
                    source = source_of(z, y, x, c)
                    if source is not None:
                        pairs.append((number(*source), number(z, y, x, c)))
    return lax.ppermute(array, AXES, pairs)


def small_source(step):
    return lambda z, y, x, c: (z, y, x + step, c) if c == 0 else (z, y + step, x, c)


def bulk_source(step):
    return lambda z, y, x, c: (z, y + step, x, c) if c == 0 else (z, y, x + step, c)


def z_source(which):
    return lambda z, y, x, c: (z + int(FETCH[c, x, which]), y, x, c)


def sibling(z, y, x, c):
    return (z, y, x, 1 - c)


def own_half(kernel):
    start = lax.axis_index("c") * (27 - HALF)
    taps = lax.dynamic_slice_in_dim(kernel.reshape(27, SHARD, C), start, HALF, 0)
    return taps.reshape(HALF * SHARD, C)


def pieces_along_z(own):
    return jnp.stack([fetch(own, z_source(0)), fetch(own, z_source(1))])


def small_stage(two):
    parts = [two] + [fetch(two, small_source(step)) for step in ROUND[1:]]
    return jnp.stack(parts)


def join_rows(parts):
    parts = parts.reshape(8, HALF, SHARD, C)
    return jnp.transpose(parts, (1, 0, 2, 3)).reshape(HALF, BUNDLE, C)


def bulk_stage(bundle):
    return [bundle] + [fetch(bundle, bulk_source(step)) for step in ROUND[1:]]


def channel_orders():
    z, y, x = (lax.axis_index(a) for a in ("z", "y", "x"))
    table = jnp.asarray(FETCH, jnp.int32)
    step = jnp.array(ROUND, jnp.int32)
    at_x = (x + step) % NX
    at_y = (y + step) % NY
    orders = []
    for half in range(2):
        at_z = (z + table[half][at_x]) % NZ
        group = at_z[None, :, :] * NY + at_y[:, None, None]
        if half == 1:
            group = jnp.transpose(group, (1, 0, 2))
        channel = group.reshape(-1, 1) * SHARD + jnp.arange(SHARD, dtype=jnp.int32)
        orders.append(channel.reshape(C))
    return jnp.stack(orders)


def conv_body(
    scalars, lag_weights, acts, order, tail, own0, own1, own2, own3, got0, got1, got2, got3,
    out, spread, weights, total, sems, *, finish,
):
    frames, rows, cols = 6, 4, 32
    own, got = (own0, own1, own2, own3), (got0, got1, got2, got3)

    def copies(half, sources):
        return [
            pltpu.make_async_copy(
                sources[k], weights.at[half, :, pl.ds(BUNDLE * k, BUNDLE), :], sems.at[half, k]
            )
            for k in range(4)
        ]

    core = scalars[0]

    @pl.when(core == 0)
    def _():
        for copy in copies(0, own) + copies(1, got):
            copy.start()

    @pl.when(core == 1)
    def _():
        for copy in copies(0, got) + copies(1, own):
            copy.start()

    wide = acts.shape[0] * acts.shape[1]
    col = lax.broadcasted_iota(jnp.int32, (wide * cols, C), 0) % cols
    for half in range(2):
        pick = (
            lax.broadcasted_iota(jnp.int32, (C, C), 0) == order[half : half + 1, :]
        ).astype(jnp.bfloat16)
        plain = jnp.dot(
            acts[...].reshape(wide * cols, C), pick, preferred_element_type=jnp.float32
        )
        before = jnp.where(col == 0, 0.0, pltpu.roll(plain, 1, 0))
        after = jnp.where(col == cols - 1, 0.0, pltpu.roll(plain, wide * cols - 1, 0))
        for tap, moved in enumerate((before, plain, after)):
            spread[half, :, :, :, pl.ds(C * tap, C)] = (
                moved.astype(jnp.bfloat16).reshape(acts.shape)
            )

    total[...] = jnp.zeros_like(total)

    def window(half, lag, row, first, count):
        block = spread[half, pl.ds(lag, frames), pl.ds(row, rows), :, pl.ds(C * first, C * count)]
        return block.reshape(frames * rows * cols, C * count)

    def add(lag, part):
        part = part.reshape(frames, rows * cols, C)
        for f in range(frames):
            total[f] += part[f] * lag_weights[lag, f]

    def group(half, first_tap, index):
        lag, row = index // 3, index % 3
        block = weights[half, pl.ds(index * 3 - first_tap, 3)].reshape(3 * C, C)
        add(lag, jnp.dot(window(half, lag, row, 0, 3), block, preferred_element_type=jnp.float32))

    for copy in copies(0, own):
        copy.wait()

    @pl.loop(0, 4)
    def _(index):
        group(0, 0, index)

    add(
        1,
        jnp.dot(
            window(0, 1, 1, 0, 2),
            weights[0, pl.ds(12, 2)].reshape(2 * C, C),
            preferred_element_type=jnp.float32,
        ),
    )
    for copy in copies(1, own):
        copy.wait()
    add(
        1,
        jnp.dot(window(1, 1, 1, 2, 1), weights[1, 1], preferred_element_type=jnp.float32),
    )

    @pl.loop(5, 9)
    def _(index):
        group(1, 13, index)

    finish(scalars, total, tail, out)


def finish_norm(scalars, total, tail, out):
    for f in range(6):
        data = total[f]
        scale = lax.rsqrt(jnp.mean(data * data, axis=-1, keepdims=True) + 1e-06)
        lifted = data * scale * tail[...]
        out[f] = (lifted * (1.0 / (1.0 + jnp.exp(-lifted)))).astype(jnp.bfloat16)


def finish_add(scalars, total, tail, out):
    for f in range(6):
        summed = tail[f].astype(jnp.float32) + total[f]
        out[f] = jnp.where(f < scalars[1], summed, 0.0).astype(jnp.bfloat16)


def conv(scalars, lag_weights, acts, orders, tail, own, got, finish):
    smem = pl.BlockSpec(memory_space=pltpu.SMEM)
    vmem = pl.BlockSpec(memory_space=pltpu.VMEM)
    return pl.pallas_call(
        lambda *refs: conv_body(*refs, finish=finish),
        out_shape=jax.ShapeDtypeStruct((6, 128, C), jnp.bfloat16),
        in_specs=[smem, smem, vmem, vmem, vmem] + [pl.BlockSpec(memory_space=pl.ANY)] * 8,
        out_specs=vmem,
        scratch_shapes=[
            pltpu.VMEM((2, 8, 6, 32, 3 * C), jnp.bfloat16),
            pltpu.VMEM((2, HALF, C, C), jnp.bfloat16),
            pltpu.VMEM((6, 128, C), jnp.float32),
            pltpu.SemaphoreType.DMA((2, 4)),
        ],
        compiler_params=pltpu.CompilerParams(vmem_limit_bytes=44 * 1024 * 1024),
        cost_estimate=pl.CostEstimate(
            flops=2 * 768 * 27 * C * C, bytes_accessed=12_000_000, transcendentals=768 * C
        ),
    )(scalars, lag_weights, acts, orders, tail, *own, *got)


def clip_positions(clip_lengths, frame_index):
    ends = jnp.cumsum(clip_lengths)
    begins = jnp.max(jnp.where(ends[None, :] <= frame_index[:, None], ends[None, :], 0), axis=1)
    return frame_index - begins


def norm_act(values, gain):
    data = values.astype(jnp.float32)
    mean_square = jnp.mean(data * data, axis=-1, keepdims=True)
    scaled = data * lax.rsqrt(mean_square + 1e-06)
    return jax.nn.silu(scaled * gain).astype(jnp.bfloat16)


def before_in_group(z, y, x, c):
    group = z * NY + y - 1
    return None if group < 0 else (group // NY, group % NY, x, c)


def row_neighbour(by):
    def source(z, y, x, c):
        row = x * NC + c + by
        return (z, y, row // NC, row % NC) if 0 <= row < NX * NC else None

    return source


def per_device(
    frames, clip_lengths, group_start, group_count, kernel_one, kernel_two, gain_one, gain_two
):
    slots = frames.shape[0]
    slot = jnp.arange(slots, dtype=jnp.int32)
    position = clip_positions(clip_lengths, group_start[0] + slot)
    lag_weights = jnp.stack([position >= 2, position >= 1, position >= 0]).astype(jnp.float32)
    scalars = jnp.stack([lax.axis_index("c").astype(jnp.int32), group_count[0]])
    orders = channel_orders()

    def extend(acts):
        last_two = lax.dynamic_slice_in_dim(acts, group_count[0] - 2, 2, 0)
        carried = fetch(last_two, before_in_group)
        acts = jnp.concatenate([carried, acts], 0)
        above = fetch(acts[:, 3:4], row_neighbour(-1))
        below = fetch(acts[:, 0:1], row_neighbour(1))
        return jnp.concatenate([above, acts, below], 1)

    one = pieces_along_z(own_half(kernel_one))
    one_parts = small_stage(one)
    one_bundles = bulk_stage(join_rows(one_parts))
    one_others = [fetch(b, sibling) for b in one_bundles]

    own_two, _ = lax.optimization_barrier((own_half(kernel_two), one))
    two = pieces_along_z(own_two)
    two, _ = lax.optimization_barrier((two, one_parts))
    two_bundle = join_rows(small_stage(two))
    two_bundle, _ = lax.optimization_barrier((two_bundle, one_bundles))
    two_bundles = bulk_stage(two_bundle)
    two_others = [fetch(b, sibling) for b in two_bundles]

    acts_one = extend(norm_act(frames, gain_one))
    acts_two = conv(
        scalars, lag_weights, acts_one, orders, gain_two.reshape(1, C),
        one_bundles, one_others, finish_norm,
    )
    acts_two = extend(acts_two.reshape(frames.shape))
    result = conv(
        scalars, lag_weights, acts_two, orders, frames.reshape(slots, 128, C),
        two_bundles, two_others, finish_add,
    )
    return result.reshape(frames.shape)


def solution(mesh):
    torus = Mesh(mesh.devices.reshape(NZ, NY, NX, NC), AXES)
    group, row = ("z", "y"), ("x", "c")
    return jax.shard_map(
        per_device,
        mesh=torus,
        in_specs=(
            P(group, row, None, None),
            P(),
            P(group),
            P(group),
            P(None, None, None, group, None),
            P(None, None, None, group, None),
            P(),
            P(),
        ),
        out_specs=P(group, row, None, None),
        check_vma=False,
    )
```

```python
import jax
import jax.numpy as jnp
import numpy as np
from jax import lax
from jax.experimental import pallas as pl
from jax.experimental.pallas import tpu as pltpu
from jax.sharding import Mesh
from jax.sharding import PartitionSpec as P

NZ, NY, NX, NC = 8, 4, 4, 2
AXES = ("z", "y", "x", "c")
C = 384
SHARD = 12
HALF = 14
BUNDLE = 96
ROUND = (0, 1, -1, 2)

FETCH = np.array(
    [
        [[4, 0], [1, 3], [-1, -3], [2, -2]],
        [[4, 0], [-1, -3], [1, 3], [-2, 2]],
    ]
)


def number(z, y, x, c):
    return ((z % NZ * NY + y % NY) * NX + x % NX) * NC + c


def fetch(array, source_of):
    pairs = []
    for z in range(NZ):
        for y in range(NY):
            for x in range(NX):
                for c in range(NC):
                    source = source_of(z, y, x, c)
                    if source is not None:
                        pairs.append((number(*source), number(z, y, x, c)))
    return lax.ppermute(array, AXES, pairs)


def small_source(step):
    return lambda z, y, x, c: (z, y, x + step, c) if c == 0 else (z, y + step, x, c)


def bulk_source(step):
    return lambda z, y, x, c: (z, y + step, x, c) if c == 0 else (z, y, x + step, c)


def z_source(which):
    return lambda z, y, x, c: (z + int(FETCH[c, x, which]), y, x, c)


def sibling(z, y, x, c):
    return (z, y, x, 1 - c)


def own_halves(kernels):
    start = lax.axis_index("c") * (27 - HALF)
    return jnp.stack(
        [
            lax.dynamic_slice_in_dim(k.reshape(27, SHARD, C), start, HALF, 0).reshape(
                HALF * SHARD, C
            )
            for k in kernels
        ]
    )


def join_rows(parts):
    parts = parts.reshape(8, HALF, SHARD, C)
    return jnp.transpose(parts, (1, 0, 2, 3)).reshape(HALF, BUNDLE, C)


def gather_bundles(kernels):
    own = own_halves(kernels)
    first = fetch(own, z_source(0))
    second = fetch(own, z_source(1))
    two = jnp.stack([first, second], 1)
    near = [fetch(two, small_source(step)) for step in ROUND[1:]]
    parts = jnp.stack([two] + near, 1)
    return [join_rows(parts[0]), join_rows(parts[1])]


def bulk_stage(bundle):
    return [bundle] + [fetch(bundle, bulk_source(step)) for step in ROUND[1:]]


def channel_orders():
    z, y, x = (lax.axis_index(a) for a in ("z", "y", "x"))
    table = jnp.asarray(FETCH, jnp.int32)
    step = jnp.array(ROUND, jnp.int32)
    at_x = (x + step) % NX
    at_y = (y + step) % NY
    orders = []
    for half in range(2):
        at_z = (z + table[half][at_x]) % NZ
        group = at_z[None, :, :] * NY + at_y[:, None, None]
        if half == 1:
            group = jnp.transpose(group, (1, 0, 2))
        channel = group.reshape(-1, 1) * SHARD + jnp.arange(SHARD, dtype=jnp.int32)
        orders.append(channel.reshape(C))
    return jnp.stack(orders)


def conv_body(
    scalars, lag_weights, acts, order, tail, own0, own1, own2, own3, got0, got1, got2, got3,
    out, spread, weights, total, sems, *, finish,
):
    frames, rows, cols = 6, 4, 32
    own, got = (own0, own1, own2, own3), (got0, got1, got2, got3)

    def copies(half, sources):
        return [
            pltpu.make_async_copy(
                sources[k], weights.at[half, :, pl.ds(BUNDLE * k, BUNDLE), :], sems.at[half, k]
            )
            for k in range(4)
        ]

    core = scalars[0]

    @pl.when(core == 0)
    def _():
        for copy in copies(0, own) + copies(1, got):
            copy.start()

    @pl.when(core == 1)
    def _():
        for copy in copies(0, got) + copies(1, own):
            copy.start()

    wide = acts.shape[0] * acts.shape[1]
    col = lax.broadcasted_iota(jnp.int32, (wide * cols, C), 0) % cols
    for half in range(2):
        pick = (
            lax.broadcasted_iota(jnp.int32, (C, C), 0) == order[half : half + 1, :]
        ).astype(jnp.bfloat16)
        plain = jnp.dot(
            acts[...].reshape(wide * cols, C), pick, preferred_element_type=jnp.float32
        )
        before = jnp.where(col == 0, 0.0, pltpu.roll(plain, 1, 0))
        after = jnp.where(col == cols - 1, 0.0, pltpu.roll(plain, wide * cols - 1, 0))
        for tap, moved in enumerate((before, plain, after)):
            spread[half, :, :, :, pl.ds(C * tap, C)] = (
                moved.astype(jnp.bfloat16).reshape(acts.shape)
            )

    total[...] = jnp.zeros_like(total)

    def window(half, lag, row, first, count):
        block = spread[half, pl.ds(lag, frames), pl.ds(row, rows), :, pl.ds(C * first, C * count)]
        return block.reshape(frames * rows * cols, C * count)

    def add(lag, part):
        part = part.reshape(frames, rows * cols, C)
        for f in range(frames):
            total[f] += part[f] * lag_weights[lag, f]

    def group(half, first_tap, index):
        lag, row = index // 3, index % 3
        block = weights[half, pl.ds(index * 3 - first_tap, 3)].reshape(3 * C, C)
        add(lag, jnp.dot(window(half, lag, row, 0, 3), block, preferred_element_type=jnp.float32))

    for copy in copies(0, own):
        copy.wait()

    @pl.loop(0, 4)
    def _(index):
        group(0, 0, index)

    add(
        1,
        jnp.dot(
            window(0, 1, 1, 0, 2),
            weights[0, pl.ds(12, 2)].reshape(2 * C, C),
            preferred_element_type=jnp.float32,
        ),
    )
    for copy in copies(1, own):
        copy.wait()
    add(
        1,
        jnp.dot(window(1, 1, 1, 2, 1), weights[1, 1], preferred_element_type=jnp.float32),
    )

    @pl.loop(5, 9)
    def _(index):
        group(1, 13, index)

    finish(scalars, total, tail, out)


def finish_norm(scalars, total, tail, out):
    for f in range(6):
        data = total[f]
        scale = lax.rsqrt(jnp.mean(data * data, axis=-1, keepdims=True) + 1e-06)
        lifted = data * scale * tail[...]
        out[f] = (lifted * (1.0 / (1.0 + jnp.exp(-lifted)))).astype(jnp.bfloat16)


def finish_add(scalars, total, tail, out):
    for f in range(6):
        summed = tail[f].astype(jnp.float32) + total[f]
        out[f] = jnp.where(f < scalars[1], summed, 0.0).astype(jnp.bfloat16)


def conv(scalars, lag_weights, acts, orders, tail, own, got, finish):
    smem = pl.BlockSpec(memory_space=pltpu.SMEM)
    vmem = pl.BlockSpec(memory_space=pltpu.VMEM)
    return pl.pallas_call(
        lambda *refs: conv_body(*refs, finish=finish),
        out_shape=jax.ShapeDtypeStruct((6, 128, C), jnp.bfloat16),
        in_specs=[smem, smem, vmem, vmem, vmem] + [pl.BlockSpec(memory_space=pl.ANY)] * 8,
        out_specs=vmem,
        scratch_shapes=[
            pltpu.VMEM((2, 8, 6, 32, 3 * C), jnp.bfloat16),
            pltpu.VMEM((2, HALF, C, C), jnp.bfloat16),
            pltpu.VMEM((6, 128, C), jnp.float32),
            pltpu.SemaphoreType.DMA((2, 4)),
        ],
        compiler_params=pltpu.CompilerParams(vmem_limit_bytes=44 * 1024 * 1024),
        cost_estimate=pl.CostEstimate(
            flops=2 * 768 * 27 * C * C, bytes_accessed=12_000_000, transcendentals=768 * C
        ),
    )(scalars, lag_weights, acts, orders, tail, *own, *got)


def clip_positions(clip_lengths, frame_index):
    ends = jnp.cumsum(clip_lengths)
    begins = jnp.max(jnp.where(ends[None, :] <= frame_index[:, None], ends[None, :], 0), axis=1)
    return frame_index - begins


def norm_act(values, gain):
    data = values.astype(jnp.float32)
    mean_square = jnp.mean(data * data, axis=-1, keepdims=True)
    scaled = data * lax.rsqrt(mean_square + 1e-06)
    return jax.nn.silu(scaled * gain).astype(jnp.bfloat16)


def before_in_group(z, y, x, c):
    group = z * NY + y - 1
    return None if group < 0 else (group // NY, group % NY, x, c)


def row_neighbour(by):
    def source(z, y, x, c):
        row = x * NC + c + by
        return (z, y, row // NC, row % NC) if 0 <= row < NX * NC else None

    return source


def per_device(
    frames, clip_lengths, group_start, group_count, kernel_one, kernel_two, gain_one, gain_two
):
    slots = frames.shape[0]
    slot = jnp.arange(slots, dtype=jnp.int32)
    position = clip_positions(clip_lengths, group_start[0] + slot)
    lag_weights = jnp.stack([position >= 2, position >= 1, position >= 0]).astype(jnp.float32)
    scalars = jnp.stack([lax.axis_index("c").astype(jnp.int32), group_count[0]])
    orders = channel_orders()

    def extend(acts):
        last_two = lax.dynamic_slice_in_dim(acts, group_count[0] - 2, 2, 0)
        carried = fetch(last_two, before_in_group)
        acts = jnp.concatenate([carried, acts], 0)
        above = fetch(acts[:, 3:4], row_neighbour(-1))
        below = fetch(acts[:, 0:1], row_neighbour(1))
        return jnp.concatenate([above, acts, below], 1)

    one_bundle, two_bundle = gather_bundles((kernel_one, kernel_two))
    one_bundles = bulk_stage(one_bundle)
    one_others = [fetch(b, sibling) for b in one_bundles]
    two_bundle, _ = lax.optimization_barrier((two_bundle, one_bundles[:3]))
    two_bundles = bulk_stage(two_bundle)
    two_others = [fetch(b, sibling) for b in two_bundles]

    acts_one = extend(norm_act(frames, gain_one))
    acts_two = conv(
        scalars, lag_weights, acts_one, orders, gain_two.reshape(1, C),
        one_bundles, one_others, finish_norm,
    )
    acts_two = extend(acts_two.reshape(frames.shape))
    result = conv(
        scalars, lag_weights, acts_two, orders, frames.reshape(slots, 128, C),
        two_bundles, two_others, finish_add,
    )
    return result.reshape(frames.shape)


def solution(mesh):
    torus = Mesh(mesh.devices.reshape(NZ, NY, NX, NC), AXES)
    group, row = ("z", "y"), ("x", "c")
    return jax.shard_map(
        per_device,
        mesh=torus,
        in_specs=(
            P(group, row, None, None),
            P(),
            P(group),
            P(group),
            P(None, None, None, group, None),
            P(None, None, None, group, None),
            P(),
            P(),
        ),
        out_specs=P(group, row, None, None),
        check_vma=False,
    )
```

```python
import jax
import jax.numpy as jnp
import numpy as np
from jax import lax
from jax.experimental import pallas as pl
from jax.experimental.pallas import tpu as pltpu
from jax.sharding import Mesh
from jax.sharding import PartitionSpec as P

NZ, NY, NX, NC = 8, 4, 4, 2
AXES = ("z", "y", "x", "c")
C = 384
SHARD = 12
HALF = 14
BUNDLE = 96
ROUND = (0, 1, -1, 2)

FETCH = np.array([[[4, 0], [1, 3], [-1, -3], [2, -2]], [[0, 4], [2, -2], [1, -3], [3, -1]]])


def number(z, y, x, c):
    return ((z % NZ * NY + y % NY) * NX + x % NX) * NC + c


def fetch(array, source_of):
    pairs = []
    for z in range(NZ):
        for y in range(NY):
            for x in range(NX):
                for c in range(NC):
                    source = source_of(z, y, x, c)
                    if source is not None:
                        pairs.append((number(*source), number(z, y, x, c)))
    return lax.ppermute(array, AXES, pairs)


def z_source(which):
    def source(z, y, x, c):
        odd = z % 2
        if c == 0:
            return (z + int(FETCH[0, x, which]), y + 2 * odd, x, c)
        return (z - odd + int(FETCH[1, (x + 2 * odd) % NX, which]), y, x, c)

    return source


def small_source(step):
    return lambda z, y, x, c: (z, y, x + step, c) if c == 0 else (z, y + step, x, c)


def bulk_source(step):
    if step == 2:
        return lambda z, y, x, c: (z + 1 if z % 2 != c else z - 1, y, x, c)
    return lambda z, y, x, c: (z, y + step, x, c) if c == 0 else (z, y, x + step, c)


def sibling(z, y, x, c):
    return (z, y, x, 1 - c)


def own_half(kernel):
    start = lax.axis_index("c") * (27 - HALF)
    taps = lax.dynamic_slice_in_dim(kernel.reshape(27, SHARD, C), start, HALF, 0)
    return taps.reshape(HALF * SHARD, C)


def z_stage(own):
    return jnp.stack([fetch(own, z_source(0)), fetch(own, z_source(1))])


def small_stage(two):
    return [two] + [fetch(two, small_source(step)) for step in ROUND[1:]]


def join_body(*refs):
    parts, out = refs[:-1], refs[-1]
    for tap in range(HALF):
        rows = [
            part[piece, pl.ds(SHARD * tap, SHARD), :].astype(jnp.float32)
            for part in parts
            for piece in range(2)
        ]
        out[tap] = jnp.concatenate(rows, 0).astype(jnp.bfloat16)


def join_rows(parts):
    vmem = pl.BlockSpec(memory_space=pltpu.VMEM)
    return pl.pallas_call(
        join_body,
        out_shape=jax.ShapeDtypeStruct((HALF, BUNDLE, C), jnp.bfloat16),
        in_specs=[vmem] * 4,
        out_specs=vmem,
        compiler_params=pltpu.CompilerParams(vmem_limit_bytes=16 * 1024 * 1024),
        cost_estimate=pl.CostEstimate(flops=0, bytes_accessed=2_000_000, transcendentals=0),
    )(*parts)


def bulk_stage(bundle):
    return [bundle] + [fetch(bundle, bulk_source(step)) for step in ROUND[1:]]


def channel_orders():
    z, y, x = (lax.axis_index(a) for a in ("z", "y", "x"))
    table = jnp.asarray(FETCH, jnp.int32)
    around = jnp.array(ROUND, jnp.int32)
    aside = jnp.array((0, 1, -1, 0), jnp.int32)
    odd = z % 2
    at_z = z + jnp.array((0, 0, 0, 1), jnp.int32) * jnp.where(odd == 1, 1, -1)
    piece_z = at_z[:, None, None] + table[0][(x + around) % NX][None, :, :]
    piece_y = (y + aside + 2 * (at_z % 2))[:, None, None]
    first = piece_z % NZ * NY + piece_y % NY
    at_z = z + jnp.array((0, 0, 0, 1), jnp.int32) * jnp.where(odd == 0, 1, -1)
    piece_z = (at_z - at_z % 2)[:, None] + table[1][(x + aside + 2 * (at_z % 2)) % NX]
    piece_y = y + around
    second = piece_z[:, None, :] % NZ * NY + piece_y[None, :, None] % NY
    ramp = jnp.arange(SHARD, dtype=jnp.int32)
    return jnp.stack([(half.reshape(-1, 1) * SHARD + ramp).reshape(C) for half in (first, second)])


def conv_body(
    scalars, lag_weights, carried, inner, beside, across, order, tail, own0, own1, own2, own3, got0, got1, got2, got3,
    out, acts, spread, weights, total, sems, *, finish,
):
    frames, rows, cols = 6, 4, 32
    own, got = (own0, own1, own2, own3), (got0, got1, got2, got3)

    def copies(half, sources):
        return [
            pltpu.make_async_copy(
                sources[k], weights.at[half, :, pl.ds(BUNDLE * k, BUNDLE), :], sems.at[half, k]
            )
            for k in range(4)
        ]

    core = scalars[0]

    @pl.when(core == 0)
    def _():
        for copy in copies(0, own) + copies(1, got):
            copy.start()

    @pl.when(core == 1)
    def _():
        for copy in copies(0, got) + copies(1, own):
            copy.start()

    acts[0:2, 1:5] = carried[...]
    acts[2:8, 1:5] = inner[...]

    @pl.when(core == 0)
    def _():
        acts[:, 0:1] = across[...]
        acts[:, 5:6] = beside[...]

    @pl.when(core == 1)
    def _():
        acts[:, 0:1] = beside[...]
        acts[:, 5:6] = across[...]

    wide = acts.shape[0] * acts.shape[1]
    col = lax.broadcasted_iota(jnp.int32, (wide * cols, C), 0) % cols
    for half in range(2):
        pick = (
            lax.broadcasted_iota(jnp.int32, (C, C), 0) == order[half : half + 1, :]
        ).astype(jnp.bfloat16)
        plain = jnp.dot(
            acts[...].reshape(wide * cols, C), pick, preferred_element_type=jnp.float32
        )
        before = jnp.where(col == 0, 0.0, pltpu.roll(plain, 1, 0))
        after = jnp.where(col == cols - 1, 0.0, pltpu.roll(plain, wide * cols - 1, 0))
        for tap, moved in enumerate((before, plain, after)):
            spread[half, :, :, :, pl.ds(C * tap, C)] = (
                moved.astype(jnp.bfloat16).reshape(acts.shape)
            )

    total[...] = jnp.zeros_like(total)

    def window(half, lag, row, first, count):
        block = spread[half, pl.ds(lag, frames), pl.ds(row, rows), :, pl.ds(C * first, C * count)]
        return block.reshape(frames * rows * cols, C * count)

    def add(lag, part):
        part = part.reshape(frames, rows * cols, C)
        for f in range(frames):
            total[f] += part[f] * lag_weights[lag, f]

    def group(half, first_tap, index):
        lag, row = index // 3, index % 3
        block = weights[half, pl.ds(index * 3 - first_tap, 3)].reshape(3 * C, C)
        add(lag, jnp.dot(window(half, lag, row, 0, 3), block, preferred_element_type=jnp.float32))

    for copy in copies(0, own):
        copy.wait()

    @pl.loop(0, 4)
    def _(index):
        group(0, 0, index)

    add(
        1,
        jnp.dot(
            window(0, 1, 1, 0, 2),
            weights[0, pl.ds(12, 2)].reshape(2 * C, C),
            preferred_element_type=jnp.float32,
        ),
    )
    for copy in copies(1, own):
        copy.wait()
    add(
        1,
        jnp.dot(window(1, 1, 1, 2, 1), weights[1, 1], preferred_element_type=jnp.float32),
    )

    @pl.loop(5, 9)
    def _(index):
        group(1, 13, index)

    finish(scalars, total, tail, out)


def finish_norm(scalars, total, tail, out):
    for f in range(6):
        data = total[f]
        scale = lax.rsqrt(jnp.mean(data * data, axis=-1, keepdims=True) + 1e-06)
        lifted = data * scale * tail[...]
        out[f] = (lifted * (1.0 / (1.0 + jnp.exp(-lifted)))).astype(jnp.bfloat16)


def finish_add(scalars, total, tail, out):
    for f in range(6):
        summed = tail[f].astype(jnp.float32) + total[f]
        out[f] = jnp.where(f < scalars[1], summed, 0.0).astype(jnp.bfloat16)


def conv(scalars, lag_weights, extended, orders, tail, own, got, finish):
    smem = pl.BlockSpec(memory_space=pltpu.SMEM)
    vmem = pl.BlockSpec(memory_space=pltpu.VMEM)
    return pl.pallas_call(
        lambda *refs: conv_body(*refs, finish=finish),
        out_shape=jax.ShapeDtypeStruct((6, 128, C), jnp.bfloat16),
        in_specs=[smem, smem] + [vmem] * 6 + [pl.BlockSpec(memory_space=pl.ANY)] * 8,
        out_specs=vmem,
        scratch_shapes=[
            pltpu.VMEM((8, 6, 32, C), jnp.bfloat16),
            pltpu.VMEM((2, 8, 6, 32, 3 * C), jnp.bfloat16),
            pltpu.VMEM((2, HALF, C, C), jnp.bfloat16),
            pltpu.VMEM((6, 128, C), jnp.float32),
            pltpu.SemaphoreType.DMA((2, 4)),
        ],
        compiler_params=pltpu.CompilerParams(vmem_limit_bytes=44 * 1024 * 1024),
        cost_estimate=pl.CostEstimate(
            flops=2 * 768 * 27 * C * C, bytes_accessed=12_000_000, transcendentals=768 * C
        ),
    )(scalars, lag_weights, *extended, orders, tail, *own, *got)


def clip_positions(clip_lengths, frame_index):
    ends = jnp.cumsum(clip_lengths)
    begins = jnp.max(jnp.where(ends[None, :] <= frame_index[:, None], ends[None, :], 0), axis=1)
    return frame_index - begins


def norm_act(values, gain):
    data = values.astype(jnp.float32)
    mean_square = jnp.mean(data * data, axis=-1, keepdims=True)
    scaled = data * lax.rsqrt(mean_square + 1e-06)
    return jax.nn.silu(scaled * gain).astype(jnp.bfloat16)


def before_in_group(z, y, x, c):
    group = z * NY + y - 1
    return None if group < 0 else (group // NY, group % NY, x, c)


def across_chips(z, y, x, c):
    x = x - 1 if c == 0 else x + 1
    return (z, y, x, 1 - c) if 0 <= x < NX else None


def across_and_before(z, y, x, c):
    place = across_chips(z, y, x, c)
    return None if place is None else before_in_group(*place)


def per_device(
    frames, clip_lengths, group_start, group_count, kernel_one, kernel_two, gain_one, gain_two
):
    slots = frames.shape[0]
    slot = jnp.arange(slots, dtype=jnp.int32)
    position = clip_positions(clip_lengths, group_start[0] + slot)
    lag_weights = jnp.stack([position >= 2, position >= 1, position >= 0]).astype(jnp.float32)
    scalars = jnp.stack([lax.axis_index("c").astype(jnp.int32), group_count[0]])
    orders = channel_orders()

    first_core = lax.axis_index("c") == 0
    last = group_count[0] - 2

    def extend(acts):
        outer = jnp.where(first_core, acts[:, 0:1], acts[:, 3:4])
        carried = fetch(lax.dynamic_slice_in_dim(acts, last, 2, 0), before_in_group)
        across = fetch(outer, across_chips)
        across_before = fetch(lax.dynamic_slice_in_dim(outer, last, 2, 0), across_and_before)
        edge = jnp.concatenate(
            [
                jnp.where(first_core, carried[:, 3:4], carried[:, 0:1]),
                jnp.where(first_core, acts[:, 3:4], acts[:, 0:1]),
            ],
            0,
        )
        beside = fetch(edge, sibling)
        return carried, acts, beside, jnp.concatenate([across_before, across], 0)

    one = z_stage(own_half(kernel_one))
    own_two, one = lax.optimization_barrier((own_half(kernel_two), one))
    one_parts = small_stage(one)
    two = z_stage(own_two)
    two, one_parts = lax.optimization_barrier((two, one_parts))
    one_bundles = bulk_stage(join_rows(one_parts))
    two_bundle = join_rows(small_stage(two))
    two_bundle, one_bundles = lax.optimization_barrier((two_bundle, one_bundles))
    one_others = [fetch(b, sibling) for b in one_bundles]
    two_bundles = bulk_stage(two_bundle)

    acts_two = conv(
        scalars, lag_weights, extend(norm_act(frames, gain_one)), orders, gain_two.reshape(1, C),
        one_bundles, one_others, finish_norm,
    ).reshape(frames.shape)
    two_bundles, acts_two = lax.optimization_barrier((two_bundles, acts_two))
    two_others = [fetch(b, sibling) for b in two_bundles]
    result = conv(
        scalars, lag_weights, extend(acts_two), orders, frames.reshape(slots, 128, C),
        two_bundles, two_others, finish_add,
    )
    return result.reshape(frames.shape)


def solution(mesh):
    torus = Mesh(mesh.devices.reshape(NZ, NY, NX, NC), AXES)
    group, row = ("z", "y"), ("x", "c")
    return jax.shard_map(
        per_device,
        mesh=torus,
        in_specs=(
            P(group, row, None, None),
            P(),
            P(group),
            P(group),
            P(None, None, None, group, None),
            P(None, None, None, group, None),
            P(),
            P(),
        ),
        out_specs=P(group, row, None, None),
        check_vma=False,
    )
```

```python
import jax
import jax.numpy as jnp
import numpy as np
from jax import lax
from jax.experimental import pallas as pl
from jax.experimental.pallas import tpu as pltpu
from jax.sharding import Mesh
from jax.sharding import PartitionSpec as P

NZ, NY, NX, NC = 8, 4, 4, 2
AXES = ("z", "y", "x", "c")
C = 384
SHARD = 12
HALF = 14
BUNDLE = 96
ROUND = (0, 1, -1, 2)

FETCH = np.array([[[4, 0], [1, 3], [-1, -3], [2, -2]], [[0, 4], [2, -2], [1, -3], [3, -1]]])


def number(z, y, x, c):
    return ((z % NZ * NY + y % NY) * NX + x % NX) * NC + c


def fetch(array, source_of):
    pairs = []
    for z in range(NZ):
        for y in range(NY):
            for x in range(NX):
                for c in range(NC):
                    source = source_of(z, y, x, c)
                    if source is not None:
                        pairs.append((number(*source), number(z, y, x, c)))
    return lax.ppermute(array, AXES, pairs)


def z_source(which):
    def source(z, y, x, c):
        odd = z % 2
        if c == 0:
            return (z + int(FETCH[0, x, which]), y + 2 * odd - 1, x, c)
        return (z - odd + int(FETCH[1, (x + 2 * odd) % NX, which]), y, x, c)

    return source


def small_source(step):
    return lambda z, y, x, c: (z, y, x + step, c) if c == 0 else (z, y + step, x, c)


def bulk_source(step):
    if step == 2:
        return lambda z, y, x, c: (z + 1 if z % 2 != c else z - 1, y, x, c)
    return lambda z, y, x, c: (z, y + step, x, c) if c == 0 else (z, y, x + step, c)


def sibling(z, y, x, c):
    return (z, y, x, 1 - c)


def own_half(kernel):
    start = lax.axis_index("c") * (27 - HALF)
    taps = lax.dynamic_slice_in_dim(kernel.reshape(27, SHARD, C), start, HALF, 0)
    return taps.reshape(HALF * SHARD, C)


def z_stage(own):
    return jnp.stack([fetch(own, z_source(0)), fetch(own, z_source(1))], 1)


def small_stage(two):
    return [two] + [fetch(two, small_source(step)) for step in ROUND[1:]]


def join_body(*refs):
    parts, out = refs[:-1], refs[-1]
    for tap in range(HALF):
        rows = [
            part[piece, pl.ds(SHARD * tap, SHARD), :].astype(jnp.float32)
            for part in parts
            for piece in range(2)
        ]
        out[tap] = jnp.concatenate(rows, 0).astype(jnp.bfloat16)


def join_rows(parts, which):
    block = pl.BlockSpec((None, 2, HALF * SHARD, C), lambda i: (which, 0, 0, 0))
    return pl.pallas_call(
        join_body,
        grid=(1,),
        out_shape=jax.ShapeDtypeStruct((HALF, BUNDLE, C), jnp.bfloat16),
        in_specs=[block] * 4,
        out_specs=pl.BlockSpec((HALF, BUNDLE, C), lambda i: (0, 0, 0)),
        compiler_params=pltpu.CompilerParams(vmem_limit_bytes=16 * 1024 * 1024),
        cost_estimate=pl.CostEstimate(flops=0, bytes_accessed=2_000_000, transcendentals=0),
    )(*parts)


def bulk_stage(bundle):
    return [bundle] + [fetch(bundle, bulk_source(step)) for step in ROUND[1:]]


def channel_orders():
    z, y, x = (lax.axis_index(a) for a in ("z", "y", "x"))
    table = jnp.asarray(FETCH, jnp.int32)
    around = jnp.array(ROUND, jnp.int32)
    aside = jnp.array((0, 1, -1, 0), jnp.int32)
    odd = z % 2
    at_z = z + jnp.array((0, 0, 0, 1), jnp.int32) * jnp.where(odd == 1, 1, -1)
    piece_z = at_z[:, None, None] + table[0][(x + around) % NX][None, :, :]
    piece_y = (y + aside + 2 * (at_z % 2) - 1)[:, None, None]
    first = piece_z % NZ * NY + piece_y % NY
    at_z = z + jnp.array((0, 0, 0, 1), jnp.int32) * jnp.where(odd == 0, 1, -1)
    piece_z = (at_z - at_z % 2)[:, None] + table[1][(x + aside + 2 * (at_z % 2)) % NX]
    piece_y = y + around
    second = piece_z[:, None, :] % NZ * NY + piece_y[None, :, None] % NY
    ramp = jnp.arange(SHARD, dtype=jnp.int32)
    return jnp.stack([(half.reshape(-1, 1) * SHARD + ramp).reshape(C) for half in (first, second)])


def conv_body(
    scalars, lag_weights, carried, inner, beside, across, order, tail, own0, own1, own2, own3, got0, got1, got2, got3,
    out, acts, spread, weights, total, sems, *, finish,
):
    frames, rows, cols = 6, 4, 32
    own, got = (own0, own1, own2, own3), (got0, got1, got2, got3)

    def copies(half, sources):
        return [
            pltpu.make_async_copy(
                sources[k], weights.at[half, :, pl.ds(BUNDLE * k, BUNDLE), :], sems.at[half, k]
            )
            for k in range(4)
        ]

    core = scalars[0]

    @pl.when(core == 0)
    def _():
        for copy in copies(0, own) + copies(1, got):
            copy.start()

    @pl.when(core == 1)
    def _():
        for copy in copies(0, got) + copies(1, own):
            copy.start()

    acts[0:2, 1:5] = carried[...]
    acts[2:8, 1:5] = inner[...]

    @pl.when(core == 0)
    def _():
        acts[:, 0:1] = across[...]
        acts[:, 5:6] = beside[...]

    @pl.when(core == 1)
    def _():
        acts[:, 0:1] = beside[...]
        acts[:, 5:6] = across[...]

    wide = acts.shape[0] * acts.shape[1]
    col = lax.broadcasted_iota(jnp.int32, (wide * cols, C), 0) % cols
    for half in range(2):
        pick = (
            lax.broadcasted_iota(jnp.int32, (C, C), 0) == order[half : half + 1, :]
        ).astype(jnp.bfloat16)
        plain = jnp.dot(
            acts[...].reshape(wide * cols, C), pick, preferred_element_type=jnp.float32
        )
        before = jnp.where(col == 0, 0.0, pltpu.roll(plain, 1, 0))
        after = jnp.where(col == cols - 1, 0.0, pltpu.roll(plain, wide * cols - 1, 0))
        for tap, moved in enumerate((before, plain, after)):
            spread[half, :, :, :, pl.ds(C * tap, C)] = (
                moved.astype(jnp.bfloat16).reshape(acts.shape)
            )

    total[...] = jnp.zeros_like(total)

    def window(half, lag, row, first, count):
        block = spread[half, pl.ds(lag, frames), pl.ds(row, rows), :, pl.ds(C * first, C * count)]
        return block.reshape(frames * rows * cols, C * count)

    def add(lag, part):
        part = part.reshape(frames, rows * cols, C)
        for f in range(frames):
            total[f] += part[f] * lag_weights[lag, f]

    def group(half, first_tap, index):
        lag, row = index // 3, index % 3
        block = weights[half, pl.ds(index * 3 - first_tap, 3)].reshape(3 * C, C)
        add(lag, jnp.dot(window(half, lag, row, 0, 3), block, preferred_element_type=jnp.float32))

    for copy in copies(0, own):
        copy.wait()

    @pl.loop(0, 4)
    def _(index):
        group(0, 0, index)

    add(
        1,
        jnp.dot(
            window(0, 1, 1, 0, 2),
            weights[0, pl.ds(12, 2)].reshape(2 * C, C),
            preferred_element_type=jnp.float32,
        ),
    )
    for copy in copies(1, own):
        copy.wait()
    add(
        1,
        jnp.dot(window(1, 1, 1, 2, 1), weights[1, 1], preferred_element_type=jnp.float32),
    )

    @pl.loop(5, 9)
    def _(index):
        group(1, 13, index)

    finish(scalars, total, tail, out)


def finish_norm(scalars, total, tail, out):
    for f in range(6):
        data = total[f]
        scale = lax.rsqrt(jnp.mean(data * data, axis=-1, keepdims=True) + 1e-06)
        lifted = data * scale * tail[...]
        out[f] = (lifted * (1.0 / (1.0 + jnp.exp(-lifted)))).astype(jnp.bfloat16)


def finish_add(scalars, total, tail, out):
    for f in range(6):
        summed = tail[f].astype(jnp.float32) + total[f]
        out[f] = jnp.where(f < scalars[1], summed, 0.0).astype(jnp.bfloat16)


def conv(scalars, lag_weights, extended, orders, tail, own, got, finish):
    smem = pl.BlockSpec(memory_space=pltpu.SMEM)
    vmem = pl.BlockSpec(memory_space=pltpu.VMEM)
    return pl.pallas_call(
        lambda *refs: conv_body(*refs, finish=finish),
        out_shape=jax.ShapeDtypeStruct((6, 128, C), jnp.bfloat16),
        in_specs=[smem, smem] + [vmem] * 6 + [pl.BlockSpec(memory_space=pl.ANY)] * 8,
        out_specs=vmem,
        scratch_shapes=[
            pltpu.VMEM((8, 6, 32, C), jnp.bfloat16),
            pltpu.VMEM((2, 8, 6, 32, 3 * C), jnp.bfloat16),
            pltpu.VMEM((2, HALF, C, C), jnp.bfloat16),
            pltpu.VMEM((6, 128, C), jnp.float32),
            pltpu.SemaphoreType.DMA((2, 4)),
        ],
        compiler_params=pltpu.CompilerParams(vmem_limit_bytes=44 * 1024 * 1024),
        cost_estimate=pl.CostEstimate(flops=1000, bytes_accessed=1000, transcendentals=0),
    )(scalars, lag_weights, *extended, orders, tail, *own, *got)


def clip_positions(clip_lengths, frame_index):
    ends = jnp.cumsum(clip_lengths)
    begins = jnp.max(jnp.where(ends[None, :] <= frame_index[:, None], ends[None, :], 0), axis=1)
    return frame_index - begins


def norm_act(values, gain):
    data = values.astype(jnp.float32)
    mean_square = jnp.mean(data * data, axis=-1, keepdims=True)
    scaled = data * lax.rsqrt(mean_square + 1e-06)
    return jax.nn.silu(scaled * gain).astype(jnp.bfloat16)


def before_in_group(z, y, x, c):
    group = z * NY + y - 1
    return None if group < 0 else (group // NY, group % NY, x, c)


def across_chips(z, y, x, c):
    x = x - 1 if c == 0 else x + 1
    return (z, y, x, 1 - c) if 0 <= x < NX else None


def across_and_before(z, y, x, c):
    place = across_chips(z, y, x, c)
    return None if place is None else before_in_group(*place)


def per_device(
    frames, clip_lengths, group_start, group_count, kernel_one, kernel_two, gain_one, gain_two
):
    slots = frames.shape[0]
    slot = jnp.arange(slots, dtype=jnp.int32)
    position = clip_positions(clip_lengths, group_start[0] + slot)
    lag_weights = jnp.stack([position >= 2, position >= 1, position >= 0]).astype(jnp.float32)
    scalars = jnp.stack([lax.axis_index("c").astype(jnp.int32), group_count[0]])
    orders = channel_orders()

    first_core = lax.axis_index("c") == 0
    last = group_count[0] - 2

    def extend(acts):
        outer = jnp.where(first_core, acts[:, 0:1], acts[:, 3:4])
        ends, corners, outer = lax.optimization_barrier(
            (
                lax.dynamic_slice_in_dim(acts, last, 2, 0),
                lax.dynamic_slice_in_dim(outer, last, 2, 0),
                outer,
            )
        )
        carried = fetch(ends, before_in_group)
        across_before = fetch(corners, across_and_before)
        across = fetch(outer, across_chips)
        edge = jnp.concatenate(
            [
                jnp.where(first_core, carried[:, 3:4], carried[:, 0:1]),
                jnp.where(first_core, acts[:, 3:4], acts[:, 0:1]),
            ],
            0,
        )
        beside = fetch(edge, sibling)
        return carried, acts, beside, jnp.concatenate([across_before, across], 0)

    acts_one = norm_act(frames, gain_one)
    parts = small_stage(z_stage(jnp.stack([own_half(kernel_one), own_half(kernel_two)])))
    parts, extended_one = lax.optimization_barrier((parts, extend(acts_one)))
    one_bundle, two_bundle = join_rows(parts, 0), join_rows(parts, 1)
    one_bundles = bulk_stage(one_bundle)
    two_bundles = bulk_stage(two_bundle)
    one_bundles, two_bundle = lax.optimization_barrier((one_bundles, two_bundle))
    one_others = [fetch(b, sibling) for b in one_bundles]

    acts_two = conv(
        scalars, lag_weights, extended_one, orders, gain_two.reshape(1, C),
        one_bundles, one_others, finish_norm,
    ).reshape(frames.shape)
    two_bundles, acts_two = lax.optimization_barrier((two_bundles, acts_two))
    extended = extend(acts_two)
    two_bundles, extended = lax.optimization_barrier((two_bundles, extended))
    two_others = [fetch(b, sibling) for b in two_bundles]
    result = conv(
        scalars, lag_weights, extended, orders, frames.reshape(slots, 128, C),
        two_bundles, two_others, finish_add,
    )
    return result.reshape(frames.shape)


def solution(mesh):
    torus = Mesh(mesh.devices.reshape(NZ, NY, NX, NC), AXES)
    group, row = ("z", "y"), ("x", "c")
    return jax.shard_map(
        per_device,
        mesh=torus,
        in_specs=(
            P(group, row, None, None),
            P(),
            P(group),
            P(group),
            P(None, None, None, group, None),
            P(None, None, None, group, None),
            P(),
            P(),
        ),
        out_specs=P(group, row, None, None),
        check_vma=False,
    )
```

```python
import jax
import jax.numpy as jnp
import numpy as np
from jax import lax
from jax.experimental import pallas as pl
from jax.experimental.pallas import tpu as pltpu
from jax.sharding import Mesh
from jax.sharding import PartitionSpec as P

NZ, NY, NX, NC = 8, 4, 4, 2
AXES = ("z", "y", "x", "c")
C = 384
SHARD = 12
HALF = 14
BUNDLE = 96
ROUND = (0, 1, -1, 2)

FETCH = np.array([[[4, 0], [1, 3], [-1, -3], [2, -2]], [[0, 4], [2, -2], [1, -3], [3, -1]]])


def number(z, y, x, c):
    return ((z % NZ * NY + y % NY) * NX + x % NX) * NC + c


def fetch(array, source_of):
    pairs = []
    for z in range(NZ):
        for y in range(NY):
            for x in range(NX):
                for c in range(NC):
                    source = source_of(z, y, x, c)
                    if source is not None:
                        pairs.append((number(*source), number(z, y, x, c)))
    return lax.ppermute(array, AXES, pairs)


def z_source(which):
    def source(z, y, x, c):
        odd = z % 2
        if c == 0:
            return (z + int(FETCH[0, x, which]), y + 2 * odd - 1, x, c)
        return (z - odd + int(FETCH[1, (x + 2 * odd) % NX, which]), y, x, c)

    return source


def small_source(step):
    return lambda z, y, x, c: (z, y, x + step, c) if c == 0 else (z, y + step, x, c)


def bulk_source(step):
    if step == 2:
        return lambda z, y, x, c: (z + 1 if z % 2 != c else z - 1, y, x, c)
    return lambda z, y, x, c: (z, y + step, x, c) if c == 0 else (z, y, x + step, c)


def sibling(z, y, x, c):
    return (z, y, x, 1 - c)


def own_half(kernel):
    start = lax.axis_index("c") * (27 - HALF)
    taps = lax.dynamic_slice_in_dim(kernel.reshape(27, SHARD, C), start, HALF, 0)
    return taps.reshape(HALF * SHARD, C)


def z_stage(own):
    return jnp.stack([fetch(own, z_source(0)), fetch(own, z_source(1))], 1)


def small_stage(two):
    return [two] + [fetch(two, small_source(step)) for step in ROUND[1:]]


def join_body(*refs):
    parts, out = refs[:-1], refs[-1]
    for tap in range(HALF):
        rows = [
            part[piece, pl.ds(SHARD * tap, SHARD), :].astype(jnp.float32)
            for part in parts
            for piece in range(2)
        ]
        out[tap] = jnp.concatenate(rows, 0).astype(jnp.bfloat16)


def join_rows(parts, which):
    block = pl.BlockSpec((None, 2, HALF * SHARD, C), lambda i: (which, 0, 0, 0))
    return pl.pallas_call(
        join_body,
        grid=(1,),
        out_shape=jax.ShapeDtypeStruct((HALF, BUNDLE, C), jnp.bfloat16),
        in_specs=[block] * 4,
        out_specs=pl.BlockSpec((HALF, BUNDLE, C), lambda i: (0, 0, 0)),
        compiler_params=pltpu.CompilerParams(vmem_limit_bytes=16 * 1024 * 1024),
        cost_estimate=pl.CostEstimate(flops=0, bytes_accessed=2_000_000, transcendentals=0),
    )(*parts)


def bulk_stage(bundle):
    return [bundle] + [fetch(bundle, bulk_source(step)) for step in ROUND[1:]]


def channel_orders():
    z, y, x = (lax.axis_index(a) for a in ("z", "y", "x"))
    table = jnp.asarray(FETCH, jnp.int32)
    around = jnp.array(ROUND, jnp.int32)
    aside = jnp.array((0, 1, -1, 0), jnp.int32)
    odd = z % 2
    at_z = z + jnp.array((0, 0, 0, 1), jnp.int32) * jnp.where(odd == 1, 1, -1)
    piece_z = at_z[:, None, None] + table[0][(x + around) % NX][None, :, :]
    piece_y = (y + aside + 2 * (at_z % 2) - 1)[:, None, None]
    first = piece_z % NZ * NY + piece_y % NY
    at_z = z + jnp.array((0, 0, 0, 1), jnp.int32) * jnp.where(odd == 0, 1, -1)
    piece_z = (at_z - at_z % 2)[:, None] + table[1][(x + aside + 2 * (at_z % 2)) % NX]
    piece_y = y + around
    second = piece_z[:, None, :] % NZ * NY + piece_y[None, :, None] % NY
    ramp = jnp.arange(SHARD, dtype=jnp.int32)
    return jnp.stack([(half.reshape(-1, 1) * SHARD + ramp).reshape(C) for half in (first, second)])


def conv_body(
    scalars, lag_weights, carried, inner, beside, across, order, tail, own0, own1, own2, own3, got0, got1, got2, got3,
    out, acts, spread, weights, total, sems, *, finish,
):
    frames, rows, cols = 6, 4, 32
    own, got = (own0, own1, own2, own3), (got0, got1, got2, got3)

    def copies(half, sources):
        return [
            pltpu.make_async_copy(
                sources[k], weights.at[half, :, pl.ds(BUNDLE * k, BUNDLE), :], sems.at[half, k]
            )
            for k in range(4)
        ]

    core = scalars[0]

    @pl.when(core == 0)
    def _():
        for copy in copies(0, own) + copies(1, got):
            copy.start()

    @pl.when(core == 1)
    def _():
        for copy in copies(0, got) + copies(1, own):
            copy.start()

    acts[0:2, 1:5] = carried[...]
    acts[2:8, 1:5] = inner[...]

    @pl.when(core == 0)
    def _():
        acts[:, 0:1] = across[...]
        acts[:, 5:6] = beside[...]

    @pl.when(core == 1)
    def _():
        acts[:, 0:1] = beside[...]
        acts[:, 5:6] = across[...]

    wide = acts.shape[0] * acts.shape[1]
    col = lax.broadcasted_iota(jnp.int32, (wide * cols, C), 0) % cols
    for half in range(2):
        pick = (
            lax.broadcasted_iota(jnp.int32, (C, C), 0) == order[half : half + 1, :]
        ).astype(jnp.bfloat16)
        plain = jnp.dot(
            acts[...].reshape(wide * cols, C), pick, preferred_element_type=jnp.float32
        )
        before = jnp.where(col == 0, 0.0, pltpu.roll(plain, 1, 0))
        after = jnp.where(col == cols - 1, 0.0, pltpu.roll(plain, wide * cols - 1, 0))
        for tap, moved in enumerate((before, plain, after)):
            spread[half, :, :, :, pl.ds(C * tap, C)] = (
                moved.astype(jnp.bfloat16).reshape(acts.shape)
            )

    total[...] = jnp.zeros_like(total)

    def window(half, lag, row, first, count):
        block = spread[half, pl.ds(lag, frames), pl.ds(row, rows), :, pl.ds(C * first, C * count)]
        return block.reshape(frames * rows * cols, C * count)

    def add(lag, part):
        part = part.reshape(frames, rows * cols, C)
        for f in range(frames):
            total[f] += part[f] * lag_weights[lag, f]

    def group(half, first_tap, index):
        lag, row = index // 3, index % 3
        block = weights[half, pl.ds(index * 3 - first_tap, 3)].reshape(3 * C, C)
        add(lag, jnp.dot(window(half, lag, row, 0, 3), block, preferred_element_type=jnp.float32))

    for copy in copies(0, own):
        copy.wait()

    @pl.loop(0, 4)
    def _(index):
        group(0, 0, index)

    add(
        1,
        jnp.dot(
            window(0, 1, 1, 0, 2),
            weights[0, pl.ds(12, 2)].reshape(2 * C, C),
            preferred_element_type=jnp.float32,
        ),
    )
    for copy in copies(1, own):
        copy.wait()
    add(
        1,
        jnp.dot(window(1, 1, 1, 2, 1), weights[1, 1], preferred_element_type=jnp.float32),
    )

    @pl.loop(5, 9)
    def _(index):
        group(1, 13, index)

    finish(scalars, total, tail, out)


def finish_norm(scalars, total, tail, out):
    for f in range(6):
        data = total[f]
        scale = lax.rsqrt(jnp.mean(data * data, axis=-1, keepdims=True) + 1e-06)
        lifted = data * scale * tail[...]
        out[f] = (lifted * (1.0 / (1.0 + jnp.exp(-lifted)))).astype(jnp.bfloat16)


def finish_add(scalars, total, tail, out):
    for f in range(6):
        summed = tail[f].astype(jnp.float32) + total[f]
        out[f] = jnp.where(f < scalars[1], summed, 0.0).astype(jnp.bfloat16)


def conv(scalars, lag_weights, extended, orders, tail, own, got, finish):
    smem = pl.BlockSpec(memory_space=pltpu.SMEM)
    vmem = pl.BlockSpec(memory_space=pltpu.VMEM)
    return pl.pallas_call(
        lambda *refs: conv_body(*refs, finish=finish),
        out_shape=jax.ShapeDtypeStruct((6, 128, C), jnp.bfloat16),
        in_specs=[smem, smem] + [vmem] * 6 + [pl.BlockSpec(memory_space=pl.ANY)] * 8,
        out_specs=vmem,
        scratch_shapes=[
            pltpu.VMEM((8, 6, 32, C), jnp.bfloat16),
            pltpu.VMEM((2, 8, 6, 32, 3 * C), jnp.bfloat16),
            pltpu.VMEM((2, HALF, C, C), jnp.bfloat16),
            pltpu.VMEM((6, 128, C), jnp.float32),
            pltpu.SemaphoreType.DMA((2, 4)),
        ],
        compiler_params=pltpu.CompilerParams(vmem_limit_bytes=26 * 1024 * 1024),
        cost_estimate=pl.CostEstimate(flops=1000, bytes_accessed=1000, transcendentals=0),
    )(scalars, lag_weights, *extended, orders, tail, *own, *got)


def clip_positions(clip_lengths, frame_index):
    ends = jnp.cumsum(clip_lengths)
    begins = jnp.max(jnp.where(ends[None, :] <= frame_index[:, None], ends[None, :], 0), axis=1)
    return frame_index - begins


def norm_act(values, gain):
    data = values.astype(jnp.float32)
    mean_square = jnp.mean(data * data, axis=-1, keepdims=True)
    scaled = data * lax.rsqrt(mean_square + 1e-06)
    return jax.nn.silu(scaled * gain).astype(jnp.bfloat16)


def before_in_group(z, y, x, c):
    group = z * NY + y - 1
    return None if group < 0 else (group // NY, group % NY, x, c)


def across_chips(z, y, x, c):
    x = x - 1 if c == 0 else x + 1
    return (z, y, x, 1 - c) if 0 <= x < NX else None


def across_and_before(z, y, x, c):
    place = across_chips(z, y, x, c)
    return None if place is None else before_in_group(*place)


def per_device(
    frames, clip_lengths, group_start, group_count, kernel_one, kernel_two, gain_one, gain_two
):
    slots = frames.shape[0]
    slot = jnp.arange(slots, dtype=jnp.int32)
    position = clip_positions(clip_lengths, group_start[0] + slot)
    lag_weights = jnp.stack([position >= 2, position >= 1, position >= 0]).astype(jnp.float32)
    scalars = jnp.stack([lax.axis_index("c").astype(jnp.int32), group_count[0]])
    orders = channel_orders()

    first_core = lax.axis_index("c") == 0
    last = group_count[0] - 2

    def sides(acts):
        return (
            jnp.where(first_core, acts[:, 3:4], acts[:, 0:1]),
            jnp.where(first_core, acts[:, 0:1], acts[:, 3:4]),
        )

    def last_two(acts):
        return lax.dynamic_slice_in_dim(acts, last, 2, 0)

    acts_one = norm_act(frames, gain_one)
    own = jnp.stack([own_half(kernel_one), own_half(kernel_two)])
    pieces = z_stage(own)
    inner, outer = sides(acts_one)
    beside, across = fetch(inner, sibling), fetch(outer, across_chips)
    pieces, beside, across, orders, lag_weights, scalars = lax.optimization_barrier(
        (pieces, beside, across, orders, lag_weights, scalars)
    )

    parts = small_stage(pieces)
    one_bundle, two_bundle = join_rows(parts, 0), join_rows(parts, 1)
    one_bundles = bulk_stage(one_bundle)
    ends = jnp.concatenate([last_two(acts_one), last_two(beside), last_two(across)], 1)
    ends, _ = lax.optimization_barrier((ends, one_bundle))
    ends = fetch(ends, before_in_group)
    extended = (
        ends[:, 0:4],
        acts_one,
        jnp.concatenate([ends[:, 4:5], beside], 0),
        jnp.concatenate([ends[:, 5:6], across], 0),
    )
    one_bundles, two_bundle, extended = lax.optimization_barrier(
        (one_bundles, two_bundle, extended)
    )
    one_others = [fetch(b, sibling) for b in one_bundles]

    two_bundle, one_others[1] = lax.optimization_barrier((two_bundle, one_others[1]))
    two_bundles = bulk_stage(two_bundle)
    acts_two = conv(
        scalars, lag_weights, extended, orders, gain_two.reshape(1, C),
        one_bundles, one_others, finish_norm,
    ).reshape(frames.shape)

    two_bundles, acts_two = lax.optimization_barrier((two_bundles, acts_two))
    two_others = [fetch(b, sibling) for b in two_bundles[:2]]
    inner, outer = sides(acts_two)
    ends, corners, outer = lax.optimization_barrier((last_two(acts_two), last_two(outer), outer))
    carried = fetch(ends, before_in_group)
    corners = fetch(corners, across_and_before)
    across = fetch(outer, across_chips)
    carried, corners, across, two_last = lax.optimization_barrier(
        (carried, corners, across, two_bundles[2:])
    )
    edge = jnp.concatenate([sides(carried)[0], inner], 0)
    beside = fetch(edge, sibling)
    two_others += [fetch(b, sibling) for b in two_last]
    extended = (carried, acts_two, beside, jnp.concatenate([corners, across], 0))
    result = conv(
        scalars, lag_weights, extended, orders, frames.reshape(slots, 128, C),
        two_bundles, two_others, finish_add,
    )
    return result.reshape(frames.shape)


def solution(mesh):
    torus = Mesh(mesh.devices.reshape(NZ, NY, NX, NC), AXES)
    group, row = ("z", "y"), ("x", "c")
    return jax.shard_map(
        per_device,
        mesh=torus,
        in_specs=(
            P(group, row, None, None),
            P(),
            P(group),
            P(group),
            P(None, None, None, group, None),
            P(None, None, None, group, None),
            P(),
            P(),
        ),
        out_specs=P(group, row, None, None),
        check_vma=False,
    )
```

```python
import jax
import jax.numpy as jnp
import numpy as np
from jax import lax
from jax.experimental import pallas as pl
from jax.experimental.pallas import tpu as pltpu
from jax.sharding import Mesh
from jax.sharding import PartitionSpec as P

NZ, NY, NX, NC = 8, 4, 4, 2
AXES = ("z", "y", "x", "c")
C = 384
SHARD = 12
HALF = 14
BUNDLE = 96
ROUND = (0, 1, -1, 2)

FETCH = np.array([[[4, 0], [1, 3], [-1, -3], [2, -2]], [[0, 4], [2, -2], [1, -3], [3, -1]]])


def number(z, y, x, c):
    return ((z % NZ * NY + y % NY) * NX + x % NX) * NC + c


def fetch(array, source_of):
    pairs = []
    for z in range(NZ):
        for y in range(NY):
            for x in range(NX):
                for c in range(NC):
                    source = source_of(z, y, x, c)
                    if source is not None:
                        pairs.append((number(*source), number(z, y, x, c)))
    return lax.ppermute(array, AXES, pairs)


def z_source(which):
    def source(z, y, x, c):
        odd = z % 2
        if c == 0:
            return (z + int(FETCH[0, x, which]), y + 2 * odd - 1, x, c)
        return (z - odd + int(FETCH[1, (x + 2 * odd) % NX, which]), y, x, c)

    return source


def small_source(step):
    return lambda z, y, x, c: (z, y, x + step, c) if c == 0 else (z, y + step, x, c)


def bulk_source(step):
    if step == 2:
        return lambda z, y, x, c: (z + 1 if z % 2 != c else z - 1, y, x, c)
    return lambda z, y, x, c: (z, y + step, x, c) if c == 0 else (z, y, x + step, c)


def sibling(z, y, x, c):
    return (z, y, x, 1 - c)


def own_half(kernel):
    start = lax.axis_index("c") * (27 - HALF)
    taps = lax.dynamic_slice_in_dim(kernel.reshape(27, SHARD, C), start, HALF, 0)
    return taps.reshape(HALF * SHARD, C)


def z_stage(own):
    return jnp.stack([fetch(own, z_source(0)), fetch(own, z_source(1))], 1)


def small_stage(two):
    return [two] + [fetch(two, small_source(step)) for step in ROUND[1:]]


def join_body(*refs):
    parts, out = refs[:-1], refs[-1]
    for tap in range(HALF):
        rows = [
            part[piece, pl.ds(SHARD * tap, SHARD), :].astype(jnp.float32)
            for part in parts
            for piece in range(2)
        ]
        out[tap] = jnp.concatenate(rows, 0).astype(jnp.bfloat16)


def join_rows(parts, which):
    block = pl.BlockSpec((None, 2, HALF * SHARD, C), lambda i: (which, 0, 0, 0))
    return pl.pallas_call(
        join_body,
        grid=(1,),
        out_shape=jax.ShapeDtypeStruct((HALF, BUNDLE, C), jnp.bfloat16),
        in_specs=[block] * 4,
        out_specs=pl.BlockSpec((HALF, BUNDLE, C), lambda i: (0, 0, 0)),
        compiler_params=pltpu.CompilerParams(vmem_limit_bytes=16 * 1024 * 1024),
        cost_estimate=pl.CostEstimate(flops=0, bytes_accessed=2_000_000, transcendentals=0),
    )(*parts)


def bulk_stage(bundle):
    return [bundle] + [fetch(bundle, bulk_source(step)) for step in ROUND[1:]]


def channel_orders():
    z, y, x = (lax.axis_index(a) for a in ("z", "y", "x"))
    table = jnp.asarray(FETCH, jnp.int32)
    around = jnp.array(ROUND, jnp.int32)
    aside = jnp.array((0, 1, -1, 0), jnp.int32)
    odd = z % 2
    at_z = z + jnp.array((0, 0, 0, 1), jnp.int32) * jnp.where(odd == 1, 1, -1)
    piece_z = at_z[:, None, None] + table[0][(x + around) % NX][None, :, :]
    piece_y = (y + aside + 2 * (at_z % 2) - 1)[:, None, None]
    first = piece_z % NZ * NY + piece_y % NY
    at_z = z + jnp.array((0, 0, 0, 1), jnp.int32) * jnp.where(odd == 0, 1, -1)
    piece_z = (at_z - at_z % 2)[:, None] + table[1][(x + aside + 2 * (at_z % 2)) % NX]
    piece_y = y + around
    second = piece_z[:, None, :] % NZ * NY + piece_y[None, :, None] % NY
    ramp = jnp.arange(SHARD, dtype=jnp.int32)
    return jnp.stack([(half.reshape(-1, 1) * SHARD + ramp).reshape(C) for half in (first, second)])


def permute_body(order, *refs):
    out, top = refs[-1], 0
    picks = [
        (lax.broadcasted_iota(jnp.int32, (C, C), 0) == order[half : half + 1, :]).astype(jnp.bfloat16)
        for half in range(2)
    ]
    for ref in refs[:-1]:
        rows = ref.shape[0]
        for half in range(2):
            out[half, top : top + rows] = jnp.dot(
                ref[...], picks[half], preferred_element_type=jnp.float32
            ).astype(jnp.bfloat16)
        top += rows


def permute(orders, *arrays):
    arrays = [array.reshape(-1, C) for array in arrays]
    rows = sum(array.shape[0] for array in arrays)
    vmem = pl.BlockSpec(memory_space=pltpu.VMEM)
    return pl.pallas_call(
        permute_body,
        out_shape=jax.ShapeDtypeStruct((2, rows, C), jnp.bfloat16),
        in_specs=[vmem] * (1 + len(arrays)),
        out_specs=vmem,
        compiler_params=pltpu.CompilerParams(vmem_limit_bytes=16 * 1024 * 1024),
        cost_estimate=pl.CostEstimate(flops=1000, bytes_accessed=1000, transcendentals=0),
    )(orders, *arrays)


def conv_body(
    scalars, lag_weights, inner, halo, tail, own0, own1, own2, own3, got0, got1, got2, got3,
    out, spread, weights, total, sems, *, finish,
):
    frames, rows, cols = 6, 4, 32
    own, got = (own0, own1, own2, own3), (got0, got1, got2, got3)

    def copies(half, sources):
        return [
            pltpu.make_async_copy(
                sources[k], weights.at[half, :, pl.ds(BUNDLE * k, BUNDLE), :], sems.at[half, k]
            )
            for k in range(4)
        ]

    core = scalars[0]

    @pl.when(core == 0)
    def _():
        for copy in copies(0, own) + copies(1, got):
            copy.start()

    @pl.when(core == 1)
    def _():
        for copy in copies(0, got) + copies(1, own):
            copy.start()

    wide, tall = frames + 2, rows + 2
    col = lax.broadcasted_iota(jnp.int32, (wide * tall * cols, C), 0) % cols
    for half in range(2):
        spread[half, 2:wide, 1:5, :, C : 2 * C] = inner[half].reshape(frames, rows, cols, C)
        spread[half, 0:2, 1:5, :, C : 2 * C] = halo[half, 0:256].reshape(2, rows, cols, C)

        @pl.when(core == 0)
        def _():
            spread[half, :, 5:6, :, C : 2 * C] = halo[half, 256:512].reshape(wide, 1, cols, C)
            spread[half, :, 0:1, :, C : 2 * C] = halo[half, 512:768].reshape(wide, 1, cols, C)

        @pl.when(core == 1)
        def _():
            spread[half, :, 0:1, :, C : 2 * C] = halo[half, 256:512].reshape(wide, 1, cols, C)
            spread[half, :, 5:6, :, C : 2 * C] = halo[half, 512:768].reshape(wide, 1, cols, C)

        plain = spread[half, :, :, :, C : 2 * C].reshape(wide * tall * cols, C).astype(jnp.float32)
        before = jnp.where(col == 0, 0.0, pltpu.roll(plain, 1, 0))
        after = jnp.where(col == cols - 1, 0.0, pltpu.roll(plain, wide * tall * cols - 1, 0))
        for place, moved in ((0, before), (2 * C, after)):
            spread[half, :, :, :, place : place + C] = (
                moved.astype(jnp.bfloat16).reshape(wide, tall, cols, C)
            )

    total[...] = jnp.zeros_like(total)

    def window(half, lag, row, first, count):
        block = spread[half, pl.ds(lag, frames), pl.ds(row, rows), :, pl.ds(C * first, C * count)]
        return block.reshape(frames * rows * cols, C * count)

    def add(lag, part):
        part = part.reshape(frames, rows * cols, C)
        for f in range(frames):
            total[f] += part[f] * lag_weights[lag, f]

    def group(half, first_tap, index):
        lag, row = index // 3, index % 3
        block = weights[half, pl.ds(index * 3 - first_tap, 3)].reshape(3 * C, C)
        add(lag, jnp.dot(window(half, lag, row, 0, 3), block, preferred_element_type=jnp.float32))

    for copy in copies(0, own):
        copy.wait()

    @pl.loop(0, 4)
    def _(index):
        group(0, 0, index)

    add(
        1,
        jnp.dot(
            window(0, 1, 1, 0, 2),
            weights[0, pl.ds(12, 2)].reshape(2 * C, C),
            preferred_element_type=jnp.float32,
        ),
    )
    for copy in copies(1, own):
        copy.wait()
    add(
        1,
        jnp.dot(window(1, 1, 1, 2, 1), weights[1, 1], preferred_element_type=jnp.float32),
    )

    @pl.loop(5, 9)
    def _(index):
        group(1, 13, index)

    finish(scalars, total, tail, out)


def finish_norm(scalars, total, tail, out):
    for f in range(6):
        data = total[f]
        scale = lax.rsqrt(jnp.mean(data * data, axis=-1, keepdims=True) + 1e-06)
        lifted = data * scale * tail[...]
        out[f] = (lifted * (1.0 / (1.0 + jnp.exp(-lifted)))).astype(jnp.bfloat16)


def finish_add(scalars, total, tail, out):
    for f in range(6):
        summed = tail[f].astype(jnp.float32) + total[f]
        out[f] = jnp.where(f < scalars[1], summed, 0.0).astype(jnp.bfloat16)


def conv(scalars, lag_weights, inner, halo, tail, own, got, finish):
    smem = pl.BlockSpec(memory_space=pltpu.SMEM)
    vmem = pl.BlockSpec(memory_space=pltpu.VMEM)
    return pl.pallas_call(
        lambda *refs: conv_body(*refs, finish=finish),
        out_shape=jax.ShapeDtypeStruct((6, 128, C), jnp.bfloat16),
        in_specs=[smem, smem] + [vmem] * 3 + [pl.BlockSpec(memory_space=pl.ANY)] * 8,
        out_specs=vmem,
        scratch_shapes=[
            pltpu.VMEM((2, 8, 6, 32, 3 * C), jnp.bfloat16),
            pltpu.VMEM((2, HALF, C, C), jnp.bfloat16),
            pltpu.VMEM((6, 128, C), jnp.float32),
            pltpu.SemaphoreType.DMA((2, 4)),
        ],
        compiler_params=pltpu.CompilerParams(vmem_limit_bytes=26 * 1024 * 1024),
        cost_estimate=pl.CostEstimate(flops=1000, bytes_accessed=1000, transcendentals=0),
    )(scalars, lag_weights, inner, halo, tail, *own, *got)


def clip_positions(clip_lengths, frame_index):
    ends = jnp.cumsum(clip_lengths)
    begins = jnp.max(jnp.where(ends[None, :] <= frame_index[:, None], ends[None, :], 0), axis=1)
    return frame_index - begins


def norm_act(values, gain):
    data = values.astype(jnp.float32)
    mean_square = jnp.mean(data * data, axis=-1, keepdims=True)
    scaled = data * lax.rsqrt(mean_square + 1e-06)
    return jax.nn.silu(scaled * gain).astype(jnp.bfloat16)


def before_in_group(z, y, x, c):
    group = z * NY + y - 1
    return None if group < 0 else (group // NY, group % NY, x, c)


def across_chips(z, y, x, c):
    x = x - 1 if c == 0 else x + 1
    return (z, y, x, 1 - c) if 0 <= x < NX else None


def across_and_before(z, y, x, c):
    place = across_chips(z, y, x, c)
    return None if place is None else before_in_group(*place)


def per_device(
    frames, clip_lengths, group_start, group_count, kernel_one, kernel_two, gain_one, gain_two
):
    slots = frames.shape[0]
    slot = jnp.arange(slots, dtype=jnp.int32)
    position = clip_positions(clip_lengths, group_start[0] + slot)
    lag_weights = jnp.stack([position >= 2, position >= 1, position >= 0]).astype(jnp.float32)
    scalars = jnp.stack([lax.axis_index("c").astype(jnp.int32), group_count[0]])
    orders = channel_orders()

    first_core = lax.axis_index("c") == 0
    last = group_count[0] - 2

    def sides(acts):
        return (
            jnp.where(first_core, acts[:, 3:4], acts[:, 0:1]),
            jnp.where(first_core, acts[:, 0:1], acts[:, 3:4]),
        )

    def last_two(acts):
        return lax.dynamic_slice_in_dim(acts, last, 2, 0)

    acts_one = norm_act(frames, gain_one)
    own = jnp.stack([own_half(kernel_one), own_half(kernel_two)])
    pieces = z_stage(own)
    inner, outer = sides(acts_one)
    ends, corners, outer = lax.optimization_barrier((last_two(acts_one), last_two(outer), outer))
    carried = fetch(ends, before_in_group)
    across = fetch(outer, across_chips)
    corners = fetch(corners, across_and_before)
    pieces, carried, across, corners, orders, lag_weights, scalars = lax.optimization_barrier(
        (pieces, carried, across, corners, orders, lag_weights, scalars)
    )

    parts = small_stage(pieces)
    one_bundle, two_bundle = join_rows(parts, 0), join_rows(parts, 1)
    one_bundles = bulk_stage(one_bundle)
    carried, _ = lax.optimization_barrier((carried, one_bundle))
    beside = fetch(jnp.concatenate([sides(carried)[0], inner], 0), sibling)
    inner = permute(orders, acts_one)
    halo = permute(orders, carried, beside, jnp.concatenate([corners, across], 0))
    one_bundles, two_bundle, inner, halo = lax.optimization_barrier(
        (one_bundles, two_bundle, inner, halo)
    )
    one_others = [fetch(b, sibling) for b in one_bundles]

    two_bundle, one_others[1] = lax.optimization_barrier((two_bundle, one_others[1]))
    two_bundles = bulk_stage(two_bundle)
    acts_two = conv(
        scalars, lag_weights, inner, halo, gain_two.reshape(1, C), one_bundles, one_others,
        finish_norm,
    ).reshape(frames.shape)

    two_bundles, acts_two = lax.optimization_barrier((two_bundles, acts_two))
    inner, outer = sides(acts_two)
    beside = fetch(inner, sibling)
    across = fetch(outer, across_chips)
    ends = jnp.concatenate([last_two(acts_two), last_two(beside)], 1)
    ends, corners = lax.optimization_barrier((ends, last_two(outer)))
    ends = fetch(ends, before_in_group)
    corners = fetch(corners, across_and_before)
    first_two, two_last = two_bundles[:2], two_bundles[2:]
    beside, first_two = lax.optimization_barrier((beside, first_two))
    two_others = [fetch(b, sibling) for b in first_two]
    inner = permute(orders, acts_two)
    ends, corners, across, two_last, inner = lax.optimization_barrier(
        (ends, corners, across, two_last, inner)
    )
    two_others += [fetch(b, sibling) for b in two_last]
    halo = permute(
        orders,
        ends[:, 0:4],
        jnp.concatenate([ends[:, 4:5], beside], 0),
        jnp.concatenate([corners, across], 0),
    )
    result = conv(
        scalars, lag_weights, inner, halo, frames.reshape(slots, 128, C), two_bundles, two_others,
        finish_add,
    )
    return result.reshape(frames.shape)


def solution(mesh):
    torus = Mesh(mesh.devices.reshape(NZ, NY, NX, NC), AXES)
    group, row = ("z", "y"), ("x", "c")
    return jax.shard_map(
        per_device,
        mesh=torus,
        in_specs=(
            P(group, row, None, None),
            P(),
            P(group),
            P(group),
            P(None, None, None, group, None),
            P(None, None, None, group, None),
            P(),
            P(),
        ),
        out_specs=P(group, row, None, None),
        check_vma=False,
    )
```

```python
import jax
import jax.numpy as jnp
import numpy as np
from jax import lax
from jax.experimental import pallas as pl
from jax.experimental.pallas import tpu as pltpu
from jax.sharding import Mesh
from jax.sharding import PartitionSpec as P

NZ, NY, NX, NC = 8, 4, 4, 2
AXES = ("z", "y", "x", "c")
C = 384
SHARD = 12
HALF = 14
BUNDLE = 96
ROUND = (0, 1, -1, 2)

FETCH = np.array([[[4, 0], [1, 3], [-1, -3], [2, -2]], [[0, 4], [2, -2], [1, -3], [3, -1]]])


def number(z, y, x, c):
    return ((z % NZ * NY + y % NY) * NX + x % NX) * NC + c


def fetch(array, source_of):
    pairs = []
    for z in range(NZ):
        for y in range(NY):
            for x in range(NX):
                for c in range(NC):
                    source = source_of(z, y, x, c)
                    if source is not None:
                        pairs.append((number(*source), number(z, y, x, c)))
    return lax.ppermute(array, AXES, pairs)


def z_source(which):
    def source(z, y, x, c):
        odd = z % 2
        if c == 0:
            return (z + int(FETCH[0, x, which]), y + 2 * odd - 1, x, c)
        return (z - odd + int(FETCH[1, (x + 2 * odd) % NX, which]), y, x, c)

    return source


def small_source(step):
    return lambda z, y, x, c: (z, y, x + step, c) if c == 0 else (z, y + step, x, c)


def bulk_source(step):
    if step == 2:
        return lambda z, y, x, c: (z + 1 if z % 2 != c else z - 1, y, x, c)
    return lambda z, y, x, c: (z, y + step, x, c) if c == 0 else (z, y, x + step, c)


def sibling(z, y, x, c):
    return (z, y, x, 1 - c)


def own_half(kernel):
    start = lax.axis_index("c") * (27 - HALF)
    taps = lax.dynamic_slice_in_dim(kernel.reshape(27, SHARD, C), start, HALF, 0)
    return taps.reshape(HALF * SHARD, C)


def z_stage(own):
    return jnp.stack([fetch(own, z_source(0)), fetch(own, z_source(1))], 1)


def join_body(*refs):
    parts, out = refs[:-1], refs[-1]
    for tap in range(HALF):
        rows = [
            part[piece, pl.ds(SHARD * tap, SHARD), :].astype(jnp.float32)
            for part in parts
            for piece in range(2)
        ]
        out[tap] = jnp.concatenate(rows, 0).astype(jnp.bfloat16)


def join_rows(parts, which):
    block = pl.BlockSpec((None, 2, HALF * SHARD, C), lambda i: (which, 0, 0, 0))
    return pl.pallas_call(
        join_body,
        grid=(1,),
        out_shape=jax.ShapeDtypeStruct((HALF, BUNDLE, C), jnp.bfloat16),
        in_specs=[block] * 4,
        out_specs=pl.BlockSpec((HALF, BUNDLE, C), lambda i: (0, 0, 0)),
        compiler_params=pltpu.CompilerParams(vmem_limit_bytes=16 * 1024 * 1024),
        cost_estimate=pl.CostEstimate(flops=0, bytes_accessed=2_000_000, transcendentals=0),
    )(*parts)


def bulk_stage(bundle):
    return [bundle] + [fetch(bundle, bulk_source(step)) for step in ROUND[1:]]


def channel_orders():
    z, y, x = (lax.axis_index(a) for a in ("z", "y", "x"))
    table = jnp.asarray(FETCH, jnp.int32)
    around = jnp.array(ROUND, jnp.int32)
    aside = jnp.array((0, 1, -1, 0), jnp.int32)
    odd = z % 2
    at_z = z + jnp.array((0, 0, 0, 1), jnp.int32) * jnp.where(odd == 1, 1, -1)
    piece_z = at_z[:, None, None] + table[0][(x + around) % NX][None, :, :]
    piece_y = (y + aside + 2 * (at_z % 2) - 1)[:, None, None]
    first = piece_z % NZ * NY + piece_y % NY
    at_z = z + jnp.array((0, 0, 0, 1), jnp.int32) * jnp.where(odd == 0, 1, -1)
    piece_z = (at_z - at_z % 2)[:, None] + table[1][(x + aside + 2 * (at_z % 2)) % NX]
    piece_y = y + around
    second = piece_z[:, None, :] % NZ * NY + piece_y[None, :, None] % NY
    ramp = jnp.arange(SHARD, dtype=jnp.int32)
    return jnp.stack([(half.reshape(-1, 1) * SHARD + ramp).reshape(C) for half in (first, second)])


def spread_cells(cells, order, half):
    rows = cells.shape[0]
    pick = (lax.broadcasted_iota(jnp.int32, (C, C), 0) == order[half : half + 1, :]).astype(jnp.bfloat16)
    plain = jnp.dot(cells, pick, preferred_element_type=jnp.float32)
    col = lax.broadcasted_iota(jnp.int32, (rows, C), 0) % 32
    before = jnp.where(col == 0, 0.0, pltpu.roll(plain, 1, 0))
    after = jnp.where(col == 31, 0.0, pltpu.roll(plain, rows - 1, 0))
    return [part.astype(jnp.bfloat16) for part in (before, plain, after)]


def spread_inner_body(order, acts, out):
    for half in range(2):
        for tap, part in enumerate(spread_cells(acts[...], order, half)):
            out[half, 2:8, 1:5, :, C * tap : C * (tap + 1)] = part.reshape(6, 4, 32, C)


def spread_inner(orders, acts):
    vmem = pl.BlockSpec(memory_space=pltpu.VMEM)
    return pl.pallas_call(
        spread_inner_body,
        out_shape=jax.ShapeDtypeStruct((2, 8, 6, 32, 3 * C), jnp.bfloat16),
        in_specs=[vmem] * 2,
        out_specs=vmem,
        compiler_params=pltpu.CompilerParams(vmem_limit_bytes=20 * 1024 * 1024),
        cost_estimate=pl.CostEstimate(flops=1000, bytes_accessed=1000, transcendentals=0),
    )(orders, acts.reshape(-1, C))


def spread_halo_body(scalars, order, carried, beside, across, _, out, frames, rows, sems):
    core = scalars[0]
    for half in range(2):
        for tap, part in enumerate(spread_cells(carried[...], order, half)):
            frames[half, :, :, :, C * tap : C * (tap + 1)] = part.reshape(2, 4, 32, C)
        for side, cells in enumerate((beside, across)):
            for tap, part in enumerate(spread_cells(cells[...], order, half)):
                rows[side, half, :, :, :, C * tap : C * (tap + 1)] = part.reshape(8, 1, 32, C)

    def copies(above, below):
        return [
            pltpu.make_async_copy(frames, out.at[:, 0:2, 1:5], sems.at[0]),
            pltpu.make_async_copy(rows.at[above], out.at[:, :, 0:1], sems.at[1]),
            pltpu.make_async_copy(rows.at[below], out.at[:, :, 5:6], sems.at[2]),
        ]

    @pl.when(core == 0)
    def _():
        for copy in copies(1, 0):
            copy.start()
        for copy in copies(1, 0):
            copy.wait()

    @pl.when(core == 1)
    def _():
        for copy in copies(0, 1):
            copy.start()
        for copy in copies(0, 1):
            copy.wait()


def spread_halo(scalars, orders, carried, beside, across, spread):
    vmem = pl.BlockSpec(memory_space=pltpu.VMEM)
    either = pl.BlockSpec(memory_space=pl.ANY)
    return pl.pallas_call(
        spread_halo_body,
        out_shape=jax.ShapeDtypeStruct(spread.shape, spread.dtype),
        in_specs=[pl.BlockSpec(memory_space=pltpu.SMEM)] + [vmem] * 4 + [either],
        out_specs=either,
        scratch_shapes=[
            pltpu.VMEM((2, 2, 4, 32, 3 * C), jnp.bfloat16),
            pltpu.VMEM((2, 2, 8, 1, 32, 3 * C), jnp.bfloat16),
            pltpu.SemaphoreType.DMA((3,)),
        ],
        input_output_aliases={5: 0},
        compiler_params=pltpu.CompilerParams(vmem_limit_bytes=20 * 1024 * 1024),
        cost_estimate=pl.CostEstimate(flops=1000, bytes_accessed=1000, transcendentals=0),
    )(scalars, orders, *(cells.reshape(-1, C) for cells in (carried, beside, across)), spread)


def conv_body(
    scalars, lag_weights, spread, tail, own0, own1, own2, own3, got0, got1, got2, got3,
    out, weights, total, sems, *, finish,
):
    frames, rows, cols = 6, 4, 32
    own, got = (own0, own1, own2, own3), (got0, got1, got2, got3)

    def copies(half, sources):
        return [
            pltpu.make_async_copy(
                sources[k], weights.at[half, :, pl.ds(BUNDLE * k, BUNDLE), :], sems.at[half, k]
            )
            for k in range(4)
        ]

    core = scalars[0]

    @pl.when(core == 0)
    def _():
        for copy in copies(0, own) + copies(1, got):
            copy.start()

    @pl.when(core == 1)
    def _():
        for copy in copies(0, got) + copies(1, own):
            copy.start()

    total[...] = jnp.zeros_like(total)

    def window(half, lag, row, first, count):
        block = spread[half, pl.ds(lag, frames), pl.ds(row, rows), :, pl.ds(C * first, C * count)]
        return block.reshape(frames * rows * cols, C * count)

    def add(lag, part):
        part = part.reshape(frames, rows * cols, C)
        for f in range(frames):
            total[f] += part[f] * lag_weights[lag, f]

    def group(half, first_tap, index):
        lag, row = index // 3, index % 3
        block = weights[half, pl.ds(index * 3 - first_tap, 3)].reshape(3 * C, C)
        add(lag, jnp.dot(window(half, lag, row, 0, 3), block, preferred_element_type=jnp.float32))

    for copy in copies(0, own):
        copy.wait()

    @pl.loop(0, 4)
    def _(index):
        group(0, 0, index)

    add(
        1,
        jnp.dot(
            window(0, 1, 1, 0, 2),
            weights[0, pl.ds(12, 2)].reshape(2 * C, C),
            preferred_element_type=jnp.float32,
        ),
    )
    for copy in copies(1, own):
        copy.wait()
    add(
        1,
        jnp.dot(window(1, 1, 1, 2, 1), weights[1, 1], preferred_element_type=jnp.float32),
    )

    @pl.loop(5, 9)
    def _(index):
        group(1, 13, index)

    finish(scalars, total, tail, out)


def finish_norm(scalars, total, tail, out):
    for f in range(6):
        data = total[f]
        scale = lax.rsqrt(jnp.mean(data * data, axis=-1, keepdims=True) + 1e-06)
        lifted = data * scale * tail[...]
        out[f] = (lifted * (1.0 / (1.0 + jnp.exp(-lifted)))).astype(jnp.bfloat16)


def finish_add(scalars, total, tail, out):
    for f in range(6):
        summed = tail[f].astype(jnp.float32) + total[f]
        out[f] = jnp.where(f < scalars[1], summed, 0.0).astype(jnp.bfloat16)


def conv(scalars, lag_weights, spread, tail, own, got, finish):
    smem = pl.BlockSpec(memory_space=pltpu.SMEM)
    vmem = pl.BlockSpec(memory_space=pltpu.VMEM)
    return pl.pallas_call(
        lambda *refs: conv_body(*refs, finish=finish),
        out_shape=jax.ShapeDtypeStruct((6, 128, C), jnp.bfloat16),
        in_specs=[smem, smem] + [vmem] * 2 + [pl.BlockSpec(memory_space=pl.ANY)] * 8,
        out_specs=vmem,
        scratch_shapes=[
            pltpu.VMEM((2, HALF, C, C), jnp.bfloat16),
            pltpu.VMEM((6, 128, C), jnp.float32),
            pltpu.SemaphoreType.DMA((2, 4)),
        ],
        compiler_params=pltpu.CompilerParams(vmem_limit_bytes=26 * 1024 * 1024),
        cost_estimate=pl.CostEstimate(flops=1000, bytes_accessed=1000, transcendentals=0),
    )(scalars, lag_weights, spread, tail, *own, *got)


def clip_positions(clip_lengths, frame_index):
    ends = jnp.cumsum(clip_lengths)
    begins = jnp.max(jnp.where(ends[None, :] <= frame_index[:, None], ends[None, :], 0), axis=1)
    return frame_index - begins


def norm_act(values, gain):
    data = values.astype(jnp.float32)
    mean_square = jnp.mean(data * data, axis=-1, keepdims=True)
    scaled = data * lax.rsqrt(mean_square + 1e-06)
    return jax.nn.silu(scaled * gain).astype(jnp.bfloat16)


def before_in_group(z, y, x, c):
    group = z * NY + y - 1
    return None if group < 0 else (group // NY, group % NY, x, c)


def across_chips(z, y, x, c):
    x = x - 1 if c == 0 else x + 1
    return (z, y, x, 1 - c) if 0 <= x < NX else None


def across_and_before(z, y, x, c):
    place = across_chips(z, y, x, c)
    return None if place is None else before_in_group(*place)


def per_device(
    frames, clip_lengths, group_start, group_count, kernel_one, kernel_two, gain_one, gain_two
):
    slots = frames.shape[0]
    slot = jnp.arange(slots, dtype=jnp.int32)
    position = clip_positions(clip_lengths, group_start[0] + slot)
    lag_weights = jnp.stack([position >= 2, position >= 1, position >= 0]).astype(jnp.float32)
    scalars = jnp.stack([lax.axis_index("c").astype(jnp.int32), group_count[0]])
    orders = channel_orders()

    first_core = lax.axis_index("c") == 0
    last = group_count[0] - 2

    def sides(acts):
        return (
            jnp.where(first_core, acts[:, 3:4], acts[:, 0:1]),
            jnp.where(first_core, acts[:, 0:1], acts[:, 3:4]),
        )

    def last_two(acts):
        return lax.dynamic_slice_in_dim(acts, last, 2, 0)

    acts_one = norm_act(frames, gain_one)
    own = jnp.stack([own_half(kernel_one), own_half(kernel_two)])
    pieces = z_stage(own)
    inner, outer = sides(acts_one)
    ends, corners, outer = lax.optimization_barrier((last_two(acts_one), last_two(outer), outer))
    carried = fetch(ends, before_in_group)
    across = fetch(outer, across_chips)
    corners = fetch(corners, across_and_before)
    pieces, orders, lag_weights, scalars = lax.optimization_barrier(
        (pieces, orders, lag_weights, scalars)
    )

    opposite = fetch(pieces, small_source(2))
    after = fetch(pieces, small_source(1))
    gated, carried, across, corners = lax.optimization_barrier((pieces, carried, across, corners))
    parts = [pieces, after, fetch(gated, small_source(-1)), opposite]
    beside = fetch(jnp.concatenate([sides(carried)[0], inner], 0), sibling)
    spread = spread_halo(
        scalars, orders, carried, beside, jnp.concatenate([corners, across], 0),
        spread_inner(orders, acts_one),
    )
    parts, spread = lax.optimization_barrier((parts, spread))

    one_bundle, two_bundle = join_rows(parts, 0), join_rows(parts, 1)
    one_bundles = bulk_stage(one_bundle)
    one_own, two_own = lax.optimization_barrier((one_bundle, two_bundle))
    one_others, two_others = [fetch(one_own, sibling)], [fetch(two_own, sibling)]
    one_bundles, two_bundle, one_others, two_others = lax.optimization_barrier(
        (one_bundles, two_bundle, one_others, two_others)
    )
    one_others += [fetch(b, sibling) for b in one_bundles[1:]]

    two_bundle, one_others[1] = lax.optimization_barrier((two_bundle, one_others[1]))
    two_bundles = bulk_stage(two_bundle)
    acts_two = conv(
        scalars, lag_weights, spread, gain_two.reshape(1, C), one_bundles, one_others, finish_norm
    ).reshape(frames.shape)

    two_bundles, acts_two = lax.optimization_barrier((two_bundles, acts_two))
    inner, outer = sides(acts_two)
    beside = fetch(inner, sibling)
    across = fetch(outer, across_chips)
    two_others.append(fetch(two_bundles[1], sibling))
    two_bundles[1], beside, two_others = lax.optimization_barrier(
        (two_bundles[1], beside, two_others)
    )
    ends = jnp.concatenate([last_two(acts_two), last_two(beside)], 1)
    ends, corners = lax.optimization_barrier((ends, last_two(outer)))
    ends = fetch(ends, before_in_group)
    corners = fetch(corners, across_and_before)
    two_others += [fetch(b, sibling) for b in two_bundles[2:]]
    spread = spread_inner(orders, acts_two)
    ends, corners, across, spread = lax.optimization_barrier((ends, corners, across, spread))
    spread = spread_halo(
        scalars, orders, ends[:, 0:4],
        jnp.concatenate([ends[:, 4:5], beside], 0),
        jnp.concatenate([corners, across], 0),
        spread,
    )
    result = conv(
        scalars, lag_weights, spread, frames.reshape(slots, 128, C), two_bundles, two_others,
        finish_add,
    )
    return result.reshape(frames.shape)


def solution(mesh):
    torus = Mesh(mesh.devices.reshape(NZ, NY, NX, NC), AXES)
    group, row = ("z", "y"), ("x", "c")
    return jax.shard_map(
        per_device,
        mesh=torus,
        in_specs=(
            P(group, row, None, None),
            P(),
            P(group),
            P(group),
            P(None, None, None, group, None),
            P(None, None, None, group, None),
            P(),
            P(),
        ),
        out_specs=P(group, row, None, None),
        check_vma=False,
    )
```

```python
import jax
import jax.numpy as jnp
import numpy as np
from jax import lax
from jax.experimental import pallas as pl
from jax.experimental.pallas import tpu as pltpu
from jax.sharding import Mesh
from jax.sharding import PartitionSpec as P

NZ, NY, NX, NC = 8, 4, 4, 2
AXES = ("z", "y", "x", "c")
C = 384
SHARD = 12
HALF = 14
BUNDLE = 96
ROUND = (0, 1, -1, 2)

FETCH = np.array([[[4, 0], [1, 3], [-1, -3], [2, -2]], [[0, 4], [2, -2], [1, -3], [3, -1]]])


def number(z, y, x, c):
    return ((z % NZ * NY + y % NY) * NX + x % NX) * NC + c


def fetch(array, source_of):
    pairs = []
    for z in range(NZ):
        for y in range(NY):
            for x in range(NX):
                for c in range(NC):
                    source = source_of(z, y, x, c)
                    if source is not None:
                        pairs.append((number(*source), number(z, y, x, c)))
    return lax.ppermute(array, AXES, pairs)


def z_source(which):
    def source(z, y, x, c):
        odd = z % 2
        if c == 0:
            return (z + int(FETCH[0, x, which]), y + 2 * odd - 1, x, c)
        return (z - odd + int(FETCH[1, (x + 2 * odd) % NX, which]), y, x, c)

    return source


def small_source(step):
    return lambda z, y, x, c: (z, y, x + step, c) if c == 0 else (z, y + step, x, c)


def bulk_source(step):
    if step == 2:
        return lambda z, y, x, c: (z + 1 if z % 2 != c else z - 1, y, x, c)
    return lambda z, y, x, c: (z, y + step, x, c) if c == 0 else (z, y, x + step, c)


def sibling(z, y, x, c):
    return (z, y, x, 1 - c)


def own_half(kernel):
    start = lax.axis_index("c") * (27 - HALF)
    taps = lax.dynamic_slice_in_dim(kernel.reshape(27, SHARD, C), start, HALF, 0)
    return taps.reshape(HALF * SHARD, C)


def z_stage(own):
    return jnp.stack([fetch(own, z_source(0)), fetch(own, z_source(1))], 1)


def join_body(*refs):
    parts, out = refs[:-1], refs[-1]
    for tap in range(HALF):
        rows = [
            part[piece, pl.ds(SHARD * tap, SHARD), :].astype(jnp.float32)
            for part in parts
            for piece in range(2)
        ]
        out[tap] = jnp.concatenate(rows, 0).astype(jnp.bfloat16)


def join_rows(parts, which):
    block = pl.BlockSpec((None, 2, HALF * SHARD, C), lambda i: (which, 0, 0, 0))
    return pl.pallas_call(
        join_body,
        grid=(1,),
        out_shape=jax.ShapeDtypeStruct((HALF, BUNDLE, C), jnp.bfloat16),
        in_specs=[block] * 4,
        out_specs=pl.BlockSpec((HALF, BUNDLE, C), lambda i: (0, 0, 0)),
        compiler_params=pltpu.CompilerParams(vmem_limit_bytes=16 * 1024 * 1024),
        cost_estimate=pl.CostEstimate(flops=0, bytes_accessed=2_000_000, transcendentals=0),
    )(*parts)


def bulk_stage(bundle):
    return [bundle] + [fetch(bundle, bulk_source(step)) for step in ROUND[1:]]


def channel_orders():
    z, y, x = (lax.axis_index(a) for a in ("z", "y", "x"))
    table = jnp.asarray(FETCH, jnp.int32)
    around = jnp.array(ROUND, jnp.int32)
    aside = jnp.array((0, 1, -1, 0), jnp.int32)
    odd = z % 2
    at_z = z + jnp.array((0, 0, 0, 1), jnp.int32) * jnp.where(odd == 1, 1, -1)
    piece_z = at_z[:, None, None] + table[0][(x + around) % NX][None, :, :]
    piece_y = (y + aside + 2 * (at_z % 2) - 1)[:, None, None]
    first = piece_z % NZ * NY + piece_y % NY
    at_z = z + jnp.array((0, 0, 0, 1), jnp.int32) * jnp.where(odd == 0, 1, -1)
    piece_z = (at_z - at_z % 2)[:, None] + table[1][(x + aside + 2 * (at_z % 2)) % NX]
    piece_y = y + around
    second = piece_z[:, None, :] % NZ * NY + piece_y[None, :, None] % NY
    ramp = jnp.arange(SHARD, dtype=jnp.int32)
    return jnp.stack([(half.reshape(-1, 1) * SHARD + ramp).reshape(C) for half in (first, second)])


def spread_cells(cells, order, half):
    rows = cells.shape[0]
    pick = (lax.broadcasted_iota(jnp.int32, (C, C), 0) == order[half : half + 1, :]).astype(jnp.bfloat16)
    plain = jnp.dot(cells, pick, preferred_element_type=jnp.float32)
    col = lax.broadcasted_iota(jnp.int32, (rows, C), 0) % 32
    before = jnp.where(col == 0, 0.0, pltpu.roll(plain, 1, 0))
    after = jnp.where(col == 31, 0.0, pltpu.roll(plain, rows - 1, 0))
    return [part.astype(jnp.bfloat16) for part in (before, plain, after)]


def spread_inner_body(order, acts, out):
    for half in range(2):
        for tap, part in enumerate(spread_cells(acts[...], order, half)):
            out[half, 2:8, 1:5, :, C * tap : C * (tap + 1)] = part.reshape(6, 4, 32, C)


def spread_inner(orders, acts):
    vmem = pl.BlockSpec(memory_space=pltpu.VMEM)
    return pl.pallas_call(
        spread_inner_body,
        out_shape=jax.ShapeDtypeStruct((2, 8, 6, 32, 3 * C), jnp.bfloat16),
        in_specs=[vmem] * 2,
        out_specs=vmem,
        compiler_params=pltpu.CompilerParams(vmem_limit_bytes=20 * 1024 * 1024),
        cost_estimate=pl.CostEstimate(flops=1000, bytes_accessed=1000, transcendentals=0),
    )(orders, acts.reshape(-1, C))


def spread_halo_body(scalars, order, carried, beside, across, _, out):
    core = scalars[0]
    for half in range(2):
        for tap, part in enumerate(spread_cells(carried[...], order, half)):
            out[half, 0:2, 1:5, :, C * tap : C * (tap + 1)] = part.reshape(2, 4, 32, C)
        for tap, part in enumerate(spread_cells(beside[...], order, half)):
            part = part.reshape(8, 1, 32, C)

            @pl.when(core == 0)
            def _():
                out[half, :, 5:6, :, C * tap : C * (tap + 1)] = part

            @pl.when(core == 1)
            def _():
                out[half, :, 0:1, :, C * tap : C * (tap + 1)] = part

        for tap, part in enumerate(spread_cells(across[...], order, half)):
            part = part.reshape(8, 1, 32, C)

            @pl.when(core == 0)
            def _():
                out[half, :, 0:1, :, C * tap : C * (tap + 1)] = part

            @pl.when(core == 1)
            def _():
                out[half, :, 5:6, :, C * tap : C * (tap + 1)] = part


def spread_halo(scalars, orders, carried, beside, across, spread):
    vmem = pl.BlockSpec(memory_space=pltpu.VMEM)
    return pl.pallas_call(
        spread_halo_body,
        out_shape=jax.ShapeDtypeStruct(spread.shape, spread.dtype),
        in_specs=[pl.BlockSpec(memory_space=pltpu.SMEM)] + [vmem] * 5,
        out_specs=vmem,
        input_output_aliases={5: 0},
        compiler_params=pltpu.CompilerParams(vmem_limit_bytes=20 * 1024 * 1024),
        cost_estimate=pl.CostEstimate(flops=1000, bytes_accessed=1000, transcendentals=0),
    )(scalars, orders, *(cells.reshape(-1, C) for cells in (carried, beside, across)), spread)


def conv_body(
    scalars, lag_weights, spread, tail, own0, own1, own2, own3, got0, got1, got2, got3,
    out, weights, total, sems, *, finish,
):
    frames, rows, cols = 6, 4, 32
    own, got = (own0, own1, own2, own3), (got0, got1, got2, got3)

    def copies(half, sources):
        return [
            pltpu.make_async_copy(
                sources[k], weights.at[half, :, pl.ds(BUNDLE * k, BUNDLE), :], sems.at[half, k]
            )
            for k in range(4)
        ]

    core = scalars[0]

    @pl.when(core == 0)
    def _():
        for copy in copies(0, own) + copies(1, got):
            copy.start()

    @pl.when(core == 1)
    def _():
        for copy in copies(0, got) + copies(1, own):
            copy.start()

    total[...] = jnp.zeros_like(total)

    def window(half, lag, row, first, count):
        block = spread[half, pl.ds(lag, frames), pl.ds(row, rows), :, pl.ds(C * first, C * count)]
        return block.reshape(frames * rows * cols, C * count)

    def add(lag, part):
        part = part.reshape(frames, rows * cols, C)
        for f in range(frames):
            total[f] += part[f] * lag_weights[lag, f]

    def group(half, first_tap, index):
        lag, row = index // 3, index % 3
        block = weights[half, pl.ds(index * 3 - first_tap, 3)].reshape(3 * C, C)
        add(lag, jnp.dot(window(half, lag, row, 0, 3), block, preferred_element_type=jnp.float32))

    for copy in copies(0, own):
        copy.wait()

    @pl.loop(0, 4)
    def _(index):
        group(0, 0, index)

    add(
        1,
        jnp.dot(
            window(0, 1, 1, 0, 2),
            weights[0, pl.ds(12, 2)].reshape(2 * C, C),
            preferred_element_type=jnp.float32,
        ),
    )
    for copy in copies(1, own):
        copy.wait()
    add(
        1,
        jnp.dot(window(1, 1, 1, 2, 1), weights[1, 1], preferred_element_type=jnp.float32),
    )

    @pl.loop(5, 9)
    def _(index):
        group(1, 13, index)

    finish(scalars, total, tail, out)


def finish_norm(scalars, total, tail, out):
    for f in range(6):
        data = total[f]
        scale = lax.rsqrt(jnp.mean(data * data, axis=-1, keepdims=True) + 1e-06)
        lifted = data * scale * tail[...]
        out[f] = (lifted * (1.0 / (1.0 + jnp.exp(-lifted)))).astype(jnp.bfloat16)


def finish_add(scalars, total, tail, out):
    for f in range(6):
        summed = tail[f].astype(jnp.float32) + total[f]
        out[f] = jnp.where(f < scalars[1], summed, 0.0).astype(jnp.bfloat16)


def conv(scalars, lag_weights, spread, tail, own, got, finish):
    smem = pl.BlockSpec(memory_space=pltpu.SMEM)
    vmem = pl.BlockSpec(memory_space=pltpu.VMEM)
    return pl.pallas_call(
        lambda *refs: conv_body(*refs, finish=finish),
        out_shape=jax.ShapeDtypeStruct((6, 128, C), jnp.bfloat16),
        in_specs=[smem, smem] + [vmem] * 2 + [pl.BlockSpec(memory_space=pl.ANY)] * 8,
        out_specs=vmem,
        scratch_shapes=[
            pltpu.VMEM((2, HALF, C, C), jnp.bfloat16),
            pltpu.VMEM((6, 128, C), jnp.float32),
            pltpu.SemaphoreType.DMA((2, 4)),
        ],
        compiler_params=pltpu.CompilerParams(vmem_limit_bytes=26 * 1024 * 1024),
        cost_estimate=pl.CostEstimate(flops=1000, bytes_accessed=1000, transcendentals=0),
    )(scalars, lag_weights, spread, tail, *own, *got)


def clip_positions(clip_lengths, frame_index):
    ends = jnp.cumsum(clip_lengths)
    begins = jnp.max(jnp.where(ends[None, :] <= frame_index[:, None], ends[None, :], 0), axis=1)
    return frame_index - begins


def norm_act(values, gain):
    data = values.astype(jnp.float32)
    mean_square = jnp.mean(data * data, axis=-1, keepdims=True)
    scaled = data * lax.rsqrt(mean_square + 1e-06)
    return jax.nn.silu(scaled * gain).astype(jnp.bfloat16)


def before_in_group(z, y, x, c):
    group = z * NY + y - 1
    return None if group < 0 else (group // NY, group % NY, x, c)


def across_chips(z, y, x, c):
    x = x - 1 if c == 0 else x + 1
    return (z, y, x, 1 - c) if 0 <= x < NX else None


def across_and_before(z, y, x, c):
    place = across_chips(z, y, x, c)
    return None if place is None else before_in_group(*place)


def per_device(
    frames, clip_lengths, group_start, group_count, kernel_one, kernel_two, gain_one, gain_two
):
    slots = frames.shape[0]
    slot = jnp.arange(slots, dtype=jnp.int32)
    position = clip_positions(clip_lengths, group_start[0] + slot)
    lag_weights = jnp.stack([position >= 2, position >= 1, position >= 0]).astype(jnp.float32)
    scalars = jnp.stack([lax.axis_index("c").astype(jnp.int32), group_count[0]])
    orders = channel_orders()

    first_core = lax.axis_index("c") == 0
    last = group_count[0] - 2

    def sides(acts):
        return (
            jnp.where(first_core, acts[:, 3:4], acts[:, 0:1]),
            jnp.where(first_core, acts[:, 0:1], acts[:, 3:4]),
        )

    def last_two(acts):
        return lax.dynamic_slice_in_dim(acts, last, 2, 0)

    acts_one = norm_act(frames, gain_one)
    own = jnp.stack([own_half(kernel_one), own_half(kernel_two)])
    pieces = z_stage(own)
    inner, outer = sides(acts_one)
    ends, outer = lax.optimization_barrier((last_two(acts_one), outer))
    carried = fetch(ends, before_in_group)
    across = fetch(outer, across_chips)
    pieces, orders, lag_weights, scalars = lax.optimization_barrier(
        (pieces, orders, lag_weights, scalars)
    )

    opposite = fetch(pieces, small_source(2))
    after = fetch(pieces, small_source(1))
    gated, carried, across = lax.optimization_barrier((pieces, carried, across))
    parts = [pieces, after, fetch(gated, small_source(-1)), opposite]
    carried_inner, carried_outer = sides(carried)
    corners = fetch(carried_outer, across_chips)
    beside = fetch(jnp.concatenate([carried_inner, inner], 0), sibling)
    spread = spread_halo(
        scalars, orders, carried, beside, jnp.concatenate([corners, across], 0),
        spread_inner(orders, acts_one),
    )
    parts, spread = lax.optimization_barrier((parts, spread))

    one_bundle, two_bundle = join_rows(parts, 0), join_rows(parts, 1)
    one_bundles = bulk_stage(one_bundle)
    one_own, two_own = lax.optimization_barrier((one_bundle, two_bundle))
    one_others, two_others = [fetch(one_own, sibling)], [fetch(two_own, sibling)]
    two_bundle, one_others, two_others = lax.optimization_barrier(
        (two_bundle, one_others, two_others)
    )
    one_bundles, one_others, two_others = lax.optimization_barrier(
        (one_bundles, one_others, two_others)
    )
    one_others += [fetch(b, sibling) for b in one_bundles[1:]]

    two_bundles = bulk_stage(two_bundle)
    acts_two = conv(
        scalars, lag_weights, spread, gain_two.reshape(1, C), one_bundles, one_others, finish_norm
    ).reshape(frames.shape)

    two_bundles, acts_two = lax.optimization_barrier((two_bundles, acts_two))
    inner, outer = sides(acts_two)
    beside = fetch(inner, sibling)
    across = fetch(outer, across_chips)
    two_bundles, beside = lax.optimization_barrier((two_bundles, beside))
    ends = jnp.concatenate([last_two(acts_two), last_two(beside)], 1)
    ends, corners = lax.optimization_barrier((ends, last_two(outer)))
    ends = fetch(ends, before_in_group)
    corners = fetch(corners, across_and_before)
    two_others += [fetch(b, sibling) for b in two_bundles[1:3]]
    spread = spread_inner(orders, acts_two)
    ends, corners, across, spread, two_last = lax.optimization_barrier(
        (ends, corners, across, spread, two_bundles[3])
    )
    two_others.append(fetch(two_last, sibling))
    spread = spread_halo(
        scalars, orders, ends[:, 0:4],
        jnp.concatenate([ends[:, 4:5], beside], 0),
        jnp.concatenate([corners, across], 0),
        spread,
    )
    result = conv(
        scalars, lag_weights, spread, frames.reshape(slots, 128, C), two_bundles, two_others,
        finish_add,
    )
    return result.reshape(frames.shape)


def solution(mesh):
    torus = Mesh(mesh.devices.reshape(NZ, NY, NX, NC), AXES)
    group, row = ("z", "y"), ("x", "c")
    return jax.shard_map(
        per_device,
        mesh=torus,
        in_specs=(
            P(group, row, None, None),
            P(),
            P(group),
            P(group),
            P(None, None, None, group, None),
            P(None, None, None, group, None),
            P(),
            P(),
        ),
        out_specs=P(group, row, None, None),
        check_vma=False,
    )
```

```python
import jax
import jax.numpy as jnp
import numpy as np
from jax import lax
from jax.experimental import pallas as pl
from jax.experimental.pallas import tpu as pltpu
from jax.sharding import Mesh
from jax.sharding import PartitionSpec as P

NZ, NY, NX, NC = 8, 4, 4, 2
AXES = ("z", "y", "x", "c")
C = 384
SHARD = 12
HALF = 14
BUNDLE = 96
ROUND = (0, 1, -1, 2)

FETCH = np.array([[[4, 0], [1, 3], [-1, -3], [2, -2]], [[0, 4], [2, -2], [1, -3], [3, -1]]])


def number(z, y, x, c):
    return ((z % NZ * NY + y % NY) * NX + x % NX) * NC + c


def fetch(array, source_of):
    pairs = []
    for z in range(NZ):
        for y in range(NY):
            for x in range(NX):
                for c in range(NC):
                    source = source_of(z, y, x, c)
                    if source is not None:
                        pairs.append((number(*source), number(z, y, x, c)))
    return lax.ppermute(array, AXES, pairs)


def z_source(which):
    def source(z, y, x, c):
        odd = z % 2
        if c == 0:
            return (z + int(FETCH[0, x, which]), y + 2 * odd - 1, x, c)
        return (z - odd + int(FETCH[1, (x + 2 * odd) % NX, which]), y, x, c)

    return source


def small_source(step):
    return lambda z, y, x, c: (z, y, x + step, c) if c == 0 else (z, y + step, x, c)


def bulk_source(step):
    if step == 2:
        return lambda z, y, x, c: (z + 1 if z % 2 != c else z - 1, y, x, c)
    return lambda z, y, x, c: (z, y + step, x, c) if c == 0 else (z, y, x + step, c)


def sibling(z, y, x, c):
    return (z, y, x, 1 - c)


def own_half(kernel):
    start = lax.axis_index("c") * (27 - HALF)
    taps = lax.dynamic_slice_in_dim(kernel.reshape(27, SHARD, C), start, HALF, 0)
    return taps.reshape(HALF * SHARD, C)


def z_stage(own):
    return jnp.stack([fetch(own, z_source(0)), fetch(own, z_source(1))], 1)


def join_body(*refs):
    parts, out = refs[:-1], refs[-1]
    for tap in range(HALF):
        rows = [
            part[piece, pl.ds(SHARD * tap, SHARD), :].astype(jnp.float32)
            for part in parts
            for piece in range(2)
        ]
        out[tap] = jnp.concatenate(rows, 0).astype(jnp.bfloat16)


def join_rows(parts, which):
    block = pl.BlockSpec((None, 2, HALF * SHARD, C), lambda i: (which, 0, 0, 0))
    return pl.pallas_call(
        join_body,
        grid=(1,),
        out_shape=jax.ShapeDtypeStruct((HALF, BUNDLE, C), jnp.bfloat16),
        in_specs=[block] * 4,
        out_specs=pl.BlockSpec((HALF, BUNDLE, C), lambda i: (0, 0, 0)),
        compiler_params=pltpu.CompilerParams(vmem_limit_bytes=16 * 1024 * 1024),
        cost_estimate=pl.CostEstimate(flops=0, bytes_accessed=2_000_000, transcendentals=0),
    )(*parts)


def bulk_stage(bundle):
    return [bundle] + [fetch(bundle, bulk_source(step)) for step in ROUND[1:]]


def channel_orders():
    z, y, x = (lax.axis_index(a) for a in ("z", "y", "x"))
    table = jnp.asarray(FETCH, jnp.int32)
    around = jnp.array(ROUND, jnp.int32)
    aside = jnp.array((0, 1, -1, 0), jnp.int32)
    odd = z % 2
    at_z = z + jnp.array((0, 0, 0, 1), jnp.int32) * jnp.where(odd == 1, 1, -1)
    piece_z = at_z[:, None, None] + table[0][(x + around) % NX][None, :, :]
    piece_y = (y + aside + 2 * (at_z % 2) - 1)[:, None, None]
    first = piece_z % NZ * NY + piece_y % NY
    at_z = z + jnp.array((0, 0, 0, 1), jnp.int32) * jnp.where(odd == 0, 1, -1)
    piece_z = (at_z - at_z % 2)[:, None] + table[1][(x + aside + 2 * (at_z % 2)) % NX]
    piece_y = y + around
    second = piece_z[:, None, :] % NZ * NY + piece_y[None, :, None] % NY
    ramp = jnp.arange(SHARD, dtype=jnp.int32)
    return jnp.stack([(half.reshape(-1, 1) * SHARD + ramp).reshape(C) for half in (first, second)])


def picks_body(order, out):
    for half in range(2):
        out[half] = (
            lax.broadcasted_iota(jnp.int32, (C, C), 0) == order[half : half + 1, :]
        ).astype(jnp.bfloat16)


def make_picks(orders):
    vmem = pl.BlockSpec(memory_space=pltpu.VMEM)
    return pl.pallas_call(
        picks_body,
        out_shape=jax.ShapeDtypeStruct((2, C, C), jnp.bfloat16),
        in_specs=[vmem],
        out_specs=vmem,
        cost_estimate=pl.CostEstimate(flops=1000, bytes_accessed=1000, transcendentals=0),
    )(orders)


def spread_cells(cells, pick):
    rows = cells.shape[0]
    plain = jnp.dot(cells, pick, preferred_element_type=jnp.float32)
    col = lax.broadcasted_iota(jnp.int32, (rows, C), 0) % 32
    before = jnp.where(col == 0, 0.0, pltpu.roll(plain, 1, 0))
    after = jnp.where(col == 31, 0.0, pltpu.roll(plain, rows - 1, 0))
    return [part.astype(jnp.bfloat16) for part in (before, plain, after)]


def spread_inner_body(picks, acts, out):
    for half in range(2):
        for tap, part in enumerate(spread_cells(acts[...], picks[half])):
            out[half, 2:8, 1:5, :, C * tap : C * (tap + 1)] = part.reshape(6, 4, 32, C)


def spread_inner(picks, acts):
    vmem = pl.BlockSpec(memory_space=pltpu.VMEM)
    return pl.pallas_call(
        spread_inner_body,
        out_shape=jax.ShapeDtypeStruct((2, 8, 6, 32, 3 * C), jnp.bfloat16),
        in_specs=[vmem] * 2,
        out_specs=vmem,
        compiler_params=pltpu.CompilerParams(vmem_limit_bytes=20 * 1024 * 1024),
        cost_estimate=pl.CostEstimate(flops=1000, bytes_accessed=1000, transcendentals=0),
    )(picks, acts.reshape(-1, C))


def spread_halo_body(scalars, picks, ends, beside, across, _, out):
    core = scalars[0]
    cells = jnp.concatenate(
        [ends[:, 0:4].reshape(256, C)]
        + [
            rows[...].reshape(-1, C)
            for rows in (ends.at[:, 4:5], beside, ends.at[:, 5:6], across)
        ],
        0,
    )
    for half in range(2):
        for tap, part in enumerate(spread_cells(cells, picks[half])):
            lanes = slice(C * tap, C * (tap + 1))
            out[half, 0:2, 1:5, :, lanes] = part[0:256].reshape(2, 4, 32, C)
            near, far = part[256:512].reshape(8, 1, 32, C), part[512:768].reshape(8, 1, 32, C)

            @pl.when(core == 0)
            def _():
                out[half, :, 0:1, :, lanes] = far
                out[half, :, 5:6, :, lanes] = near

            @pl.when(core == 1)
            def _():
                out[half, :, 0:1, :, lanes] = near
                out[half, :, 5:6, :, lanes] = far


def spread_halo(scalars, picks, ends, beside, across, spread):
    vmem = pl.BlockSpec(memory_space=pltpu.VMEM)
    return pl.pallas_call(
        spread_halo_body,
        out_shape=jax.ShapeDtypeStruct(spread.shape, spread.dtype),
        in_specs=[pl.BlockSpec(memory_space=pltpu.SMEM)] + [vmem] * 5,
        out_specs=vmem,
        input_output_aliases={5: 0},
        compiler_params=pltpu.CompilerParams(vmem_limit_bytes=20 * 1024 * 1024),
        cost_estimate=pl.CostEstimate(flops=1000, bytes_accessed=1000, transcendentals=0),
    )(scalars, picks, ends, beside, across, spread)


def conv_body(
    scalars, lag_weights, spread, tail, own0, own1, own2, own3, got0, got1, got2, got3,
    out, weights, total, sems, *, finish,
):
    frames, rows, cols = 6, 4, 32
    own, got = (own0, own1, own2, own3), (got0, got1, got2, got3)

    def copies(half, sources):
        return [
            pltpu.make_async_copy(
                sources[k], weights.at[half, :, pl.ds(BUNDLE * k, BUNDLE), :], sems.at[half, k]
            )
            for k in range(4)
        ]

    core = scalars[0]

    @pl.when(core == 0)
    def _():
        for copy in copies(0, own) + copies(1, got):
            copy.start()

    @pl.when(core == 1)
    def _():
        for copy in copies(0, got) + copies(1, own):
            copy.start()

    total[...] = jnp.zeros_like(total)

    def window(half, lag, row, first, count):
        block = spread[half, pl.ds(lag, frames), pl.ds(row, rows), :, pl.ds(C * first, C * count)]
        return block.reshape(frames * rows * cols, C * count)

    def add(lag, part):
        part = part.reshape(frames, rows * cols, C)
        for f in range(frames):
            total[f] += part[f] * lag_weights[lag, f]

    def group(half, first_tap, index):
        lag, row = index // 3, index % 3
        block = weights[half, pl.ds(index * 3 - first_tap, 3)].reshape(3 * C, C)
        add(lag, jnp.dot(window(half, lag, row, 0, 3), block, preferred_element_type=jnp.float32))

    for copy in copies(0, own):
        copy.wait()

    @pl.loop(0, 4)
    def _(index):
        group(0, 0, index)

    add(
        1,
        jnp.dot(
            window(0, 1, 1, 0, 2),
            weights[0, pl.ds(12, 2)].reshape(2 * C, C),
            preferred_element_type=jnp.float32,
        ),
    )
    for copy in copies(1, own):
        copy.wait()
    add(
        1,
        jnp.dot(window(1, 1, 1, 2, 1), weights[1, 1], preferred_element_type=jnp.float32),
    )

    @pl.loop(5, 9)
    def _(index):
        group(1, 13, index)

    finish(scalars, total, tail, out)


def finish_norm(scalars, total, tail, out):
    for f in range(6):
        data = total[f]
        scale = lax.rsqrt(jnp.mean(data * data, axis=-1, keepdims=True) + 1e-06)
        lifted = data * scale * tail[...]
        out[f] = (lifted * (1.0 / (1.0 + jnp.exp(-lifted)))).astype(jnp.bfloat16)


def finish_add(scalars, total, tail, out):
    for f in range(6):
        summed = tail[f].astype(jnp.float32) + total[f]
        out[f] = jnp.where(f < scalars[1], summed, 0.0).astype(jnp.bfloat16)


def conv(scalars, lag_weights, spread, tail, own, got, finish):
    smem = pl.BlockSpec(memory_space=pltpu.SMEM)
    vmem = pl.BlockSpec(memory_space=pltpu.VMEM)
    return pl.pallas_call(
        lambda *refs: conv_body(*refs, finish=finish),
        out_shape=jax.ShapeDtypeStruct((6, 128, C), jnp.bfloat16),
        in_specs=[smem, smem] + [vmem] * 2 + [pl.BlockSpec(memory_space=pl.ANY)] * 8,
        out_specs=vmem,
        scratch_shapes=[
            pltpu.VMEM((2, HALF, C, C), jnp.bfloat16),
            pltpu.VMEM((6, 128, C), jnp.float32),
            pltpu.SemaphoreType.DMA((2, 4)),
        ],
        compiler_params=pltpu.CompilerParams(vmem_limit_bytes=26 * 1024 * 1024),
        cost_estimate=pl.CostEstimate(flops=1000, bytes_accessed=1000, transcendentals=0),
    )(scalars, lag_weights, spread, tail, *own, *got)


def clip_positions(clip_lengths, frame_index):
    ends = jnp.cumsum(clip_lengths)
    begins = jnp.max(jnp.where(ends[None, :] <= frame_index[:, None], ends[None, :], 0), axis=1)
    return frame_index - begins


def norm_act(values, gain):
    data = values.astype(jnp.float32)
    mean_square = jnp.mean(data * data, axis=-1, keepdims=True)
    scaled = data * lax.rsqrt(mean_square + 1e-06)
    return jax.nn.silu(scaled * gain).astype(jnp.bfloat16)


def before_in_group(z, y, x, c):
    group = z * NY + y - 1
    return None if group < 0 else (group // NY, group % NY, x, c)


def across_chips(z, y, x, c):
    x = x - 1 if c == 0 else x + 1
    return (z, y, x, 1 - c) if 0 <= x < NX else None


def per_device(
    frames, clip_lengths, group_start, group_count, kernel_one, kernel_two, gain_one, gain_two
):
    slots = frames.shape[0]
    slot = jnp.arange(slots, dtype=jnp.int32)
    position = clip_positions(clip_lengths, group_start[0] + slot)
    lag_weights = jnp.stack([position >= 2, position >= 1, position >= 0]).astype(jnp.float32)
    scalars = jnp.stack([lax.axis_index("c").astype(jnp.int32), group_count[0]])
    orders = channel_orders()

    first_core = lax.axis_index("c") == 0
    last = group_count[0] - 2

    def sides(acts):
        return (
            jnp.where(first_core, acts[:, 3:4], acts[:, 0:1]),
            jnp.where(first_core, acts[:, 0:1], acts[:, 3:4]),
        )

    def with_rows(*arrays):
        return jnp.concatenate([lax.dynamic_slice_in_dim(a, last, 2, 0) for a in arrays], 1)

    acts_one = norm_act(frames, gain_one)
    own = jnp.stack([own_half(kernel_one), own_half(kernel_two)])
    pieces = z_stage(own)
    inner, outer = sides(acts_one)
    beside, across = fetch(inner, sibling), fetch(outer, across_chips)
    ends = fetch(with_rows(acts_one, beside, across), before_in_group)
    picks = make_picks(orders)
    pieces, picks, lag_weights, scalars = lax.optimization_barrier(
        (pieces, picks, lag_weights, scalars)
    )

    opposite = fetch(pieces, small_source(2))
    after = fetch(pieces, small_source(1))
    gated, ends = lax.optimization_barrier((pieces, ends))
    parts = [pieces, after, fetch(gated, small_source(-1)), opposite]
    spread = spread_halo(scalars, picks, ends, beside, across, spread_inner(picks, acts_one))
    parts, spread = lax.optimization_barrier((parts, spread))

    one_bundle, two_bundle = join_rows(parts, 0), join_rows(parts, 1)
    one_bundles = bulk_stage(one_bundle)
    one_own, two_own = lax.optimization_barrier((one_bundle, two_bundle))
    one_others, two_others = [fetch(one_own, sibling)], [fetch(two_own, sibling)]
    two_bundle, one_others, two_others = lax.optimization_barrier(
        (two_bundle, one_others, two_others)
    )
    one_bundles, one_others, two_others = lax.optimization_barrier(
        (one_bundles, one_others, two_others)
    )
    one_others += [fetch(b, sibling) for b in one_bundles[1:]]

    two_bundles = bulk_stage(two_bundle)
    acts_two = conv(
        scalars, lag_weights, spread, gain_two.reshape(1, C), one_bundles, one_others, finish_norm
    ).reshape(frames.shape)

    two_bundles, acts_two = lax.optimization_barrier((two_bundles, acts_two))
    inner, outer = sides(acts_two)
    across, beside = fetch(outer, across_chips), fetch(inner, sibling)
    two_bundles, beside, across = lax.optimization_barrier((two_bundles, beside, across))
    two_others += [fetch(b, sibling) for b in two_bundles[1:]]
    ends = fetch(with_rows(acts_two, beside, across), before_in_group)
    spread = spread_inner(picks, acts_two)
    ends, spread = lax.optimization_barrier((ends, spread))
    spread = spread_halo(scalars, picks, ends, beside, across, spread)
    result = conv(
        scalars, lag_weights, spread, frames.reshape(slots, 128, C), two_bundles, two_others,
        finish_add,
    )
    return result.reshape(frames.shape)


def solution(mesh):
    torus = Mesh(mesh.devices.reshape(NZ, NY, NX, NC), AXES)
    group, row = ("z", "y"), ("x", "c")
    return jax.shard_map(
        per_device,
        mesh=torus,
        in_specs=(
            P(group, row, None, None),
            P(),
            P(group),
            P(group),
            P(None, None, None, group, None),
            P(None, None, None, group, None),
            P(),
            P(),
        ),
        out_specs=P(group, row, None, None),
        check_vma=False,
    )
```

```python
import jax
import jax.numpy as jnp
import numpy as np
from jax import lax
from jax.experimental import pallas as pl
from jax.experimental.pallas import tpu as pltpu
from jax.sharding import Mesh
from jax.sharding import PartitionSpec as P

NZ, NY, NX, NC = 8, 4, 4, 2
AXES = ("z", "y", "x", "c")
C = 384
SHARD = 12
HALF = 14
BUNDLE = 96
ROUND = (0, 1, -1, 2)

FETCH = np.array([[0, 4], [2, -2], [1, -3], [3, -1]])


def number(z, y, x, c):
    return ((z % NZ * NY + y % NY) * NX + x % NX) * NC + c


def fetch(array, source_of):
    pairs = []
    for z in range(NZ):
        for y in range(NY):
            for x in range(NX):
                for c in range(NC):
                    source = source_of(z, y, x, c)
                    if source is not None:
                        pairs.append((number(*source), number(z, y, x, c)))
    return lax.ppermute(array, AXES, pairs)


def z_source(which):
    def source(z, y, x, c):
        odd = z % 2
        from_z = z - odd + int(FETCH[(x + 2 * odd) % NX, which])
        return (from_z, y + 2 * odd - 1, x, c) if c == 0 else (from_z, y, x, c)

    return source


def small_source(step):
    return lambda z, y, x, c: (z, y, x + step, c) if c == 0 else (z, y + step, x, c)


def bulk_source(step):
    if step == 2:
        return lambda z, y, x, c: (z + 1 if z % 2 != c else z - 1, y, x, c)
    return lambda z, y, x, c: (z, y + step, x, c) if c == 0 else (z, y, x + step, c)


def sibling(z, y, x, c):
    return (z, y, x, 1 - c)


def own_half(kernel):
    start = lax.axis_index("c") * (27 - HALF)
    taps = lax.dynamic_slice_in_dim(kernel.reshape(27, SHARD, C), start, HALF, 0)
    return taps.reshape(HALF * SHARD, C)


def z_stage(own):
    return jnp.stack([fetch(own, z_source(0)), fetch(own, z_source(1))], 1)


def join_body(*refs):
    parts, out = refs[:-1], refs[-1]
    for tap in range(HALF):
        rows = [
            part[piece, pl.ds(SHARD * tap, SHARD), :].astype(jnp.float32)
            for part in parts
            for piece in range(2)
        ]
        out[tap] = jnp.concatenate(rows, 0).astype(jnp.bfloat16)


def join_rows(parts, which):
    block = pl.BlockSpec((None, 2, HALF * SHARD, C), lambda i: (which, 0, 0, 0))
    return pl.pallas_call(
        join_body,
        grid=(1,),
        out_shape=jax.ShapeDtypeStruct((HALF, BUNDLE, C), jnp.bfloat16),
        in_specs=[block] * 4,
        out_specs=pl.BlockSpec((HALF, BUNDLE, C), lambda i: (0, 0, 0)),
        compiler_params=pltpu.CompilerParams(vmem_limit_bytes=16 * 1024 * 1024),
        cost_estimate=pl.CostEstimate(flops=0, bytes_accessed=2_000_000, transcendentals=0),
    )(*parts)


def bulk_stage(bundle):
    return [bundle] + [fetch(bundle, bulk_source(step)) for step in ROUND[1:]]


def channel_orders():
    z, y, x = (lax.axis_index(a) for a in ("z", "y", "x"))
    table = jnp.asarray(FETCH, jnp.int32)
    around = jnp.array(ROUND, jnp.int32)
    aside = jnp.array((0, 1, -1, 0), jnp.int32)
    odd = z % 2
    at_z = z + jnp.array((0, 0, 0, 1), jnp.int32) * jnp.where(odd == 1, 1, -1)
    at_x = x + around[None, :] + 2 * (at_z % 2)[:, None]
    piece_z = (at_z - at_z % 2)[:, None, None] + table[at_x % NX]
    piece_y = (y + aside + 2 * (at_z % 2) - 1)[:, None, None]
    first = piece_z % NZ * NY + piece_y % NY
    at_z = z + jnp.array((0, 0, 0, 1), jnp.int32) * jnp.where(odd == 0, 1, -1)
    piece_z = (at_z - at_z % 2)[:, None] + table[(x + aside + 2 * (at_z % 2)) % NX]
    piece_y = y + around
    second = piece_z[:, None, :] % NZ * NY + piece_y[None, :, None] % NY
    ramp = jnp.arange(SHARD, dtype=jnp.int32)
    return jnp.stack([(half.reshape(-1, 1) * SHARD + ramp).reshape(C) for half in (first, second)])


def picks_body(order, out):
    for half in range(2):
        out[half] = (
            lax.broadcasted_iota(jnp.int32, (C, C), 0) == order[half : half + 1, :]
        ).astype(jnp.bfloat16)


def make_picks(orders):
    vmem = pl.BlockSpec(memory_space=pltpu.VMEM)
    return pl.pallas_call(
        picks_body,
        out_shape=jax.ShapeDtypeStruct((2, C, C), jnp.bfloat16),
        in_specs=[vmem],
        out_specs=vmem,
        cost_estimate=pl.CostEstimate(flops=1000, bytes_accessed=1000, transcendentals=0),
    )(orders)


def spread_cells(cells, pick):
    rows = cells.shape[0]
    plain = jnp.dot(cells, pick, preferred_element_type=jnp.float32)
    col = lax.broadcasted_iota(jnp.int32, (rows, C), 0) % 32
    before = jnp.where(col == 0, 0.0, pltpu.roll(plain, 1, 0))
    after = jnp.where(col == 31, 0.0, pltpu.roll(plain, rows - 1, 0))
    return [part.astype(jnp.bfloat16) for part in (before, plain, after)]


def spread_inner_body(picks, acts, out):
    for half in range(2):
        for tap, part in enumerate(spread_cells(acts[...], picks[half])):
            out[half, 2:8, 1:5, :, C * tap : C * (tap + 1)] = part.reshape(6, 4, 32, C)


def spread_inner(picks, acts):
    vmem = pl.BlockSpec(memory_space=pltpu.VMEM)
    return pl.pallas_call(
        spread_inner_body,
        out_shape=jax.ShapeDtypeStruct((2, 8, 6, 32, 3 * C), jnp.bfloat16),
        in_specs=[vmem] * 2,
        out_specs=vmem,
        compiler_params=pltpu.CompilerParams(vmem_limit_bytes=20 * 1024 * 1024),
        cost_estimate=pl.CostEstimate(flops=1000, bytes_accessed=1000, transcendentals=0),
    )(picks, acts.reshape(-1, C))


def spread_halo_body(scalars, picks, ends, corners, beside, across, _, out):
    core = scalars[0]
    cells = jnp.concatenate(
        [part[...].reshape(-1, C) for part in (ends, beside, corners, across)], 0
    )
    for half in range(2):
        for tap, part in enumerate(spread_cells(cells, picks[half])):
            lanes = slice(C * tap, C * (tap + 1))
            out[half, 0:2, 1:5, :, lanes] = part[0:256].reshape(2, 4, 32, C)
            near, far = part[256:512].reshape(8, 1, 32, C), part[512:768].reshape(8, 1, 32, C)

            @pl.when(core == 0)
            def _():
                out[half, :, 0:1, :, lanes] = far
                out[half, :, 5:6, :, lanes] = near

            @pl.when(core == 1)
            def _():
                out[half, :, 0:1, :, lanes] = near
                out[half, :, 5:6, :, lanes] = far


def spread_halo(scalars, picks, ends, corners, beside, across, spread):
    vmem = pl.BlockSpec(memory_space=pltpu.VMEM)
    return pl.pallas_call(
        spread_halo_body,
        out_shape=jax.ShapeDtypeStruct(spread.shape, spread.dtype),
        in_specs=[pl.BlockSpec(memory_space=pltpu.SMEM)] + [vmem] * 6,
        out_specs=vmem,
        input_output_aliases={6: 0},
        compiler_params=pltpu.CompilerParams(vmem_limit_bytes=20 * 1024 * 1024),
        cost_estimate=pl.CostEstimate(flops=1000, bytes_accessed=1000, transcendentals=0),
    )(scalars, picks, ends, corners, beside, across, spread)


def conv_body(
    scalars, lag_weights, spread, tail, own0, own1, own2, own3, got0, got1, got2, got3,
    out, weights, total, sems, *, finish,
):
    frames, rows, cols = 6, 4, 32
    own, got = (own0, own1, own2, own3), (got0, got1, got2, got3)

    def copies(half, sources):
        return [
            pltpu.make_async_copy(
                sources[k], weights.at[half, :, pl.ds(BUNDLE * k, BUNDLE), :], sems.at[half, k]
            )
            for k in range(4)
        ]

    core = scalars[0]

    @pl.when(core == 0)
    def _():
        for copy in copies(0, own) + copies(1, got):
            copy.start()

    @pl.when(core == 1)
    def _():
        for copy in copies(0, got) + copies(1, own):
            copy.start()

    total[...] = jnp.zeros_like(total)

    def window(half, lag, row, first, count):
        block = spread[half, pl.ds(lag, frames), pl.ds(row, rows), :, pl.ds(C * first, C * count)]
        return block.reshape(frames * rows * cols, C * count)

    def add(lag, part):
        part = part.reshape(frames, rows * cols, C)
        for f in range(frames):
            total[f] += part[f] * lag_weights[lag, f]

    def group(half, first_tap, index):
        lag, row = index // 3, index % 3
        block = weights[half, pl.ds(index * 3 - first_tap, 3)].reshape(3 * C, C)
        add(lag, jnp.dot(window(half, lag, row, 0, 3), block, preferred_element_type=jnp.float32))

    for copy in copies(0, own):
        copy.wait()

    @pl.loop(0, 4)
    def _(index):
        group(0, 0, index)

    add(
        1,
        jnp.dot(
            window(0, 1, 1, 0, 2),
            weights[0, pl.ds(12, 2)].reshape(2 * C, C),
            preferred_element_type=jnp.float32,
        ),
    )
    for copy in copies(1, own):
        copy.wait()
    add(
        1,
        jnp.dot(window(1, 1, 1, 2, 1), weights[1, 1], preferred_element_type=jnp.float32),
    )

    @pl.loop(5, 9)
    def _(index):
        group(1, 13, index)

    finish(scalars, total, tail, out)


def finish_norm(scalars, total, tail, out):
    for f in range(6):
        data = total[f]
        scale = lax.rsqrt(jnp.mean(data * data, axis=-1, keepdims=True) + 1e-06)
        lifted = data * scale * tail[...]
        out[f] = (lifted * (1.0 / (1.0 + jnp.exp(-lifted)))).astype(jnp.bfloat16)


def finish_add(scalars, total, tail, out):
    for f in range(6):
        summed = tail[f].astype(jnp.float32) + total[f]
        out[f] = jnp.where(f < scalars[1], summed, 0.0).astype(jnp.bfloat16)


def conv(scalars, lag_weights, spread, tail, own, got, finish):
    smem = pl.BlockSpec(memory_space=pltpu.SMEM)
    vmem = pl.BlockSpec(memory_space=pltpu.VMEM)
    return pl.pallas_call(
        lambda *refs: conv_body(*refs, finish=finish),
        out_shape=jax.ShapeDtypeStruct((6, 128, C), jnp.bfloat16),
        in_specs=[smem, smem] + [vmem] * 2 + [pl.BlockSpec(memory_space=pl.ANY)] * 8,
        out_specs=vmem,
        scratch_shapes=[
            pltpu.VMEM((2, HALF, C, C), jnp.bfloat16),
            pltpu.VMEM((6, 128, C), jnp.float32),
            pltpu.SemaphoreType.DMA((2, 4)),
        ],
        compiler_params=pltpu.CompilerParams(vmem_limit_bytes=26 * 1024 * 1024),
        cost_estimate=pl.CostEstimate(flops=1000, bytes_accessed=1000, transcendentals=0),
    )(scalars, lag_weights, spread, tail, *own, *got)


def clip_positions(clip_lengths, frame_index):
    ends = jnp.cumsum(clip_lengths)
    begins = jnp.max(jnp.where(ends[None, :] <= frame_index[:, None], ends[None, :], 0), axis=1)
    return frame_index - begins


def norm_act(values, gain):
    data = values.astype(jnp.float32)
    mean_square = jnp.mean(data * data, axis=-1, keepdims=True)
    scaled = data * lax.rsqrt(mean_square + 1e-06)
    return jax.nn.silu(scaled * gain).astype(jnp.bfloat16)


def before_in_group(z, y, x, c):
    group = z * NY + y - 1
    return None if group < 0 else (group // NY, group % NY, x, c)


def across_chips(z, y, x, c):
    x = x - 1 if c == 0 else x + 1
    return (z, y, x, 1 - c) if 0 <= x < NX else None


def across_and_before(z, y, x, c):
    place = across_chips(z, y, x, c)
    return None if place is None else before_in_group(*place)


def per_device(
    frames, clip_lengths, group_start, group_count, kernel_one, kernel_two, gain_one, gain_two
):
    slots = frames.shape[0]
    slot = jnp.arange(slots, dtype=jnp.int32)
    position = clip_positions(clip_lengths, group_start[0] + slot)
    lag_weights = jnp.stack([position >= 2, position >= 1, position >= 0]).astype(jnp.float32)
    scalars = jnp.stack([lax.axis_index("c").astype(jnp.int32), group_count[0]])
    orders = channel_orders()

    first_core = lax.axis_index("c") == 0
    last = group_count[0] - 2

    def sides(acts):
        return (
            jnp.where(first_core, acts[:, 3:4], acts[:, 0:1]),
            jnp.where(first_core, acts[:, 0:1], acts[:, 3:4]),
        )

    def last_two(acts):
        return lax.dynamic_slice_in_dim(acts, last, 2, 0)

    acts_one = norm_act(frames, gain_one)
    own = jnp.stack([own_half(kernel_one), own_half(kernel_two)])
    pieces = z_stage(own)
    inner, outer = sides(acts_one)
    beside, across = fetch(inner, sibling), fetch(outer, across_chips)
    ends = jnp.concatenate([last_two(acts_one), last_two(beside)], 1)
    ends, corners = fetch(ends, before_in_group), fetch(last_two(outer), across_and_before)
    picks = make_picks(orders)
    pieces, picks, lag_weights, scalars = lax.optimization_barrier(
        (pieces, picks, lag_weights, scalars)
    )

    opposite = fetch(pieces, small_source(2))
    after = fetch(pieces, small_source(1))
    gated, ends, corners, across = lax.optimization_barrier((pieces, ends, corners, across))
    parts = [pieces, after, fetch(gated, small_source(-1)), opposite]
    beside = jnp.concatenate([ends[:, 4:5], beside], 0)
    spread = spread_halo(
        scalars, picks, ends[:, 0:4], corners, beside, across, spread_inner(picks, acts_one)
    )
    parts, spread = lax.optimization_barrier((parts, spread))

    one_bundle, two_bundle = join_rows(parts, 0), join_rows(parts, 1)
    one_bundles = bulk_stage(one_bundle)
    one_own, two_own = lax.optimization_barrier((one_bundle, two_bundle))
    one_others, two_others = [fetch(one_own, sibling)], [fetch(two_own, sibling)]
    two_bundle, one_others, two_others = lax.optimization_barrier(
        (two_bundle, one_others, two_others)
    )
    one_bundles, one_others, two_others = lax.optimization_barrier(
        (one_bundles, one_others, two_others)
    )
    one_others += [fetch(b, sibling) for b in one_bundles[1:]]

    two_bundles = bulk_stage(two_bundle)
    acts_two = conv(
        scalars, lag_weights, spread, gain_two.reshape(1, C), one_bundles, one_others, finish_norm
    ).reshape(frames.shape)

    two_bundles, acts_two = lax.optimization_barrier((two_bundles, acts_two))
    inner, outer = sides(acts_two)
    ends, corners, outer = lax.optimization_barrier((last_two(acts_two), last_two(outer), outer))
    ends = fetch(ends, before_in_group)
    across = fetch(outer, across_chips)
    corners = fetch(corners, across_and_before)
    two_others += [fetch(b, sibling) for b in two_bundles[1:3]]
    spread = spread_inner(picks, acts_two)
    ends, corners, across, spread, two_others = lax.optimization_barrier(
        (ends, corners, across, spread, two_others)
    )
    beside = fetch(jnp.concatenate([sides(ends)[0], inner], 0), sibling)
    two_last, beside = lax.optimization_barrier((two_bundles[3], beside))
    two_others.append(fetch(two_last, sibling))
    spread = spread_halo(scalars, picks, ends, corners, beside, across, spread)
    result = conv(
        scalars, lag_weights, spread, frames.reshape(slots, 128, C), two_bundles, two_others,
        finish_add,
    )
    return result.reshape(frames.shape)


def solution(mesh):
    torus = Mesh(mesh.devices.reshape(NZ, NY, NX, NC), AXES)
    group, row = ("z", "y"), ("x", "c")
    return jax.shard_map(
        per_device,
        mesh=torus,
        in_specs=(
            P(group, row, None, None),
            P(),
            P(group),
            P(group),
            P(None, None, None, group, None),
            P(None, None, None, group, None),
            P(),
            P(),
        ),
        out_specs=P(group, row, None, None),
        check_vma=False,
    )
```

```python
import jax
import jax.numpy as jnp
import numpy as np
from jax import lax
from jax.experimental import pallas as pl
from jax.experimental.pallas import tpu as pltpu
from jax.sharding import Mesh
from jax.sharding import PartitionSpec as P

NZ, NY, NX, NC = 8, 4, 4, 2
AXES = ("z", "y", "x", "c")
C = 384
SHARD = 12
HALF = 14
BUNDLE = 96
ROUND = (0, 1, -1, 2)

FETCH = np.array([[0, 4], [2, -2], [1, -3], [3, -1]])


def number(z, y, x, c):
    return ((z % NZ * NY + y % NY) * NX + x % NX) * NC + c


def fetch(array, source_of):
    pairs = []
    for z in range(NZ):
        for y in range(NY):
            for x in range(NX):
                for c in range(NC):
                    source = source_of(z, y, x, c)
                    if source is not None:
                        pairs.append((number(*source), number(z, y, x, c)))
    return lax.ppermute(array, AXES, pairs)


def z_source(which):
    def source(z, y, x, c):
        odd = z % 2
        from_z = z - odd + int(FETCH[(x + 2 * odd) % NX, which])
        return (from_z, y + 2 * odd - 1, x, c) if c == 0 else (from_z, y, x, c)

    return source


def small_source(step):
    return lambda z, y, x, c: (z, y, x + step, c) if c == 0 else (z, y + step, x, c)


def bulk_source(step):
    if step == 2:
        return lambda z, y, x, c: (z + 1 if z % 2 != c else z - 1, y, x, c)
    return lambda z, y, x, c: (z, y + step, x, c) if c == 0 else (z, y, x + step, c)


def sibling(z, y, x, c):
    return (z, y, x, 1 - c)


def own_half(kernel):
    start = lax.axis_index("c") * (27 - HALF)
    taps = lax.dynamic_slice_in_dim(kernel.reshape(27, SHARD, C), start, HALF, 0)
    return taps.reshape(HALF * SHARD, C)


def z_stage(own):
    return jnp.stack([fetch(own, z_source(0)), fetch(own, z_source(1))], 1)


def join_body(*refs):
    parts, out = refs[:-1], refs[-1]
    for tap in range(HALF):
        rows = [
            part[piece, pl.ds(SHARD * tap, SHARD), :].astype(jnp.float32)
            for part in parts
            for piece in range(2)
        ]
        out[tap] = jnp.concatenate(rows, 0).astype(jnp.bfloat16)


def join_rows(parts, which):
    block = pl.BlockSpec((None, 2, HALF * SHARD, C), lambda i: (which, 0, 0, 0))
    return pl.pallas_call(
        join_body,
        grid=(1,),
        out_shape=jax.ShapeDtypeStruct((HALF, BUNDLE, C), jnp.bfloat16),
        in_specs=[block] * 4,
        out_specs=pl.BlockSpec((HALF, BUNDLE, C), lambda i: (0, 0, 0)),
        compiler_params=pltpu.CompilerParams(vmem_limit_bytes=16 * 1024 * 1024),
        cost_estimate=pl.CostEstimate(flops=0, bytes_accessed=2_000_000, transcendentals=0),
    )(*parts)


def bulk_stage(bundle):
    return [bundle] + [fetch(bundle, bulk_source(step)) for step in ROUND[1:]]


def channel_orders():
    z, y, x = (lax.axis_index(a) for a in ("z", "y", "x"))
    table = jnp.asarray(FETCH, jnp.int32)
    around = jnp.array(ROUND, jnp.int32)
    aside = jnp.array((0, 1, -1, 0), jnp.int32)
    odd = z % 2
    at_z = z + jnp.array((0, 0, 0, 1), jnp.int32) * jnp.where(odd == 1, 1, -1)
    at_x = x + around[None, :] + 2 * (at_z % 2)[:, None]
    piece_z = (at_z - at_z % 2)[:, None, None] + table[at_x % NX]
    piece_y = (y + aside + 2 * (at_z % 2) - 1)[:, None, None]
    first = piece_z % NZ * NY + piece_y % NY
    at_z = z + jnp.array((0, 0, 0, 1), jnp.int32) * jnp.where(odd == 0, 1, -1)
    piece_z = (at_z - at_z % 2)[:, None] + table[(x + aside + 2 * (at_z % 2)) % NX]
    piece_y = y + around
    second = piece_z[:, None, :] % NZ * NY + piece_y[None, :, None] % NY
    ramp = jnp.arange(SHARD, dtype=jnp.int32)
    return jnp.stack([(half.reshape(-1, 1) * SHARD + ramp).reshape(C) for half in (first, second)])


def picks_body(order, out):
    for half in range(2):
        out[half] = (
            lax.broadcasted_iota(jnp.int32, (C, C), 0) == order[half : half + 1, :]
        ).astype(jnp.bfloat16)


def make_picks(orders):
    vmem = pl.BlockSpec(memory_space=pltpu.VMEM)
    return pl.pallas_call(
        picks_body,
        out_shape=jax.ShapeDtypeStruct((2, C, C), jnp.bfloat16),
        in_specs=[vmem],
        out_specs=vmem,
        cost_estimate=pl.CostEstimate(flops=1000, bytes_accessed=1000, transcendentals=0),
    )(orders)


def spread_cells(cells, pick):
    rows = cells.shape[0]
    plain = jnp.dot(cells, pick, preferred_element_type=jnp.float32)
    col = lax.broadcasted_iota(jnp.int32, (rows, C), 0) % 32
    before = jnp.where(col == 0, 0.0, pltpu.roll(plain, 1, 0))
    after = jnp.where(col == 31, 0.0, pltpu.roll(plain, rows - 1, 0))
    return [part.astype(jnp.bfloat16) for part in (before, plain, after)]


def spread_inner_body(picks, acts, out):
    for half in range(2):
        for tap, part in enumerate(spread_cells(acts[...], picks[half])):
            out[half, 2:8, 1:5, :, C * tap : C * (tap + 1)] = part.reshape(6, 4, 32, C)


def spread_inner(picks, acts):
    vmem = pl.BlockSpec(memory_space=pltpu.VMEM)
    return pl.pallas_call(
        spread_inner_body,
        out_shape=jax.ShapeDtypeStruct((2, 8, 6, 32, 3 * C), jnp.bfloat16),
        in_specs=[vmem] * 2,
        out_specs=vmem,
        compiler_params=pltpu.CompilerParams(vmem_limit_bytes=20 * 1024 * 1024),
        cost_estimate=pl.CostEstimate(flops=1000, bytes_accessed=1000, transcendentals=0),
    )(picks, acts.reshape(-1, C))


def spread_halo_body(scalars, picks, ends, beside, across, _, out):
    core = scalars[0]
    cells = jnp.concatenate(
        [part[...].reshape(-1, C) for part in (ends, beside, across)], 0
    )
    for half in range(2):
        for tap, part in enumerate(spread_cells(cells, picks[half])):
            lanes = slice(C * tap, C * (tap + 1))
            out[half, 0:2, 1:5, :, lanes] = part[0:256].reshape(2, 4, 32, C)
            near, far = part[256:512].reshape(8, 1, 32, C), part[512:768].reshape(8, 1, 32, C)

            @pl.when(core == 0)
            def _():
                out[half, :, 0:1, :, lanes] = far
                out[half, :, 5:6, :, lanes] = near

            @pl.when(core == 1)
            def _():
                out[half, :, 0:1, :, lanes] = near
                out[half, :, 5:6, :, lanes] = far


def spread_halo(scalars, picks, ends, beside, across, spread):
    vmem = pl.BlockSpec(memory_space=pltpu.VMEM)
    return pl.pallas_call(
        spread_halo_body,
        out_shape=jax.ShapeDtypeStruct(spread.shape, spread.dtype),
        in_specs=[pl.BlockSpec(memory_space=pltpu.SMEM)] + [vmem] * 5,
        out_specs=vmem,
        input_output_aliases={5: 0},
        compiler_params=pltpu.CompilerParams(vmem_limit_bytes=20 * 1024 * 1024),
        cost_estimate=pl.CostEstimate(flops=1000, bytes_accessed=1000, transcendentals=0),
    )(scalars, picks, ends, beside, across, spread)


def conv_body(
    scalars, lag_weights, spread, tail, own0, own1, own2, own3, got0, got1, got2, got3,
    out, weights, total, sems, *, finish,
):
    frames, rows, cols = 6, 4, 32
    own, got = (own0, own1, own2, own3), (got0, got1, got2, got3)

    def copies(half, sources):
        return [
            pltpu.make_async_copy(
                sources[k], weights.at[half, :, pl.ds(BUNDLE * k, BUNDLE), :], sems.at[half, k]
            )
            for k in range(4)
        ]

    core = scalars[0]

    @pl.when(core == 0)
    def _():
        for copy in copies(0, own) + copies(1, got):
            copy.start()

    @pl.when(core == 1)
    def _():
        for copy in copies(0, got) + copies(1, own):
            copy.start()

    total[...] = jnp.zeros_like(total)

    def window(half, lag, row, first, count):
        block = spread[half, pl.ds(lag, frames), pl.ds(row, rows), :, pl.ds(C * first, C * count)]
        return block.reshape(frames * rows * cols, C * count)

    def add(lag, part):
        part = part.reshape(frames, rows * cols, C)
        for f in range(frames):
            total[f] += part[f] * lag_weights[lag, f]

    def group(half, first_tap, index):
        lag, row = index // 3, index % 3
        block = weights[half, pl.ds(index * 3 - first_tap, 3)].reshape(3 * C, C)
        add(lag, jnp.dot(window(half, lag, row, 0, 3), block, preferred_element_type=jnp.float32))

    for copy in copies(0, own):
        copy.wait()

    @pl.loop(0, 4)
    def _(index):
        group(0, 0, index)

    add(
        1,
        jnp.dot(
            window(0, 1, 1, 0, 2),
            weights[0, pl.ds(12, 2)].reshape(2 * C, C),
            preferred_element_type=jnp.float32,
        ),
    )
    for copy in copies(1, own):
        copy.wait()
    add(
        1,
        jnp.dot(window(1, 1, 1, 2, 1), weights[1, 1], preferred_element_type=jnp.float32),
    )

    @pl.loop(5, 9)
    def _(index):
        group(1, 13, index)

    finish(scalars, total, tail, out)


def finish_norm(scalars, total, tail, out):
    for f in range(6):
        data = total[f]
        scale = lax.rsqrt(jnp.mean(data * data, axis=-1, keepdims=True) + 1e-06)
        lifted = data * scale * tail[...]
        out[f] = (lifted * (1.0 / (1.0 + jnp.exp(-lifted)))).astype(jnp.bfloat16)


def finish_add(scalars, total, tail, out):
    for f in range(6):
        summed = tail[f].astype(jnp.float32) + total[f]
        out[f] = jnp.where(f < scalars[1], summed, 0.0).astype(jnp.bfloat16)


def conv(scalars, lag_weights, spread, tail, own, got, finish):
    smem = pl.BlockSpec(memory_space=pltpu.SMEM)
    vmem = pl.BlockSpec(memory_space=pltpu.VMEM)
    return pl.pallas_call(
        lambda *refs: conv_body(*refs, finish=finish),
        out_shape=jax.ShapeDtypeStruct((6, 128, C), jnp.bfloat16),
        in_specs=[smem, smem] + [vmem] * 2 + [pl.BlockSpec(memory_space=pl.ANY)] * 8,
        out_specs=vmem,
        scratch_shapes=[
            pltpu.VMEM((2, HALF, C, C), jnp.bfloat16),
            pltpu.VMEM((6, 128, C), jnp.float32),
            pltpu.SemaphoreType.DMA((2, 4)),
        ],
        compiler_params=pltpu.CompilerParams(vmem_limit_bytes=26 * 1024 * 1024),
        cost_estimate=pl.CostEstimate(flops=1000, bytes_accessed=1000, transcendentals=0),
    )(scalars, lag_weights, spread, tail, *own, *got)


def clip_positions(clip_lengths, frame_index):
    ends = jnp.cumsum(clip_lengths)
    begins = jnp.max(jnp.where(ends[None, :] <= frame_index[:, None], ends[None, :], 0), axis=1)
    return frame_index - begins


def norm_act(values, gain):
    data = values.astype(jnp.float32)
    mean_square = jnp.mean(data * data, axis=-1, keepdims=True)
    scaled = data * lax.rsqrt(mean_square + 1e-06)
    return jax.nn.silu(scaled * gain).astype(jnp.bfloat16)


def before_in_group(z, y, x, c):
    group = z * NY + y - 1
    return None if group < 0 else (group // NY, group % NY, x, c)


def across_chips(z, y, x, c):
    x = x - 1 if c == 0 else x + 1
    return (z, y, x, 1 - c) if 0 <= x < NX else None


def across_and_before(z, y, x, c):
    place = across_chips(z, y, x, c)
    return None if place is None else before_in_group(*place)


def per_device(
    frames, clip_lengths, group_start, group_count, kernel_one, kernel_two, gain_one, gain_two
):
    slots = frames.shape[0]
    slot = jnp.arange(slots, dtype=jnp.int32)
    position = clip_positions(clip_lengths, group_start[0] + slot)
    lag_weights = jnp.stack([position >= 2, position >= 1, position >= 0]).astype(jnp.float32)
    scalars = jnp.stack([lax.axis_index("c").astype(jnp.int32), group_count[0]])
    orders = channel_orders()

    first_core = lax.axis_index("c") == 0
    last = group_count[0] - 2

    def sides(acts):
        return (
            jnp.where(first_core, acts[:, 3:4], acts[:, 0:1]),
            jnp.where(first_core, acts[:, 0:1], acts[:, 3:4]),
        )

    def last_two(acts):
        return lax.dynamic_slice_in_dim(acts, last, 2, 0)

    acts_one = norm_act(frames, gain_one)
    own = jnp.stack([own_half(kernel_one), own_half(kernel_two)])
    pieces = z_stage(own)
    ends = fetch(last_two(acts_one), before_in_group)
    picks = make_picks(orders)
    pieces, picks, lag_weights, scalars = lax.optimization_barrier(
        (pieces, picks, lag_weights, scalars)
    )

    opposite = fetch(pieces, small_source(2))
    after = fetch(pieces, small_source(1))
    gated, ends = lax.optimization_barrier((pieces, ends))
    parts = [pieces, after, fetch(gated, small_source(-1)), opposite]
    inner, outer = sides(jnp.concatenate([ends, acts_one], 0))
    across = fetch(outer, across_chips)
    parts, across = lax.optimization_barrier((parts, across))

    one_bundle, two_bundle = join_rows(parts, 0), join_rows(parts, 1)
    one_bundles = bulk_stage(one_bundle)
    one_own, two_own = lax.optimization_barrier((one_bundle, two_bundle))
    one_others, two_others = [fetch(one_own, sibling)], [fetch(two_own, sibling)]
    two_bundle, one_others, two_others, inner = lax.optimization_barrier(
        (two_bundle, one_others, two_others, inner)
    )
    beside = fetch(inner, sibling)
    spread = spread_halo(scalars, picks, ends, beside, across, spread_inner(picks, acts_one))
    one_bundles, one_others, two_others, spread = lax.optimization_barrier(
        (one_bundles, one_others, two_others, spread)
    )
    one_others += [fetch(b, sibling) for b in one_bundles[1:]]

    two_bundles = bulk_stage(two_bundle)
    acts_two = conv(
        scalars, lag_weights, spread, gain_two.reshape(1, C), one_bundles, one_others, finish_norm
    ).reshape(frames.shape)

    two_bundles, acts_two = lax.optimization_barrier((two_bundles, acts_two))
    inner, outer = sides(acts_two)
    ends, corners, outer = lax.optimization_barrier((last_two(acts_two), last_two(outer), outer))
    ends = fetch(ends, before_in_group)
    across = fetch(outer, across_chips)
    corners = fetch(corners, across_and_before)
    two_others += [fetch(b, sibling) for b in two_bundles[1:3]]
    spread = spread_inner(picks, acts_two)
    ends, corners, across, spread, two_others = lax.optimization_barrier(
        (ends, corners, across, spread, two_others)
    )
    beside = fetch(jnp.concatenate([sides(ends)[0], inner], 0), sibling)
    two_last, beside = lax.optimization_barrier((two_bundles[3], beside))
    two_others.append(fetch(two_last, sibling))
    across = jnp.concatenate([corners, across], 0)
    spread = spread_halo(scalars, picks, ends, beside, across, spread)
    result = conv(
        scalars, lag_weights, spread, frames.reshape(slots, 128, C), two_bundles, two_others,
        finish_add,
    )
    return result.reshape(frames.shape)


def solution(mesh):
    torus = Mesh(mesh.devices.reshape(NZ, NY, NX, NC), AXES)
    group, row = ("z", "y"), ("x", "c")
    return jax.shard_map(
        per_device,
        mesh=torus,
        in_specs=(
            P(group, row, None, None),
            P(),
            P(group),
            P(group),
            P(None, None, None, group, None),
            P(None, None, None, group, None),
            P(),
            P(),
        ),
        out_specs=P(group, row, None, None),
        check_vma=False,
    )
```

```python
import jax
import jax.numpy as jnp
import numpy as np
from jax import lax
from jax.experimental import pallas as pl
from jax.experimental.pallas import tpu as pltpu
from jax.sharding import Mesh
from jax.sharding import PartitionSpec as P

NZ, NY, NX, NC = 8, 4, 4, 2
AXES = ("z", "y", "x", "c")
C = 384
SHARD = 12
HALF = 14
BUNDLE = 96
ROUND = (0, 1, -1, 2)

FETCH = np.array([[0, 4], [2, -2], [1, -3], [3, -1]])


def number(z, y, x, c):
    return ((z % NZ * NY + y % NY) * NX + x % NX) * NC + c


def fetch(array, source_of):
    pairs = []
    for z in range(NZ):
        for y in range(NY):
            for x in range(NX):
                for c in range(NC):
                    source = source_of(z, y, x, c)
                    if source is not None:
                        pairs.append((number(*source), number(z, y, x, c)))
    return lax.ppermute(array, AXES, pairs)


def z_source(which):
    def source(z, y, x, c):
        odd = z % 2
        from_z = z - odd + int(FETCH[(x + 2 * odd) % NX, which])
        return (from_z, y + 2 * odd - 1, x, c) if c == 0 else (from_z, y, x, c)

    return source


def small_source(step):
    return lambda z, y, x, c: (z, y, x + step, c) if c == 0 else (z, y + step, x, c)


def bulk_source(step):
    if step == 2:
        return lambda z, y, x, c: (z + 1 if z % 2 != c else z - 1, y, x, c)
    return lambda z, y, x, c: (z, y + step, x, c) if c == 0 else (z, y, x + step, c)


def sibling(z, y, x, c):
    return (z, y, x, 1 - c)


def own_half(kernel):
    start = lax.axis_index("c") * (27 - HALF)
    taps = lax.dynamic_slice_in_dim(kernel.reshape(27, SHARD, C), start, HALF, 0)
    return taps.reshape(HALF * SHARD, C)


def z_stage(own):
    return jnp.stack([fetch(own, z_source(0)), fetch(own, z_source(1))], 1)


def join_body(*refs):
    parts, out = refs[:-1], refs[-1]
    for tap in range(HALF):
        rows = [
            part[piece, pl.ds(SHARD * tap, SHARD), :].astype(jnp.float32)
            for part in parts
            for piece in range(2)
        ]
        out[tap] = jnp.concatenate(rows, 0).astype(jnp.bfloat16)


def join_rows(parts, which):
    block = pl.BlockSpec((None, 2, HALF * SHARD, C), lambda i: (which, 0, 0, 0))
    return pl.pallas_call(
        join_body,
        grid=(1,),
        out_shape=jax.ShapeDtypeStruct((HALF, BUNDLE, C), jnp.bfloat16),
        in_specs=[block] * 4,
        out_specs=pl.BlockSpec((HALF, BUNDLE, C), lambda i: (0, 0, 0)),
        compiler_params=pltpu.CompilerParams(vmem_limit_bytes=16 * 1024 * 1024),
        cost_estimate=pl.CostEstimate(flops=0, bytes_accessed=2_000_000, transcendentals=0),
    )(*parts)


def bulk_stage(bundle):
    return [bundle] + [fetch(bundle, bulk_source(step)) for step in ROUND[1:]]


def channel_orders():
    z, y, x = (lax.axis_index(a) for a in ("z", "y", "x"))
    table = jnp.asarray(FETCH, jnp.int32)
    around = jnp.array(ROUND, jnp.int32)
    aside = jnp.array((0, 1, -1, 0), jnp.int32)
    odd = z % 2
    at_z = z + jnp.array((0, 0, 0, 1), jnp.int32) * jnp.where(odd == 1, 1, -1)
    at_x = x + around[None, :] + 2 * (at_z % 2)[:, None]
    piece_z = (at_z - at_z % 2)[:, None, None] + table[at_x % NX]
    piece_y = (y + aside + 2 * (at_z % 2) - 1)[:, None, None]
    first = piece_z % NZ * NY + piece_y % NY
    at_z = z + jnp.array((0, 0, 0, 1), jnp.int32) * jnp.where(odd == 0, 1, -1)
    piece_z = (at_z - at_z % 2)[:, None] + table[(x + aside + 2 * (at_z % 2)) % NX]
    piece_y = y + around
    second = piece_z[:, None, :] % NZ * NY + piece_y[None, :, None] % NY
    ramp = jnp.arange(SHARD, dtype=jnp.int32)
    return jnp.stack([(half.reshape(-1, 1) * SHARD + ramp).reshape(C) for half in (first, second)])


def picks_body(order, out):
    for half in range(2):
        out[half] = (
            lax.broadcasted_iota(jnp.int32, (C, C), 0) == order[half : half + 1, :]
        ).astype(jnp.bfloat16)


def make_picks(orders):
    vmem = pl.BlockSpec(memory_space=pltpu.VMEM)
    return pl.pallas_call(
        picks_body,
        out_shape=jax.ShapeDtypeStruct((2, C, C), jnp.bfloat16),
        in_specs=[vmem],
        out_specs=vmem,
        cost_estimate=pl.CostEstimate(flops=1000, bytes_accessed=1000, transcendentals=0),
    )(orders)


def spread_cells(cells, pick):
    rows = cells.shape[0]
    plain = jnp.dot(cells, pick, preferred_element_type=jnp.float32)
    col = lax.broadcasted_iota(jnp.int32, (rows, C), 0) % 32
    before = jnp.where(col == 0, 0.0, pltpu.roll(plain, 1, 0))
    after = jnp.where(col == 31, 0.0, pltpu.roll(plain, rows - 1, 0))
    return [part.astype(jnp.bfloat16) for part in (before, plain, after)]


def spread_inner_body(picks, acts, out):
    for half in range(2):
        for tap, part in enumerate(spread_cells(acts[...], picks[half])):
            out[half, 2:8, 1:5, :, C * tap : C * (tap + 1)] = part.reshape(6, 4, 32, C)


def spread_inner(picks, acts):
    vmem = pl.BlockSpec(memory_space=pltpu.VMEM)
    return pl.pallas_call(
        spread_inner_body,
        out_shape=jax.ShapeDtypeStruct((2, 8, 6, 32, 3 * C), jnp.bfloat16),
        in_specs=[vmem] * 2,
        out_specs=vmem,
        compiler_params=pltpu.CompilerParams(vmem_limit_bytes=20 * 1024 * 1024),
        cost_estimate=pl.CostEstimate(flops=1000, bytes_accessed=1000, transcendentals=0),
    )(picks, acts.reshape(-1, C))


def spread_halo_body(scalars, picks, ends, beside, across, _, out):
    core = scalars[0]
    cells = jnp.concatenate(
        [part[...].reshape(-1, C) for part in (ends, beside, across)], 0
    )
    for half in range(2):
        for tap, part in enumerate(spread_cells(cells, picks[half])):
            lanes = slice(C * tap, C * (tap + 1))
            out[half, 0:2, 1:5, :, lanes] = part[0:256].reshape(2, 4, 32, C)
            near, far = part[256:512].reshape(8, 1, 32, C), part[512:768].reshape(8, 1, 32, C)

            @pl.when(core == 0)
            def _():
                out[half, :, 0:1, :, lanes] = far
                out[half, :, 5:6, :, lanes] = near

            @pl.when(core == 1)
            def _():
                out[half, :, 0:1, :, lanes] = near
                out[half, :, 5:6, :, lanes] = far


def spread_halo(scalars, picks, ends, beside, across, spread):
    vmem = pl.BlockSpec(memory_space=pltpu.VMEM)
    return pl.pallas_call(
        spread_halo_body,
        out_shape=jax.ShapeDtypeStruct(spread.shape, spread.dtype),
        in_specs=[pl.BlockSpec(memory_space=pltpu.SMEM)] + [vmem] * 5,
        out_specs=vmem,
        input_output_aliases={5: 0},
        compiler_params=pltpu.CompilerParams(vmem_limit_bytes=20 * 1024 * 1024),
        cost_estimate=pl.CostEstimate(flops=1000, bytes_accessed=1000, transcendentals=0),
    )(scalars, picks, ends, beside, across, spread)


def conv_body(
    scalars, lag_weights, spread, tail, own0, own1, own2, own3, got0, got1, got2, got3,
    out, weights, total, sems, *, finish,
):
    frames, rows, cols = 6, 4, 32
    own, got = (own0, own1, own2, own3), (got0, got1, got2, got3)

    def copies(half, sources):
        return [
            pltpu.make_async_copy(
                sources[k], weights.at[half, :, pl.ds(BUNDLE * k, BUNDLE), :], sems.at[half, k]
            )
            for k in range(4)
        ]

    core = scalars[0]

    @pl.when(core == 0)
    def _():
        for copy in copies(0, own) + copies(1, got):
            copy.start()

    @pl.when(core == 1)
    def _():
        for copy in copies(0, got) + copies(1, own):
            copy.start()

    total[...] = jnp.zeros_like(total)

    def window(half, lag, row, long=frames, tall=rows, first=0, count=3):
        block = spread[half, lag : lag + long, row : row + tall, :, C * first : C * (first + count)]
        return block.reshape(long * tall * cols, C * count)

    def taps(half, tap, lanes, count=3):
        return weights[half, tap : tap + count, :, lanes].reshape(count * C, -1)

    def times(cells, block):
        return jnp.dot(cells, block, preferred_element_type=jnp.float32)

    def add(lag, part, lanes):
        for f in range(frames):
            total[f, :, lanes] += part[f].reshape(rows * cols, -1) * lag_weights[lag, f]

    low, high = slice(0, 256), slice(256, C)

    def two_rows(half, lags, places, first_taps):
        for lag, row, tap in zip(lags, places, first_taps):
            part = times(window(half, lag, row), taps(half, tap, low))
            add(lag, part.reshape(frames, rows, cols, 256), low)
        more_frames, more_rows = lags[1] - lags[0], places[1] - places[0]
        cells = window(half, lags[0], places[0], frames + more_frames, rows + more_rows)
        block = jnp.concatenate([taps(half, tap, high) for tap in first_taps], 1)
        part = times(cells, block).reshape(frames + more_frames, rows + more_rows, cols, 256)
        add(lags[0], part[:frames, :rows, :, :128], high)
        add(lags[1], part[more_frames:, more_rows:, :, 128:], high)

    for copy in copies(0, own):
        copy.wait()
    two_rows(0, (0, 1), (0, 0), (0, 9))
    two_rows(0, (0, 0), (1, 2), (3, 6))
    everything = slice(0, C)
    part = times(window(0, 1, 1, count=2), taps(0, 12, everything, 2))
    add(1, part.reshape(frames, rows, cols, C), everything)
    for copy in copies(1, own):
        copy.wait()
    part = times(window(1, 1, 1, first=2, count=1), taps(1, 1, everything, 1))
    add(1, part.reshape(frames, rows, cols, C), everything)
    two_rows(1, (1, 2), (2, 2), (2, 11))
    two_rows(1, (2, 2), (0, 1), (5, 8))

    finish(scalars, total, tail, out)


def finish_norm(scalars, total, tail, out):
    for f in range(6):
        data = total[f]
        scale = lax.rsqrt(jnp.mean(data * data, axis=-1, keepdims=True) + 1e-06)
        lifted = data * scale * tail[...]
        out[f] = (lifted * (1.0 / (1.0 + jnp.exp(-lifted)))).astype(jnp.bfloat16)


def finish_add(scalars, total, tail, out):
    for f in range(6):
        summed = tail[f].astype(jnp.float32) + total[f]
        out[f] = jnp.where(f < scalars[1], summed, 0.0).astype(jnp.bfloat16)


def conv(scalars, lag_weights, spread, tail, own, got, finish):
    smem = pl.BlockSpec(memory_space=pltpu.SMEM)
    vmem = pl.BlockSpec(memory_space=pltpu.VMEM)
    return pl.pallas_call(
        lambda *refs: conv_body(*refs, finish=finish),
        out_shape=jax.ShapeDtypeStruct((6, 128, C), jnp.bfloat16),
        in_specs=[smem, smem] + [vmem] * 2 + [pl.BlockSpec(memory_space=pl.ANY)] * 8,
        out_specs=vmem,
        scratch_shapes=[
            pltpu.VMEM((2, HALF, C, C), jnp.bfloat16),
            pltpu.VMEM((6, 128, C), jnp.float32),
            pltpu.SemaphoreType.DMA((2, 4)),
        ],
        compiler_params=pltpu.CompilerParams(vmem_limit_bytes=26 * 1024 * 1024),
        cost_estimate=pl.CostEstimate(flops=1000, bytes_accessed=1000, transcendentals=0),
    )(scalars, lag_weights, spread, tail, *own, *got)


def clip_positions(clip_lengths, frame_index):
    ends = jnp.cumsum(clip_lengths)
    begins = jnp.max(jnp.where(ends[None, :] <= frame_index[:, None], ends[None, :], 0), axis=1)
    return frame_index - begins


def norm_act(values, gain):
    data = values.astype(jnp.float32)
    mean_square = jnp.mean(data * data, axis=-1, keepdims=True)
    scaled = data * lax.rsqrt(mean_square + 1e-06)
    return jax.nn.silu(scaled * gain).astype(jnp.bfloat16)


def before_in_group(z, y, x, c):
    group = z * NY + y - 1
    return None if group < 0 else (group // NY, group % NY, x, c)


def across_chips(z, y, x, c):
    x = x - 1 if c == 0 else x + 1
    return (z, y, x, 1 - c) if 0 <= x < NX else None


def across_and_before(z, y, x, c):
    place = across_chips(z, y, x, c)
    return None if place is None else before_in_group(*place)


def per_device(
    frames, clip_lengths, group_start, group_count, kernel_one, kernel_two, gain_one, gain_two
):
    slots = frames.shape[0]
    slot = jnp.arange(slots, dtype=jnp.int32)
    position = clip_positions(clip_lengths, group_start[0] + slot)
    lag_weights = jnp.stack([position >= 2, position >= 1, position >= 0]).astype(jnp.float32)
    scalars = jnp.stack([lax.axis_index("c").astype(jnp.int32), group_count[0]])
    orders = channel_orders()

    first_core = lax.axis_index("c") == 0
    last = group_count[0] - 2

    def sides(acts):
        return (
            jnp.where(first_core, acts[:, 3:4], acts[:, 0:1]),
            jnp.where(first_core, acts[:, 0:1], acts[:, 3:4]),
        )

    def last_two(acts):
        return lax.dynamic_slice_in_dim(acts, last, 2, 0)

    acts_one = norm_act(frames, gain_one)
    own = jnp.stack([own_half(kernel_one), own_half(kernel_two)])
    pieces = z_stage(own)
    inner, outer = sides(acts_one)
    ends, across = fetch(last_two(acts_one), before_in_group), fetch(outer, across_chips)
    picks = make_picks(orders)
    pieces, across, lag_weights, scalars = lax.optimization_barrier(
        (pieces, across, lag_weights, scalars)
    )

    opposite = fetch(pieces, small_source(2))
    after = fetch(pieces, small_source(1))
    gated, ends = lax.optimization_barrier((pieces, ends))
    parts = [pieces, after, fetch(gated, small_source(-1)), opposite]
    inner, outer = jnp.concatenate([sides(ends)[0], inner], 0), sides(ends)[1]
    corners = fetch(outer, across_chips)
    parts, corners = lax.optimization_barrier((parts, corners))
    across = jnp.concatenate([corners, across], 0)

    one_bundle, two_bundle = join_rows(parts, 0), join_rows(parts, 1)
    one_bundles = bulk_stage(one_bundle)
    one_own, two_own = lax.optimization_barrier((one_bundle, two_bundle))
    one_others, two_others = [fetch(one_own, sibling)], [fetch(two_own, sibling)]
    two_bundle, one_others, two_others, inner = lax.optimization_barrier(
        (two_bundle, one_others, two_others, inner)
    )
    beside = fetch(inner, sibling)
    spread = spread_halo(scalars, picks, ends, beside, across, spread_inner(picks, acts_one))
    one_bundles, one_others, two_others, spread = lax.optimization_barrier(
        (one_bundles, one_others, two_others, spread)
    )
    one_others += [fetch(b, sibling) for b in one_bundles[1:]]

    two_bundles = bulk_stage(two_bundle)
    acts_two = conv(
        scalars, lag_weights, spread, gain_two.reshape(1, C), one_bundles, one_others, finish_norm
    ).reshape(frames.shape)

    two_bundles, acts_two = lax.optimization_barrier((two_bundles, acts_two))
    inner, outer = sides(acts_two)
    ends, corners, outer = lax.optimization_barrier((last_two(acts_two), last_two(outer), outer))
    ends = fetch(ends, before_in_group)
    across = fetch(outer, across_chips)
    corners = fetch(corners, across_and_before)
    two_others += [fetch(b, sibling) for b in two_bundles[1:3]]
    spread = spread_inner(picks, acts_two)
    ends, corners, across, spread, two_others = lax.optimization_barrier(
        (ends, corners, across, spread, two_others)
    )
    beside = fetch(jnp.concatenate([sides(ends)[0], inner], 0), sibling)
    two_last, beside = lax.optimization_barrier((two_bundles[3], beside))
    two_others.append(fetch(two_last, sibling))
    across = jnp.concatenate([corners, across], 0)
    spread = spread_halo(scalars, picks, ends, beside, across, spread)
    result = conv(
        scalars, lag_weights, spread, frames.reshape(slots, 128, C), two_bundles, two_others,
        finish_add,
    )
    return result.reshape(frames.shape)


def solution(mesh):
    torus = Mesh(mesh.devices.reshape(NZ, NY, NX, NC), AXES)
    group, row = ("z", "y"), ("x", "c")
    return jax.shard_map(
        per_device,
        mesh=torus,
        in_specs=(
            P(group, row, None, None),
            P(),
            P(group),
            P(group),
            P(None, None, None, group, None),
            P(None, None, None, group, None),
            P(),
            P(),
        ),
        out_specs=P(group, row, None, None),
        check_vma=False,
    )
```

```python
import jax
import jax.numpy as jnp
import numpy as np
from jax import lax
from jax.experimental import pallas as pl
from jax.experimental.pallas import tpu as pltpu
from jax.sharding import Mesh
from jax.sharding import PartitionSpec as P

NZ, NY, NX, NC = 8, 4, 4, 2
AXES = ("z", "y", "x", "c")
C = 384
SHARD = 12
HALF = 14
BUNDLE = 96
ROUND = (0, 1, -1, 2)

FETCH = np.array([[0, 4], [2, -2], [1, -3], [3, -1]])


def number(z, y, x, c):
    return ((z % NZ * NY + y % NY) * NX + x % NX) * NC + c


def fetch(array, source_of):
    pairs = []
    for z in range(NZ):
        for y in range(NY):
            for x in range(NX):
                for c in range(NC):
                    source = source_of(z, y, x, c)
                    if source is not None:
                        pairs.append((number(*source), number(z, y, x, c)))
    return lax.ppermute(array, AXES, pairs)


def z_source(which):
    def source(z, y, x, c):
        odd = z % 2
        from_z = z - odd + int(FETCH[(x + 2 * odd) % NX, which])
        return (from_z, y + 2 * odd - 1, x, c) if c == 0 else (from_z, y, x, c)

    return source


def small_source(step):
    return lambda z, y, x, c: (z, y, x + step, c) if c == 0 else (z, y + step, x, c)


def bulk_source(step):
    if step == 2:
        return lambda z, y, x, c: (z + 1 if z % 2 != c else z - 1, y, x, c)
    return lambda z, y, x, c: (z, y + step, x, c) if c == 0 else (z, y, x + step, c)


def sibling(z, y, x, c):
    return (z, y, x, 1 - c)


def own_half(kernel):
    start = lax.axis_index("c") * (27 - HALF)
    taps = lax.dynamic_slice_in_dim(kernel.reshape(27, SHARD, C), start, HALF, 0)
    return taps.reshape(HALF * SHARD, C)


def z_stage(own):
    return jnp.stack([fetch(own, z_source(0)), fetch(own, z_source(1))], 1)


def join_body(*refs):
    parts, out = refs[:-1], refs[-1]
    for tap in range(HALF):
        rows = [
            part[piece, pl.ds(SHARD * tap, SHARD), :].astype(jnp.float32)
            for part in parts
            for piece in range(2)
        ]
        out[tap] = jnp.concatenate(rows, 0).astype(jnp.bfloat16)


def join_rows(parts, which):
    block = pl.BlockSpec((None, 2, HALF * SHARD, C), lambda i: (which, 0, 0, 0))
    return pl.pallas_call(
        join_body,
        grid=(1,),
        out_shape=jax.ShapeDtypeStruct((HALF, BUNDLE, C), jnp.bfloat16),
        in_specs=[block] * 4,
        out_specs=pl.BlockSpec((HALF, BUNDLE, C), lambda i: (0, 0, 0)),
        compiler_params=pltpu.CompilerParams(vmem_limit_bytes=16 * 1024 * 1024),
        cost_estimate=pl.CostEstimate(flops=0, bytes_accessed=2_000_000, transcendentals=0),
    )(*parts)


def bulk_stage(bundle):
    return [bundle] + [fetch(bundle, bulk_source(step)) for step in ROUND[1:]]


def channel_orders():
    z, y, x = (lax.axis_index(a) for a in ("z", "y", "x"))
    table = jnp.asarray(FETCH, jnp.int32)
    around = jnp.array(ROUND, jnp.int32)
    aside = jnp.array((0, 1, -1, 0), jnp.int32)
    odd = z % 2
    at_z = z + jnp.array((0, 0, 0, 1), jnp.int32) * jnp.where(odd == 1, 1, -1)
    at_x = x + around[None, :] + 2 * (at_z % 2)[:, None]
    piece_z = (at_z - at_z % 2)[:, None, None] + table[at_x % NX]
    piece_y = (y + aside + 2 * (at_z % 2) - 1)[:, None, None]
    first = piece_z % NZ * NY + piece_y % NY
    at_z = z + jnp.array((0, 0, 0, 1), jnp.int32) * jnp.where(odd == 0, 1, -1)
    piece_z = (at_z - at_z % 2)[:, None] + table[(x + aside + 2 * (at_z % 2)) % NX]
    piece_y = y + around
    second = piece_z[:, None, :] % NZ * NY + piece_y[None, :, None] % NY
    ramp = jnp.arange(SHARD, dtype=jnp.int32)
    return jnp.stack([(half.reshape(-1, 1) * SHARD + ramp).reshape(C) for half in (first, second)])


def picks_body(order, out):
    for half in range(2):
        out[half] = (
            lax.broadcasted_iota(jnp.int32, (C, C), 0) == order[half : half + 1, :]
        ).astype(jnp.bfloat16)


def make_picks(orders):
    vmem = pl.BlockSpec(memory_space=pltpu.VMEM)
    return pl.pallas_call(
        picks_body,
        out_shape=jax.ShapeDtypeStruct((2, C, C), jnp.bfloat16),
        in_specs=[vmem],
        out_specs=vmem,
        cost_estimate=pl.CostEstimate(flops=1000, bytes_accessed=1000, transcendentals=0),
    )(orders)


def spread_cells(cells, pick):
    rows = cells.shape[0]
    plain = jnp.dot(cells, pick, preferred_element_type=jnp.float32)
    col = lax.broadcasted_iota(jnp.int32, (rows, C), 0) % 32
    before = jnp.where(col == 0, 0.0, pltpu.roll(plain, 1, 0))
    after = jnp.where(col == 31, 0.0, pltpu.roll(plain, rows - 1, 0))
    return [part.astype(jnp.bfloat16) for part in (before, plain, after)]


def spread_inner_body(picks, acts, out):
    for half in range(2):
        for tap, part in enumerate(spread_cells(acts[...], picks[half])):
            out[half, 2:8, 1:5, :, C * tap : C * (tap + 1)] = part.reshape(6, 4, 32, C)


def spread_inner(picks, acts):
    vmem = pl.BlockSpec(memory_space=pltpu.VMEM)
    return pl.pallas_call(
        spread_inner_body,
        out_shape=jax.ShapeDtypeStruct((2, 8, 6, 32, 3 * C), jnp.bfloat16),
        in_specs=[vmem] * 2,
        out_specs=vmem,
        compiler_params=pltpu.CompilerParams(vmem_limit_bytes=16 * 1024 * 1024),
        cost_estimate=pl.CostEstimate(flops=1000, bytes_accessed=1000, transcendentals=0),
    )(picks, acts.reshape(-1, C))


def spread_halo_body(scalars, picks, ends, beside, across, _, out):
    core = scalars[0]
    cells = jnp.concatenate(
        [part[...].reshape(-1, C) for part in (ends, beside, across)], 0
    )
    for half in range(2):
        for tap, part in enumerate(spread_cells(cells, picks[half])):
            lanes = slice(C * tap, C * (tap + 1))
            out[half, 0:2, 1:5, :, lanes] = part[0:256].reshape(2, 4, 32, C)
            near, far = part[256:512].reshape(8, 1, 32, C), part[512:768].reshape(8, 1, 32, C)

            @pl.when(core == 0)
            def _():
                out[half, :, 0:1, :, lanes] = far
                out[half, :, 5:6, :, lanes] = near

            @pl.when(core == 1)
            def _():
                out[half, :, 0:1, :, lanes] = near
                out[half, :, 5:6, :, lanes] = far


def spread_halo(scalars, picks, ends, beside, across, spread):
    vmem = pl.BlockSpec(memory_space=pltpu.VMEM)
    return pl.pallas_call(
        spread_halo_body,
        out_shape=jax.ShapeDtypeStruct(spread.shape, spread.dtype),
        in_specs=[pl.BlockSpec(memory_space=pltpu.SMEM)] + [vmem] * 5,
        out_specs=vmem,
        input_output_aliases={5: 0},
        compiler_params=pltpu.CompilerParams(vmem_limit_bytes=16 * 1024 * 1024),
        cost_estimate=pl.CostEstimate(flops=1000, bytes_accessed=1000, transcendentals=0),
    )(scalars, picks, ends, beside, across, spread)


def conv_body(
    scalars, lag_weights, spread, tail, own0, own1, own2, own3, got0, got1, got2, got3,
    out, weights, total, sems, *, finish,
):
    frames, rows, cols = 6, 4, 32
    own, got = (own0, own1, own2, own3), (got0, got1, got2, got3)

    def copies(half, sources):
        return [
            pltpu.make_async_copy(
                sources[k], weights.at[half, :, pl.ds(BUNDLE * k, BUNDLE), :], sems.at[half, k]
            )
            for k in range(4)
        ]

    core = scalars[0]

    @pl.when(core == 0)
    def _():
        for copy in copies(0, own) + copies(1, got):
            copy.start()

    @pl.when(core == 1)
    def _():
        for copy in copies(0, got) + copies(1, own):
            copy.start()

    total[...] = jnp.zeros_like(total)

    def window(half, lag, row, long=frames, tall=rows, first=0, count=3):
        block = spread[half, lag : lag + long, row : row + tall, :, C * first : C * (first + count)]
        return block.reshape(long * tall * cols, C * count)

    def taps(half, tap, lanes, count=3):
        return weights[half, tap : tap + count, :, lanes].reshape(count * C, -1)

    def times(cells, block):
        return jnp.dot(cells, block, preferred_element_type=jnp.float32)

    def add(lag, part, lanes):
        for f in range(frames):
            total[f, :, lanes] += part[f].reshape(rows * cols, -1) * lag_weights[lag, f]

    low, high = slice(0, 256), slice(256, C)

    def two_rows(half, lags, places, first_taps):
        for lag, row, tap in zip(lags, places, first_taps):
            part = times(window(half, lag, row), taps(half, tap, low))
            add(lag, part.reshape(frames, rows, cols, 256), low)
        more_frames, more_rows = lags[1] - lags[0], places[1] - places[0]
        cells = window(half, lags[0], places[0], frames + more_frames, rows + more_rows)
        block = jnp.concatenate([taps(half, tap, high) for tap in first_taps], 1)
        part = times(cells, block).reshape(frames + more_frames, rows + more_rows, cols, 256)
        add(lags[0], part[:frames, :rows, :, :128], high)
        add(lags[1], part[more_frames:, more_rows:, :, 128:], high)

    for copy in copies(0, own):
        copy.wait()
    two_rows(0, (0, 1), (0, 0), (0, 9))
    two_rows(0, (0, 0), (1, 2), (3, 6))
    everything = slice(0, C)
    part = times(window(0, 1, 1, count=2), taps(0, 12, everything, 2))
    add(1, part.reshape(frames, rows, cols, C), everything)
    for copy in copies(1, own):
        copy.wait()
    part = times(window(1, 1, 1, first=2, count=1), taps(1, 1, everything, 1))
    add(1, part.reshape(frames, rows, cols, C), everything)
    two_rows(1, (1, 2), (2, 2), (2, 11))
    two_rows(1, (2, 2), (0, 1), (5, 8))

    finish(scalars, total, tail, out)


def finish_norm(scalars, total, tail, out):
    for f in range(6):
        data = total[f]
        scale = lax.rsqrt(jnp.mean(data * data, axis=-1, keepdims=True) + 1e-06)
        lifted = data * scale * tail[...]
        out[f] = (lifted * (1.0 / (1.0 + jnp.exp(-lifted)))).astype(jnp.bfloat16)


def finish_add(scalars, total, tail, out):
    for f in range(6):
        summed = tail[f].astype(jnp.float32) + total[f]
        out[f] = jnp.where(f < scalars[1], summed, 0.0).astype(jnp.bfloat16)


def conv(scalars, lag_weights, spread, tail, own, got, finish):
    smem = pl.BlockSpec(memory_space=pltpu.SMEM)
    vmem = pl.BlockSpec(memory_space=pltpu.VMEM)
    return pl.pallas_call(
        lambda *refs: conv_body(*refs, finish=finish),
        out_shape=jax.ShapeDtypeStruct((6, 128, C), jnp.bfloat16),
        in_specs=[smem, smem] + [vmem] * 2 + [pl.BlockSpec(memory_space=pl.ANY)] * 8,
        out_specs=vmem,
        scratch_shapes=[
            pltpu.VMEM((2, HALF, C, C), jnp.bfloat16),
            pltpu.VMEM((6, 128, C), jnp.float32),
            pltpu.SemaphoreType.DMA((2, 4)),
        ],
        compiler_params=pltpu.CompilerParams(vmem_limit_bytes=22 * 1024 * 1024),
        cost_estimate=pl.CostEstimate(flops=1000, bytes_accessed=1000, transcendentals=0),
    )(scalars, lag_weights, spread, tail, *own, *got)


def clip_positions(clip_lengths, frame_index):
    ends = jnp.cumsum(clip_lengths)
    begins = jnp.max(jnp.where(ends[None, :] <= frame_index[:, None], ends[None, :], 0), axis=1)
    return frame_index - begins


def norm_act(values, gain):
    data = values.astype(jnp.float32)
    mean_square = jnp.mean(data * data, axis=-1, keepdims=True)
    scaled = data * lax.rsqrt(mean_square + 1e-06)
    return jax.nn.silu(scaled * gain).astype(jnp.bfloat16)


def before_in_group(z, y, x, c):
    group = z * NY + y - 1
    return None if group < 0 else (group // NY, group % NY, x, c)


def across_chips(z, y, x, c):
    x = x - 1 if c == 0 else x + 1
    return (z, y, x, 1 - c) if 0 <= x < NX else None


def across_and_before(z, y, x, c):
    place = across_chips(z, y, x, c)
    return None if place is None else before_in_group(*place)


def per_device(
    frames, clip_lengths, group_start, group_count, kernel_one, kernel_two, gain_one, gain_two
):
    slots = frames.shape[0]
    slot = jnp.arange(slots, dtype=jnp.int32)
    position = clip_positions(clip_lengths, group_start[0] + slot)
    lag_weights = jnp.stack([position >= 2, position >= 1, position >= 0]).astype(jnp.float32)
    scalars = jnp.stack([lax.axis_index("c").astype(jnp.int32), group_count[0]])
    orders = channel_orders()

    first_core = lax.axis_index("c") == 0
    last = group_count[0] - 2

    def sides(acts):
        return (
            jnp.where(first_core, acts[:, 3:4], acts[:, 0:1]),
            jnp.where(first_core, acts[:, 0:1], acts[:, 3:4]),
        )

    def last_two(acts):
        return lax.dynamic_slice_in_dim(acts, last, 2, 0)

    acts_one = norm_act(frames, gain_one)
    own = jnp.stack([own_half(kernel_one), own_half(kernel_two)])
    pieces = z_stage(own)
    inner, outer = sides(acts_one)
    ends, across = fetch(last_two(acts_one), before_in_group), fetch(outer, across_chips)
    picks = make_picks(orders)
    pieces, across, lag_weights, scalars = lax.optimization_barrier(
        (pieces, across, lag_weights, scalars)
    )

    opposite = fetch(pieces, small_source(2))
    after = fetch(pieces, small_source(1))
    gated, ends = lax.optimization_barrier((pieces, ends))
    parts = [pieces, after, fetch(gated, small_source(-1)), opposite]
    inner, outer = jnp.concatenate([sides(ends)[0], inner], 0), sides(ends)[1]
    corners = fetch(outer, across_chips)
    parts, corners = lax.optimization_barrier((parts, corners))
    across = jnp.concatenate([corners, across], 0)

    one_bundle, two_bundle = join_rows(parts, 0), join_rows(parts, 1)
    one_bundles = bulk_stage(one_bundle)
    one_own, two_own = lax.optimization_barrier((one_bundle, two_bundle))
    one_others, two_others = [fetch(one_own, sibling)], [fetch(two_own, sibling)]
    two_bundle, one_others, two_others, inner = lax.optimization_barrier(
        (two_bundle, one_others, two_others, inner)
    )
    beside = fetch(inner, sibling)
    spread = spread_halo(scalars, picks, ends, beside, across, spread_inner(picks, acts_one))
    one_bundles, one_others, two_others, spread = lax.optimization_barrier(
        (one_bundles, one_others, two_others, spread)
    )
    one_others += [fetch(b, sibling) for b in one_bundles[1:]]

    two_bundles = bulk_stage(two_bundle)
    acts_two = conv(
        scalars, lag_weights, spread, gain_two.reshape(1, C), one_bundles, one_others, finish_norm
    ).reshape(frames.shape)

    two_bundles, acts_two = lax.optimization_barrier((two_bundles, acts_two))
    inner, outer = sides(acts_two)
    ends, corners, outer = lax.optimization_barrier((last_two(acts_two), last_two(outer), outer))
    ends = fetch(ends, before_in_group)
    across = fetch(outer, across_chips)
    corners = fetch(corners, across_and_before)
    two_others += [fetch(b, sibling) for b in two_bundles[1:3]]
    spread = spread_inner(picks, acts_two)
    ends, corners, across, spread, two_others = lax.optimization_barrier(
        (ends, corners, across, spread, two_others)
    )
    beside = fetch(jnp.concatenate([sides(ends)[0], inner], 0), sibling)
    two_last, beside = lax.optimization_barrier((two_bundles[3], beside))
    two_others.append(fetch(two_last, sibling))
    across = jnp.concatenate([corners, across], 0)
    spread = spread_halo(scalars, picks, ends, beside, across, spread)
    result = conv(
        scalars, lag_weights, spread, frames.reshape(slots, 128, C), two_bundles, two_others,
        finish_add,
    )
    return result.reshape(frames.shape)


def solution(mesh):
    torus = Mesh(mesh.devices.reshape(NZ, NY, NX, NC), AXES)
    group, row = ("z", "y"), ("x", "c")
    return jax.shard_map(
        per_device,
        mesh=torus,
        in_specs=(
            P(group, row, None, None),
            P(),
            P(group),
            P(group),
            P(None, None, None, group, None),
            P(None, None, None, group, None),
            P(),
            P(),
        ),
        out_specs=P(group, row, None, None),
        check_vma=False,
    )
```

```python
import jax
import jax.numpy as jnp
import numpy as np
from jax import lax
from jax.experimental import pallas as pl
from jax.experimental.pallas import tpu as pltpu
from jax.sharding import Mesh
from jax.sharding import PartitionSpec as P

NZ, NY, NX, NC = 8, 4, 4, 2
AXES = ("z", "y", "x", "c")
C = 384
SHARD = 12
HALF = 14
BUNDLE = 96
ROUND = (0, 1, -1, 2)

FETCH = np.array([[0, 4], [2, -2], [1, -3], [3, -1]])


def number(z, y, x, c):
    return ((z % NZ * NY + y % NY) * NX + x % NX) * NC + c


def fetch(array, source_of):
    pairs = []
    for z in range(NZ):
        for y in range(NY):
            for x in range(NX):
                for c in range(NC):
                    source = source_of(z, y, x, c)
                    if source is not None:
                        pairs.append((number(*source), number(z, y, x, c)))
    return lax.ppermute(array, AXES, pairs)


def z_source(which):
    def source(z, y, x, c):
        odd = z % 2
        from_z = z - odd + int(FETCH[(x + 2 * odd) % NX, which])
        return (from_z, y + 2 * odd - 1, x, c) if c == 0 else (from_z, y, x, c)

    return source


def small_source(step):
    return lambda z, y, x, c: (z, y, x + step, c) if c == 0 else (z, y + step, x, c)


def bulk_source(step):
    if step == 2:
        return lambda z, y, x, c: (z + 1 if z % 2 != c else z - 1, y, x, c)
    return lambda z, y, x, c: (z, y + step, x, c) if c == 0 else (z, y, x + step, c)


def sibling(z, y, x, c):
    return (z, y, x, 1 - c)


def own_half(kernel):
    start = lax.axis_index("c") * (27 - HALF)
    taps = lax.dynamic_slice_in_dim(kernel.reshape(27, SHARD, C), start, HALF, 0)
    return taps.reshape(HALF * SHARD, C)


def z_stage(own):
    return jnp.stack([fetch(own, z_source(0)), fetch(own, z_source(1))], 1)


def join_body(*refs):
    parts, out = refs[:-1], refs[-1]
    for tap in range(HALF):
        rows = [
            part[piece, pl.ds(SHARD * tap, SHARD), :].astype(jnp.float32)
            for part in parts
            for piece in range(2)
        ]
        out[tap] = jnp.concatenate(rows, 0).astype(jnp.bfloat16)


def join_rows(parts, which):
    block = pl.BlockSpec((None, 2, HALF * SHARD, C), lambda i: (which, 0, 0, 0))
    return pl.pallas_call(
        join_body,
        grid=(1,),
        out_shape=jax.ShapeDtypeStruct((HALF, BUNDLE, C), jnp.bfloat16),
        in_specs=[block] * 4,
        out_specs=pl.BlockSpec((HALF, BUNDLE, C), lambda i: (0, 0, 0)),
        compiler_params=pltpu.CompilerParams(vmem_limit_bytes=16 * 1024 * 1024),
        cost_estimate=pl.CostEstimate(flops=0, bytes_accessed=2_000_000, transcendentals=0),
    )(*parts)


def bulk_stage(bundle):
    return [bundle] + [fetch(bundle, bulk_source(step)) for step in ROUND[1:]]


def channel_orders():
    z, y, x = (lax.axis_index(a) for a in ("z", "y", "x"))
    table = jnp.asarray(FETCH, jnp.int32)
    around = jnp.array(ROUND, jnp.int32)
    aside = jnp.array((0, 1, -1, 0), jnp.int32)
    odd = z % 2
    at_z = z + jnp.array((0, 0, 0, 1), jnp.int32) * jnp.where(odd == 1, 1, -1)
    at_x = x + around[None, :] + 2 * (at_z % 2)[:, None]
    piece_z = (at_z - at_z % 2)[:, None, None] + table[at_x % NX]
    piece_y = (y + aside + 2 * (at_z % 2) - 1)[:, None, None]
    first = piece_z % NZ * NY + piece_y % NY
    at_z = z + jnp.array((0, 0, 0, 1), jnp.int32) * jnp.where(odd == 0, 1, -1)
    piece_z = (at_z - at_z % 2)[:, None] + table[(x + aside + 2 * (at_z % 2)) % NX]
    piece_y = y + around
    second = piece_z[:, None, :] % NZ * NY + piece_y[None, :, None] % NY
    ramp = jnp.arange(SHARD, dtype=jnp.int32)
    return jnp.stack([(half.reshape(-1, 1) * SHARD + ramp).reshape(C) for half in (first, second)])


def picks_body(order, out):
    for half in range(2):
        out[half] = (
            lax.broadcasted_iota(jnp.int32, (C, C), 0) == order[half : half + 1, :]
        ).astype(jnp.bfloat16)


def make_picks(orders):
    vmem = pl.BlockSpec(memory_space=pltpu.VMEM)
    return pl.pallas_call(
        picks_body,
        out_shape=jax.ShapeDtypeStruct((2, C, C), jnp.bfloat16),
        in_specs=[vmem],
        out_specs=vmem,
        cost_estimate=pl.CostEstimate(flops=1000, bytes_accessed=1000, transcendentals=0),
    )(orders)


def spread_cells(cells, pick):
    rows = cells.shape[0]
    plain = jnp.dot(cells, pick, preferred_element_type=jnp.float32)
    col = lax.broadcasted_iota(jnp.int32, (rows, C), 0) % 32
    before = jnp.where(col == 0, 0.0, pltpu.roll(plain, 1, 0))
    after = jnp.where(col == 31, 0.0, pltpu.roll(plain, rows - 1, 0))
    return [part.astype(jnp.bfloat16) for part in (before, plain, after)]


def spread_inner_body(picks, acts, out):
    for half in range(2):
        for tap, part in enumerate(spread_cells(acts[...], picks[half])):
            out[half, 2:8, 1:5, :, C * tap : C * (tap + 1)] = part.reshape(6, 4, 32, C)


def spread_inner(picks, acts):
    vmem = pl.BlockSpec(memory_space=pltpu.VMEM)
    return pl.pallas_call(
        spread_inner_body,
        out_shape=jax.ShapeDtypeStruct((2, 8, 6, 32, 3 * C), jnp.bfloat16),
        in_specs=[vmem] * 2,
        out_specs=vmem,
        compiler_params=pltpu.CompilerParams(vmem_limit_bytes=20 * 1024 * 1024),
        cost_estimate=pl.CostEstimate(flops=1000, bytes_accessed=1000, transcendentals=0),
    )(picks, acts.reshape(-1, C))


def spread_halo_body(scalars, picks, ends, beside, across, _, out):
    core = scalars[0]
    cells = jnp.concatenate(
        [part[...].reshape(-1, C) for part in (ends, beside, across)], 0
    )
    for half in range(2):
        for tap, part in enumerate(spread_cells(cells, picks[half])):
            lanes = slice(C * tap, C * (tap + 1))
            out[half, 0:2, 1:5, :, lanes] = part[0:256].reshape(2, 4, 32, C)
            near, far = part[256:512].reshape(8, 1, 32, C), part[512:768].reshape(8, 1, 32, C)

            @pl.when(core == 0)
            def _():
                out[half, :, 0:1, :, lanes] = far
                out[half, :, 5:6, :, lanes] = near

            @pl.when(core == 1)
            def _():
                out[half, :, 0:1, :, lanes] = near
                out[half, :, 5:6, :, lanes] = far


def spread_halo(scalars, picks, ends, beside, across, spread):
    vmem = pl.BlockSpec(memory_space=pltpu.VMEM)
    return pl.pallas_call(
        spread_halo_body,
        out_shape=jax.ShapeDtypeStruct(spread.shape, spread.dtype),
        in_specs=[pl.BlockSpec(memory_space=pltpu.SMEM)] + [vmem] * 5,
        out_specs=vmem,
        input_output_aliases={5: 0},
        compiler_params=pltpu.CompilerParams(vmem_limit_bytes=20 * 1024 * 1024),
        cost_estimate=pl.CostEstimate(flops=1000, bytes_accessed=1000, transcendentals=0),
    )(scalars, picks, ends, beside, across, spread)


def conv_body(
    scalars, lag_weights, spread, tail, own0, own1, own2, own3, got0, got1, got2, got3,
    out, weights, total, sems, *, finish,
):
    frames, rows, cols = 6, 4, 32
    own, got = (own0, own1, own2, own3), (got0, got1, got2, got3)

    def copies(half, sources):
        return [
            pltpu.make_async_copy(
                sources[k], weights.at[half, :, pl.ds(BUNDLE * k, BUNDLE), :], sems.at[half, k]
            )
            for k in range(4)
        ]

    core = scalars[0]

    @pl.when(core == 0)
    def _():
        for copy in copies(0, own) + copies(1, got):
            copy.start()

    @pl.when(core == 1)
    def _():
        for copy in copies(0, got) + copies(1, own):
            copy.start()

    total[...] = jnp.zeros_like(total)

    def window(half, lag, row, long=frames, tall=rows, first=0, count=3):
        block = spread[half, lag : lag + long, row : row + tall, :, C * first : C * (first + count)]
        return block.reshape(long * tall * cols, C * count)

    def taps(half, tap, lanes, count=3):
        return weights[half, tap : tap + count, :, lanes].reshape(count * C, -1)

    def times(cells, block):
        return jnp.dot(cells, block, preferred_element_type=jnp.float32)

    def add(lag, part, lanes):
        for f in range(frames):
            total[f, :, lanes] += part[f].reshape(rows * cols, -1) * lag_weights[lag, f]

    low, high = slice(0, 256), slice(256, C)

    def two_rows(half, lags, places, first_taps):
        for lag, row, tap in zip(lags, places, first_taps):
            part = times(window(half, lag, row), taps(half, tap, low))
            add(lag, part.reshape(frames, rows, cols, 256), low)
        more_frames, more_rows = lags[1] - lags[0], places[1] - places[0]
        cells = window(half, lags[0], places[0], frames + more_frames, rows + more_rows)
        block = jnp.concatenate([taps(half, tap, high) for tap in first_taps], 1)
        part = times(cells, block).reshape(frames + more_frames, rows + more_rows, cols, 256)
        add(lags[0], part[:frames, :rows, :, :128], high)
        add(lags[1], part[more_frames:, more_rows:, :, 128:], high)

    for copy in copies(0, own):
        copy.wait()
    two_rows(0, (0, 1), (0, 0), (0, 9))
    two_rows(0, (0, 0), (1, 2), (3, 6))
    everything = slice(0, C)
    part = times(window(0, 1, 1, count=2), taps(0, 12, everything, 2))
    add(1, part.reshape(frames, rows, cols, C), everything)
    for copy in copies(1, own):
        copy.wait()
    part = times(window(1, 1, 1, first=2, count=1), taps(1, 1, everything, 1))
    add(1, part.reshape(frames, rows, cols, C), everything)
    two_rows(1, (1, 2), (2, 2), (2, 11))
    two_rows(1, (2, 2), (0, 1), (5, 8))

    finish(scalars, total, tail, out)


def finish_norm(scalars, total, tail, out):
    for f in range(6):
        data = total[f]
        scale = lax.rsqrt(jnp.mean(data * data, axis=-1, keepdims=True) + 1e-06)
        lifted = data * scale * tail[...]
        out[f] = (lifted * (1.0 / (1.0 + jnp.exp(-lifted)))).astype(jnp.bfloat16)


def finish_add(scalars, total, tail, out):
    for f in range(6):
        summed = tail[f].astype(jnp.float32) + total[f]
        out[f] = jnp.where(f < scalars[1], summed, 0.0).astype(jnp.bfloat16)


def conv(scalars, lag_weights, spread, tail, own, got, finish):
    smem = pl.BlockSpec(memory_space=pltpu.SMEM)
    vmem = pl.BlockSpec(memory_space=pltpu.VMEM)
    return pl.pallas_call(
        lambda *refs: conv_body(*refs, finish=finish),
        out_shape=jax.ShapeDtypeStruct((6, 128, C), jnp.bfloat16),
        in_specs=[smem, smem] + [vmem] * 2 + [pl.BlockSpec(memory_space=pl.ANY)] * 8,
        out_specs=vmem,
        scratch_shapes=[
            pltpu.VMEM((2, HALF, C, C), jnp.bfloat16),
            pltpu.VMEM((6, 128, C), jnp.float32),
            pltpu.SemaphoreType.DMA((2, 4)),
        ],
        compiler_params=pltpu.CompilerParams(vmem_limit_bytes=26 * 1024 * 1024),
        cost_estimate=pl.CostEstimate(flops=1000, bytes_accessed=1000, transcendentals=0),
    )(scalars, lag_weights, spread, tail, *own, *got)


def clip_positions(clip_lengths, frame_index):
    ends = jnp.cumsum(clip_lengths)
    begins = jnp.max(jnp.where(ends[None, :] <= frame_index[:, None], ends[None, :], 0), axis=1)
    return frame_index - begins


def norm_act(values, gain):
    data = values.astype(jnp.float32)
    mean_square = jnp.mean(data * data, axis=-1, keepdims=True)
    scaled = data * lax.rsqrt(mean_square + 1e-06)
    return jax.nn.silu(scaled * gain).astype(jnp.bfloat16)


def before_in_group(z, y, x, c):
    group = z * NY + y - 1
    return None if group < 0 else (group // NY, group % NY, x, c)


def across_chips(z, y, x, c):
    x = x - 1 if c == 0 else x + 1
    return (z, y, x, 1 - c) if 0 <= x < NX else None


def across_and_before(z, y, x, c):
    place = across_chips(z, y, x, c)
    return None if place is None else before_in_group(*place)


def per_device(
    frames, clip_lengths, group_start, group_count, kernel_one, kernel_two, gain_one, gain_two
):
    slots = frames.shape[0]
    slot = jnp.arange(slots, dtype=jnp.int32)
    position = clip_positions(clip_lengths, group_start[0] + slot)
    lag_weights = jnp.stack([position >= 2, position >= 1, position >= 0]).astype(jnp.float32)
    scalars = jnp.stack([lax.axis_index("c").astype(jnp.int32), group_count[0]])
    orders = channel_orders()

    first_core = lax.axis_index("c") == 0
    last = group_count[0] - 2

    def sides(acts):
        return (
            jnp.where(first_core, acts[:, 3:4], acts[:, 0:1]),
            jnp.where(first_core, acts[:, 0:1], acts[:, 3:4]),
        )

    def last_two(acts):
        return lax.dynamic_slice_in_dim(acts, last, 2, 0)

    acts_one = norm_act(frames, gain_one)
    own = jnp.stack([own_half(kernel_one), own_half(kernel_two)])
    pieces = z_stage(own)
    ends = fetch(last_two(acts_one), before_in_group)
    picks = make_picks(orders)
    pieces, picks, lag_weights, scalars = lax.optimization_barrier(
        (pieces, picks, lag_weights, scalars)
    )

    opposite = fetch(pieces, small_source(2))
    after = fetch(pieces, small_source(1))
    gated, ends = lax.optimization_barrier((pieces, ends))
    parts = [pieces, after, fetch(gated, small_source(-1)), opposite]
    inner, outer = sides(jnp.concatenate([ends, acts_one], 0))
    across = fetch(outer, across_chips)
    parts, across = lax.optimization_barrier((parts, across))

    one_bundle, two_bundle = join_rows(parts, 0), join_rows(parts, 1)
    one_bundles = bulk_stage(one_bundle)
    one_own, two_own = lax.optimization_barrier((one_bundle, two_bundle))
    one_others, two_others = [fetch(one_own, sibling)], [fetch(two_own, sibling)]
    two_bundle, one_others, two_others, inner = lax.optimization_barrier(
        (two_bundle, one_others, two_others, inner)
    )
    beside = fetch(inner, sibling)
    spread = spread_halo(scalars, picks, ends, beside, across, spread_inner(picks, acts_one))
    one_bundles, one_others, two_others, spread = lax.optimization_barrier(
        (one_bundles, one_others, two_others, spread)
    )
    one_others += [fetch(b, sibling) for b in one_bundles[1:]]

    two_bundles = bulk_stage(two_bundle)
    acts_two = conv(
        scalars, lag_weights, spread, gain_two.reshape(1, C), one_bundles, one_others, finish_norm
    ).reshape(frames.shape)

    two_bundles, acts_two = lax.optimization_barrier((two_bundles, acts_two))
    inner, outer = sides(acts_two)
    ends, corners, outer = lax.optimization_barrier((last_two(acts_two), last_two(outer), outer))
    ends = fetch(ends, before_in_group)
    across = fetch(outer, across_chips)
    corners = fetch(corners, across_and_before)
    two_others += [fetch(b, sibling) for b in two_bundles[1:3]]
    spread = spread_inner(picks, acts_two)
    ends, corners, across, spread, two_others = lax.optimization_barrier(
        (ends, corners, across, spread, two_others)
    )
    beside = fetch(jnp.concatenate([sides(ends)[0], inner], 0), sibling)
    two_last, beside = lax.optimization_barrier((two_bundles[3], beside))
    two_others.append(fetch(two_last, sibling))
    across = jnp.concatenate([corners, across], 0)
    spread = spread_halo(scalars, picks, ends, beside, across, spread)
    result = conv(
        scalars, lag_weights, spread, frames.reshape(slots, 128, C), two_bundles, two_others,
        finish_add,
    )
    return result.reshape(frames.shape)


def solution(mesh):
    torus = Mesh(mesh.devices.reshape(NZ, NY, NX, NC), AXES)
    group, row = ("z", "y"), ("x", "c")
    return jax.shard_map(
        per_device,
        mesh=torus,
        in_specs=(
            P(group, row, None, None),
            P(),
            P(group),
            P(group),
            P(None, None, None, group, None),
            P(None, None, None, group, None),
            P(),
            P(),
        ),
        out_specs=P(group, row, None, None),
        check_vma=False,
    )
```

```python
import jax
import jax.numpy as jnp
import numpy as np
from jax import lax
from jax.experimental import pallas as pl
from jax.experimental.pallas import tpu as pltpu
from jax.sharding import Mesh
from jax.sharding import PartitionSpec as P

NZ, NY, NX, NC = 8, 4, 4, 2
AXES = ("z", "y", "x", "c")
C = 384
SHARD = 12
HALF = 14
BUNDLE = 96
ROUND = (0, 1, -1, 2)

FETCH = np.array([[0, 4], [2, -2], [1, -3], [3, -1]])


def number(z, y, x, c):
    return ((z % NZ * NY + y % NY) * NX + x % NX) * NC + c


def fetch(array, source_of):
    pairs = []
    for z in range(NZ):
        for y in range(NY):
            for x in range(NX):
                for c in range(NC):
                    source = source_of(z, y, x, c)
                    if source is not None:
                        pairs.append((number(*source), number(z, y, x, c)))
    return lax.ppermute(array, AXES, pairs)


def z_source(which):
    def source(z, y, x, c):
        odd = z % 2
        from_z = z - odd + int(FETCH[(x + 2 * odd) % NX, which])
        return (from_z, y + 2 * odd - 1, x, c) if c == 0 else (from_z, y, x, c)

    return source


def small_source(step):
    return lambda z, y, x, c: (z, y, x + step, c) if c == 0 else (z, y + step, x, c)


def bulk_source(step):
    if step == 2:
        return lambda z, y, x, c: (z + 1 if z % 2 != c else z - 1, y, x, c)
    return lambda z, y, x, c: (z, y + step, x, c) if c == 0 else (z, y, x + step, c)


def sibling(z, y, x, c):
    return (z, y, x, 1 - c)


def own_half(kernel):
    start = lax.axis_index("c") * (27 - HALF)
    taps = lax.dynamic_slice_in_dim(kernel.reshape(27, SHARD, C), start, HALF, 0)
    return taps.reshape(HALF * SHARD, C)


def z_stage(own):
    return jnp.stack([fetch(own, z_source(0)), fetch(own, z_source(1))], 1)


def join_body(*refs):
    parts, out = refs[:-1], refs[-1]
    for tap in range(HALF):
        rows = [
            part[piece, pl.ds(SHARD * tap, SHARD), :].astype(jnp.float32)
            for part in parts
            for piece in range(2)
        ]
        out[tap] = jnp.concatenate(rows, 0).astype(jnp.bfloat16)


def join_rows(parts, which):
    block = pl.BlockSpec((None, 2, HALF * SHARD, C), lambda i: (which, 0, 0, 0))
    return pl.pallas_call(
        join_body,
        grid=(1,),
        out_shape=jax.ShapeDtypeStruct((HALF, BUNDLE, C), jnp.bfloat16),
        in_specs=[block] * 4,
        out_specs=pl.BlockSpec((HALF, BUNDLE, C), lambda i: (0, 0, 0)),
        compiler_params=pltpu.CompilerParams(vmem_limit_bytes=16 * 1024 * 1024),
        cost_estimate=pl.CostEstimate(flops=0, bytes_accessed=2_000_000, transcendentals=0),
    )(*parts)


def bulk_stage(bundle):
    return [bundle] + [fetch(bundle, bulk_source(step)) for step in ROUND[1:]]


def channel_orders():
    z, y, x = (lax.axis_index(a) for a in ("z", "y", "x"))
    table = jnp.asarray(FETCH, jnp.int32)
    around = jnp.array(ROUND, jnp.int32)
    aside = jnp.array((0, 1, -1, 0), jnp.int32)
    odd = z % 2
    at_z = z + jnp.array((0, 0, 0, 1), jnp.int32) * jnp.where(odd == 1, 1, -1)
    at_x = x + around[None, :] + 2 * (at_z % 2)[:, None]
    piece_z = (at_z - at_z % 2)[:, None, None] + table[at_x % NX]
    piece_y = (y + aside + 2 * (at_z % 2) - 1)[:, None, None]
    first = piece_z % NZ * NY + piece_y % NY
    at_z = z + jnp.array((0, 0, 0, 1), jnp.int32) * jnp.where(odd == 0, 1, -1)
    piece_z = (at_z - at_z % 2)[:, None] + table[(x + aside + 2 * (at_z % 2)) % NX]
    piece_y = y + around
    second = piece_z[:, None, :] % NZ * NY + piece_y[None, :, None] % NY
    ramp = jnp.arange(SHARD, dtype=jnp.int32)
    return jnp.stack([(half.reshape(-1, 1) * SHARD + ramp).reshape(C) for half in (first, second)])


def picks_body(order, out):
    for half in range(2):
        out[half] = (
            lax.broadcasted_iota(jnp.int32, (C, C), 0) == order[half : half + 1, :]
        ).astype(jnp.bfloat16)


def make_picks(orders):
    vmem = pl.BlockSpec(memory_space=pltpu.VMEM)
    return pl.pallas_call(
        picks_body,
        out_shape=jax.ShapeDtypeStruct((2, C, C), jnp.bfloat16),
        in_specs=[vmem],
        out_specs=vmem,
        cost_estimate=pl.CostEstimate(flops=1000, bytes_accessed=1000, transcendentals=0),
    )(orders)


def spread_cells(cells, pick):
    rows = cells.shape[0]
    plain = jnp.dot(cells, pick, preferred_element_type=jnp.float32)
    col = lax.broadcasted_iota(jnp.int32, (rows, C), 0) % 32
    before = jnp.where(col == 0, 0.0, pltpu.roll(plain, 1, 0))
    after = jnp.where(col == 31, 0.0, pltpu.roll(plain, rows - 1, 0))
    return [part.astype(jnp.bfloat16) for part in (before, plain, after)]


def spread_inner_body(picks, acts, out):
    for half in range(2):
        for tap, part in enumerate(spread_cells(acts[...], picks[half])):
            out[half, 2:8, 1:5, :, C * tap : C * (tap + 1)] = part.reshape(6, 4, 32, C)


def spread_inner(picks, acts):
    vmem = pl.BlockSpec(memory_space=pltpu.VMEM)
    return pl.pallas_call(
        spread_inner_body,
        out_shape=jax.ShapeDtypeStruct((2, 8, 6, 32, 3 * C), jnp.bfloat16),
        in_specs=[vmem] * 2,
        out_specs=vmem,
        compiler_params=pltpu.CompilerParams(vmem_limit_bytes=20 * 1024 * 1024),
        cost_estimate=pl.CostEstimate(flops=1000, bytes_accessed=1000, transcendentals=0),
    )(picks, acts.reshape(-1, C))


def spread_halo_body(scalars, picks, ends, beside, across, _, out):
    core = scalars[0]
    cells = jnp.concatenate(
        [part[...].reshape(-1, C) for part in (ends, beside, across)], 0
    )
    for half in range(2):
        for tap, part in enumerate(spread_cells(cells, picks[half])):
            lanes = slice(C * tap, C * (tap + 1))
            out[half, 0:2, 1:5, :, lanes] = part[0:256].reshape(2, 4, 32, C)
            near, far = part[256:512].reshape(8, 1, 32, C), part[512:768].reshape(8, 1, 32, C)

            @pl.when(core == 0)
            def _():
                out[half, :, 0:1, :, lanes] = far
                out[half, :, 5:6, :, lanes] = near

            @pl.when(core == 1)
            def _():
                out[half, :, 0:1, :, lanes] = near
                out[half, :, 5:6, :, lanes] = far


def spread_halo(scalars, picks, ends, beside, across, spread):
    vmem = pl.BlockSpec(memory_space=pltpu.VMEM)
    return pl.pallas_call(
        spread_halo_body,
        out_shape=jax.ShapeDtypeStruct(spread.shape, spread.dtype),
        in_specs=[pl.BlockSpec(memory_space=pltpu.SMEM)] + [vmem] * 5,
        out_specs=vmem,
        input_output_aliases={5: 0},
        compiler_params=pltpu.CompilerParams(vmem_limit_bytes=20 * 1024 * 1024),
        cost_estimate=pl.CostEstimate(flops=1000, bytes_accessed=1000, transcendentals=0),
    )(scalars, picks, ends, beside, across, spread)


def conv_body(
    scalars, lag_weights, spread, tail, own0, own1, own2, own3, got0, got1, got2, got3,
    out, weights, total, sems, *, finish,
):
    frames, rows, cols = 6, 4, 32
    own, got = (own0, own1, own2, own3), (got0, got1, got2, got3)

    def copies(half, sources):
        return [
            pltpu.make_async_copy(
                sources[k], weights.at[half, :, pl.ds(BUNDLE * k, BUNDLE), :], sems.at[half, k]
            )
            for k in range(4)
        ]

    core = scalars[0]

    @pl.when(core == 0)
    def _():
        for copy in copies(0, own) + copies(1, got):
            copy.start()

    @pl.when(core == 1)
    def _():
        for copy in copies(0, got) + copies(1, own):
            copy.start()

    total[...] = jnp.zeros_like(total)

    def window(half, lag, row, long=frames, tall=rows, first=0, count=3):
        block = spread[half, lag : lag + long, row : row + tall, :, C * first : C * (first + count)]
        return block.reshape(long * tall * cols, C * count)

    def taps(half, tap, lanes, count=3):
        return weights[half, tap : tap + count, :, lanes].reshape(count * C, -1)

    def times(cells, block):
        return jnp.dot(cells, block, preferred_element_type=jnp.float32)

    def add(lag, part, lanes):
        for f in range(frames):
            total[f, :, lanes] += part[f].reshape(rows * cols, -1) * lag_weights[lag, f]

    low, high = slice(0, 256), slice(256, C)

    def two_rows(half, lags, places, first_taps):
        for lag, row, tap in zip(lags, places, first_taps):
            part = times(window(half, lag, row), taps(half, tap, low))
            add(lag, part.reshape(frames, rows, cols, 256), low)
        more_frames, more_rows = lags[1] - lags[0], places[1] - places[0]
        cells = window(half, lags[0], places[0], frames + more_frames, rows + more_rows)
        block = jnp.concatenate([taps(half, tap, high) for tap in first_taps], 1)
        part = times(cells, block).reshape(frames + more_frames, rows + more_rows, cols, 256)
        add(lags[0], part[:frames, :rows, :, :128], high)
        add(lags[1], part[more_frames:, more_rows:, :, 128:], high)

    for copy in copies(0, own):
        copy.wait()
    two_rows(0, (0, 1), (0, 0), (0, 9))
    two_rows(0, (0, 0), (1, 2), (3, 6))
    everything = slice(0, C)
    part = times(window(0, 1, 1, count=2), taps(0, 12, everything, 2))
    add(1, part.reshape(frames, rows, cols, C), everything)
    for copy in copies(1, own):
        copy.wait()
    part = times(window(1, 1, 1, first=2, count=1), taps(1, 1, everything, 1))
    add(1, part.reshape(frames, rows, cols, C), everything)
    two_rows(1, (1, 2), (2, 2), (2, 11))
    two_rows(1, (2, 2), (0, 1), (5, 8))

    finish(scalars, total, tail, out)


def finish_norm(scalars, total, tail, out):
    for f in range(6):
        data = total[f]
        scale = lax.rsqrt(jnp.mean(data * data, axis=-1, keepdims=True) + 1e-06)
        lifted = data * scale * tail[...]
        out[f] = (lifted * (1.0 / (1.0 + jnp.exp(-lifted)))).astype(jnp.bfloat16)


def finish_add(scalars, total, tail, out):
    for f in range(6):
        summed = tail[f].astype(jnp.float32) + total[f]
        out[f] = jnp.where(f < scalars[1], summed, 0.0).astype(jnp.bfloat16)


def conv(scalars, lag_weights, spread, tail, own, got, finish):
    smem = pl.BlockSpec(memory_space=pltpu.SMEM)
    vmem = pl.BlockSpec(memory_space=pltpu.VMEM)
    return pl.pallas_call(
        lambda *refs: conv_body(*refs, finish=finish),
        out_shape=jax.ShapeDtypeStruct((6, 128, C), jnp.bfloat16),
        in_specs=[smem, smem] + [vmem] * 2 + [pl.BlockSpec(memory_space=pl.ANY)] * 8,
        out_specs=vmem,
        scratch_shapes=[
            pltpu.VMEM((2, HALF, C, C), jnp.bfloat16),
            pltpu.VMEM((6, 128, C), jnp.float32),
            pltpu.SemaphoreType.DMA((2, 4)),
        ],
        compiler_params=pltpu.CompilerParams(vmem_limit_bytes=26 * 1024 * 1024),
        cost_estimate=pl.CostEstimate(flops=1000, bytes_accessed=1000, transcendentals=0),
    )(scalars, lag_weights, spread, tail, *own, *got)


def clip_positions(clip_lengths, frame_index):
    ends = jnp.cumsum(clip_lengths)
    begins = jnp.max(jnp.where(ends[None, :] <= frame_index[:, None], ends[None, :], 0), axis=1)
    return frame_index - begins


def norm_act(values, gain):
    data = values.astype(jnp.float32)
    mean_square = jnp.mean(data * data, axis=-1, keepdims=True)
    scaled = data * lax.rsqrt(mean_square + 1e-06)
    return jax.nn.silu(scaled * gain).astype(jnp.bfloat16)


def before_in_group(z, y, x, c):
    group = z * NY + y - 1
    return None if group < 0 else (group // NY, group % NY, x, c)


def across_chips(z, y, x, c):
    x = x - 1 if c == 0 else x + 1
    return (z, y, x, 1 - c) if 0 <= x < NX else None


def across_and_before(z, y, x, c):
    place = across_chips(z, y, x, c)
    return None if place is None else before_in_group(*place)


def per_device(
    frames, clip_lengths, group_start, group_count, kernel_one, kernel_two, gain_one, gain_two
):
    slots = frames.shape[0]
    slot = jnp.arange(slots, dtype=jnp.int32)
    position = clip_positions(clip_lengths, group_start[0] + slot)
    lag_weights = jnp.stack([position >= 2, position >= 1, position >= 0]).astype(jnp.float32)
    scalars = jnp.stack([lax.axis_index("c").astype(jnp.int32), group_count[0]])
    orders = channel_orders()

    first_core = lax.axis_index("c") == 0
    last = group_count[0] - 2

    def sides(acts):
        return (
            jnp.where(first_core, acts[:, 3:4], acts[:, 0:1]),
            jnp.where(first_core, acts[:, 0:1], acts[:, 3:4]),
        )

    def last_two(acts):
        return lax.dynamic_slice_in_dim(acts, last, 2, 0)

    acts_one = norm_act(frames, gain_one)
    own = jnp.stack([own_half(kernel_one), own_half(kernel_two)])
    pieces = z_stage(own)
    ends = fetch(last_two(acts_one), before_in_group)
    picks = make_picks(orders)
    pieces, picks, lag_weights, scalars = lax.optimization_barrier(
        (pieces, picks, lag_weights, scalars)
    )

    opposite = fetch(pieces, small_source(2))
    after = fetch(pieces, small_source(1))
    gated, ends = lax.optimization_barrier((pieces, ends))
    parts = [pieces, after, fetch(gated, small_source(-1)), opposite]
    inner, outer = sides(jnp.concatenate([ends, acts_one], 0))
    across = fetch(outer, across_chips)
    parts, across = lax.optimization_barrier((parts, across))

    one_bundle, two_bundle = join_rows(parts, 0), join_rows(parts, 1)
    one_bundles = bulk_stage(one_bundle)
    one_own, two_own = lax.optimization_barrier((one_bundle, two_bundle))
    one_others, two_others = [fetch(one_own, sibling)], [fetch(two_own, sibling)]
    two_bundle, one_others, two_others, inner = lax.optimization_barrier(
        (two_bundle, one_others, two_others, inner)
    )
    beside = fetch(inner, sibling)
    spread = spread_halo(scalars, picks, ends, beside, across, spread_inner(picks, acts_one))
    one_bundles, one_others, two_others, spread = lax.optimization_barrier(
        (one_bundles, one_others, two_others, spread)
    )
    one_others += [fetch(b, sibling) for b in one_bundles[1:]]

    two_bundles = bulk_stage(two_bundle)
    acts_two = conv(
        scalars, lag_weights, spread, gain_two.reshape(1, C), one_bundles, one_others, finish_norm
    ).reshape(frames.shape)

    inner, outer = sides(acts_two)
    ends, corners, outer = lax.optimization_barrier((last_two(acts_two), last_two(outer), outer))
    ends = fetch(ends, before_in_group)
    across = fetch(outer, across_chips)
    corners = fetch(corners, across_and_before)
    spread = spread_inner(picks, acts_two)
    ends, corners, across, spread, two_bundles = lax.optimization_barrier(
        (ends, corners, across, spread, two_bundles)
    )
    beside = fetch(jnp.concatenate([sides(ends)[0], inner], 0), sibling)
    two_others.append(fetch(two_bundles[1], sibling))
    two_last, beside = lax.optimization_barrier((two_bundles[2:], beside))
    two_others += [fetch(b, sibling) for b in two_last]
    across = jnp.concatenate([corners, across], 0)
    spread = spread_halo(scalars, picks, ends, beside, across, spread)
    result = conv(
        scalars, lag_weights, spread, frames.reshape(slots, 128, C), two_bundles, two_others,
        finish_add,
    )
    return result.reshape(frames.shape)


def solution(mesh):
    torus = Mesh(mesh.devices.reshape(NZ, NY, NX, NC), AXES)
    group, row = ("z", "y"), ("x", "c")
    return jax.shard_map(
        per_device,
        mesh=torus,
        in_specs=(
            P(group, row, None, None),
            P(),
            P(group),
            P(group),
            P(None, None, None, group, None),
            P(None, None, None, group, None),
            P(),
            P(),
        ),
        out_specs=P(group, row, None, None),
        check_vma=False,
    )
```

```python
import jax
import jax.numpy as jnp
import numpy as np
from jax import lax
from jax.experimental import pallas as pl
from jax.experimental.pallas import tpu as pltpu
from jax.sharding import Mesh
from jax.sharding import PartitionSpec as P

NZ, NY, NX, NC = 8, 4, 4, 2
AXES = ("z", "y", "x", "c")
C = 384
SHARD = 12
HALF = 14
BUNDLE = 96
ROUND = (0, 1, -1, 2)

FETCH = np.array([[0, 4], [2, -2], [1, -3], [3, -1]])


def number(z, y, x, c):
    return ((z % NZ * NY + y % NY) * NX + x % NX) * NC + c


def fetch(array, source_of):
    pairs = []
    for z in range(NZ):
        for y in range(NY):
            for x in range(NX):
                for c in range(NC):
                    source = source_of(z, y, x, c)
                    if source is not None:
                        pairs.append((number(*source), number(z, y, x, c)))
    return lax.ppermute(array, AXES, pairs)


def z_source(which):
    def source(z, y, x, c):
        odd = z % 2
        from_z = z - odd + int(FETCH[(x + 2 * odd) % NX, which])
        return (from_z, y + 2 * odd - 1, x, c) if c == 0 else (from_z, y, x, c)

    return source


def small_source(step):
    return lambda z, y, x, c: (z, y, x + step, c) if c == 0 else (z, y + step, x, c)


def bulk_source(step):
    if step == 2:
        return lambda z, y, x, c: (z + 1 if z % 2 != c else z - 1, y, x, c)
    return lambda z, y, x, c: (z, y + step, x, c) if c == 0 else (z, y, x + step, c)


def sibling(z, y, x, c):
    return (z, y, x, 1 - c)


def own_half(kernel):
    start = lax.axis_index("c") * (27 - HALF)
    taps = lax.dynamic_slice_in_dim(kernel.reshape(27, SHARD, C), start, HALF, 0)
    return taps.reshape(HALF * SHARD, C)


def z_stage(own):
    return jnp.stack([fetch(own, z_source(0)), fetch(own, z_source(1))], 1)


def join_body(*refs):
    parts, out = refs[:-1], refs[-1]
    for tap in range(HALF):
        rows = [
            part[piece, pl.ds(SHARD * tap, SHARD), :].astype(jnp.float32)
            for part in parts
            for piece in range(2)
        ]
        out[tap] = jnp.concatenate(rows, 0).astype(jnp.bfloat16)


def join_rows(parts, which):
    block = pl.BlockSpec((None, 2, HALF * SHARD, C), lambda i: (which, 0, 0, 0))
    return pl.pallas_call(
        join_body,
        grid=(1,),
        out_shape=jax.ShapeDtypeStruct((HALF, BUNDLE, C), jnp.bfloat16),
        in_specs=[block] * 4,
        out_specs=pl.BlockSpec((HALF, BUNDLE, C), lambda i: (0, 0, 0)),
        compiler_params=pltpu.CompilerParams(vmem_limit_bytes=16 * 1024 * 1024),
        cost_estimate=pl.CostEstimate(flops=0, bytes_accessed=2_000_000, transcendentals=0),
    )(*parts)


def bulk_stage(bundle):
    return [bundle] + [fetch(bundle, bulk_source(step)) for step in ROUND[1:]]


def channel_orders():
    z, y, x = (lax.axis_index(a) for a in ("z", "y", "x"))
    table = jnp.asarray(FETCH, jnp.int32)
    around = jnp.array(ROUND, jnp.int32)
    aside = jnp.array((0, 1, -1, 0), jnp.int32)
    odd = z % 2
    at_z = z + jnp.array((0, 0, 0, 1), jnp.int32) * jnp.where(odd == 1, 1, -1)
    at_x = x + around[None, :] + 2 * (at_z % 2)[:, None]
    piece_z = (at_z - at_z % 2)[:, None, None] + table[at_x % NX]
    piece_y = (y + aside + 2 * (at_z % 2) - 1)[:, None, None]
    first = piece_z % NZ * NY + piece_y % NY
    at_z = z + jnp.array((0, 0, 0, 1), jnp.int32) * jnp.where(odd == 0, 1, -1)
    piece_z = (at_z - at_z % 2)[:, None] + table[(x + aside + 2 * (at_z % 2)) % NX]
    piece_y = y + around
    second = piece_z[:, None, :] % NZ * NY + piece_y[None, :, None] % NY
    ramp = jnp.arange(SHARD, dtype=jnp.int32)
    return jnp.stack([(half.reshape(-1, 1) * SHARD + ramp).reshape(C) for half in (first, second)])


def picks_body(order, out):
    for half in range(2):
        out[half] = (
            lax.broadcasted_iota(jnp.int32, (C, C), 0) == order[half : half + 1, :]
        ).astype(jnp.bfloat16)


def make_picks(orders):
    vmem = pl.BlockSpec(memory_space=pltpu.VMEM)
    return pl.pallas_call(
        picks_body,
        out_shape=jax.ShapeDtypeStruct((2, C, C), jnp.bfloat16),
        in_specs=[vmem],
        out_specs=vmem,
        cost_estimate=pl.CostEstimate(flops=1000, bytes_accessed=1000, transcendentals=0),
    )(orders)


def spread_cells(cells, pick):
    rows = cells.shape[0]
    plain = jnp.dot(cells, pick, preferred_element_type=jnp.float32)
    col = lax.broadcasted_iota(jnp.int32, (rows, C), 0) % 32
    before = jnp.where(col == 0, 0.0, pltpu.roll(plain, 1, 0))
    after = jnp.where(col == 31, 0.0, pltpu.roll(plain, rows - 1, 0))
    return [part.astype(jnp.bfloat16) for part in (before, plain, after)]


def spread_inner_body(picks, acts, out):
    for half in range(2):
        for tap, part in enumerate(spread_cells(acts[...], picks[half])):
            out[half, 2:8, 1:5, :, C * tap : C * (tap + 1)] = part.reshape(6, 4, 32, C)


def spread_inner(picks, acts):
    vmem = pl.BlockSpec(memory_space=pltpu.VMEM)
    return pl.pallas_call(
        spread_inner_body,
        out_shape=jax.ShapeDtypeStruct((2, 8, 6, 32, 3 * C), jnp.bfloat16),
        in_specs=[vmem] * 2,
        out_specs=vmem,
        compiler_params=pltpu.CompilerParams(vmem_limit_bytes=20 * 1024 * 1024),
        cost_estimate=pl.CostEstimate(flops=1000, bytes_accessed=1000, transcendentals=0),
    )(picks, acts.reshape(-1, C))


def spread_halo_body(scalars, picks, ends, beside, across, _, out):
    core = scalars[0]
    cells = jnp.concatenate(
        [part[...].reshape(-1, C) for part in (ends, beside, across)], 0
    )
    for half in range(2):
        for tap, part in enumerate(spread_cells(cells, picks[half])):
            lanes = slice(C * tap, C * (tap + 1))
            out[half, 0:2, 1:5, :, lanes] = part[0:256].reshape(2, 4, 32, C)
            near, far = part[256:512].reshape(8, 1, 32, C), part[512:768].reshape(8, 1, 32, C)

            @pl.when(core == 0)
            def _():
                out[half, :, 0:1, :, lanes] = far
                out[half, :, 5:6, :, lanes] = near

            @pl.when(core == 1)
            def _():
                out[half, :, 0:1, :, lanes] = near
                out[half, :, 5:6, :, lanes] = far


def spread_halo(scalars, picks, ends, beside, across, spread):
    vmem = pl.BlockSpec(memory_space=pltpu.VMEM)
    return pl.pallas_call(
        spread_halo_body,
        out_shape=jax.ShapeDtypeStruct(spread.shape, spread.dtype),
        in_specs=[pl.BlockSpec(memory_space=pltpu.SMEM)] + [vmem] * 5,
        out_specs=vmem,
        input_output_aliases={5: 0},
        compiler_params=pltpu.CompilerParams(vmem_limit_bytes=20 * 1024 * 1024),
        cost_estimate=pl.CostEstimate(flops=1000, bytes_accessed=1000, transcendentals=0),
    )(scalars, picks, ends, beside, across, spread)


def conv_body(
    scalars, lag_weights, spread, tail, own0, own1, own2, own3, got0, got1, got2, got3,
    out, weights, total, sems, *, finish,
):
    frames, rows, cols = 6, 4, 32
    own, got = (own0, own1, own2, own3), (got0, got1, got2, got3)

    def copies(half, sources):
        return [
            pltpu.make_async_copy(
                sources[k], weights.at[half, :, pl.ds(BUNDLE * k, BUNDLE), :], sems.at[half, k]
            )
            for k in range(4)
        ]

    core = scalars[0]

    @pl.when(core == 0)
    def _():
        for copy in copies(0, own) + copies(1, got):
            copy.start()

    @pl.when(core == 1)
    def _():
        for copy in copies(0, got) + copies(1, own):
            copy.start()

    total[...] = jnp.zeros_like(total)

    def window(half, lag, row, long=frames, tall=rows, first=0, count=3):
        block = spread[half, lag : lag + long, row : row + tall, :, C * first : C * (first + count)]
        return block.reshape(long * tall * cols, C * count)

    def taps(half, tap, lanes, count=3):
        return weights[half, tap : tap + count, :, lanes].reshape(count * C, -1)

    def times(cells, block):
        return jnp.dot(cells, block, preferred_element_type=jnp.float32)

    def add(lag, part, lanes):
        for f in range(frames):
            total[f, :, lanes] += part[f].reshape(rows * cols, -1) * lag_weights[lag, f]

    low, high = slice(0, 256), slice(256, C)

    def two_rows(half, lags, places, first_taps):
        for lag, row, tap in zip(lags, places, first_taps):
            part = times(window(half, lag, row), taps(half, tap, low))
            add(lag, part.reshape(frames, rows, cols, 256), low)
        more_frames, more_rows = lags[1] - lags[0], places[1] - places[0]
        cells = window(half, lags[0], places[0], frames + more_frames, rows + more_rows)
        block = jnp.concatenate([taps(half, tap, high) for tap in first_taps], 1)
        part = times(cells, block).reshape(frames + more_frames, rows + more_rows, cols, 256)
        add(lags[0], part[:frames, :rows, :, :128], high)
        add(lags[1], part[more_frames:, more_rows:, :, 128:], high)

    for copy in copies(0, own):
        copy.wait()
    two_rows(0, (0, 1), (0, 0), (0, 9))
    two_rows(0, (0, 0), (1, 2), (3, 6))
    everything = slice(0, C)
    part = times(window(0, 1, 1, count=2), taps(0, 12, everything, 2))
    add(1, part.reshape(frames, rows, cols, C), everything)
    for copy in copies(1, own):
        copy.wait()
    part = times(window(1, 1, 1, first=2, count=1), taps(1, 1, everything, 1))
    add(1, part.reshape(frames, rows, cols, C), everything)
    two_rows(1, (1, 2), (2, 2), (2, 11))
    two_rows(1, (2, 2), (0, 1), (5, 8))

    finish(scalars, total, tail, out)


def finish_norm(scalars, total, tail, out):
    for f in range(6):
        data = total[f]
        scale = lax.rsqrt(jnp.mean(data * data, axis=-1, keepdims=True) + 1e-06)
        lifted = data * scale * tail[...]
        out[f] = (lifted * (1.0 / (1.0 + jnp.exp(-lifted)))).astype(jnp.bfloat16)


def finish_add(scalars, total, tail, out):
    for f in range(6):
        summed = tail[f].astype(jnp.float32) + total[f]
        out[f] = jnp.where(f < scalars[1], summed, 0.0).astype(jnp.bfloat16)


def conv(scalars, lag_weights, spread, tail, own, got, finish):
    smem = pl.BlockSpec(memory_space=pltpu.SMEM)
    vmem = pl.BlockSpec(memory_space=pltpu.VMEM)
    return pl.pallas_call(
        lambda *refs: conv_body(*refs, finish=finish),
        out_shape=jax.ShapeDtypeStruct((6, 128, C), jnp.bfloat16),
        in_specs=[smem, smem] + [vmem] * 2 + [pl.BlockSpec(memory_space=pl.ANY)] * 8,
        out_specs=vmem,
        scratch_shapes=[
            pltpu.VMEM((2, HALF, C, C), jnp.bfloat16),
            pltpu.VMEM((6, 128, C), jnp.float32),
            pltpu.SemaphoreType.DMA((2, 4)),
        ],
        compiler_params=pltpu.CompilerParams(vmem_limit_bytes=26 * 1024 * 1024),
        cost_estimate=pl.CostEstimate(flops=1000, bytes_accessed=1000, transcendentals=0),
    )(scalars, lag_weights, spread, tail, *own, *got)


def clip_positions(clip_lengths, frame_index):
    ends = jnp.cumsum(clip_lengths)
    begins = jnp.max(jnp.where(ends[None, :] <= frame_index[:, None], ends[None, :], 0), axis=1)
    return frame_index - begins


def norm_act(values, gain):
    data = values.astype(jnp.float32)
    mean_square = jnp.mean(data * data, axis=-1, keepdims=True)
    scaled = data * lax.rsqrt(mean_square + 1e-06)
    return jax.nn.silu(scaled * gain).astype(jnp.bfloat16)


def before_in_group(z, y, x, c):
    group = z * NY + y - 1
    return None if group < 0 else (group // NY, group % NY, x, c)


def across_chips(z, y, x, c):
    x = x - 1 if c == 0 else x + 1
    return (z, y, x, 1 - c) if 0 <= x < NX else None


def across_and_before(z, y, x, c):
    place = across_chips(z, y, x, c)
    return None if place is None else before_in_group(*place)


def per_device(
    frames, clip_lengths, group_start, group_count, kernel_one, kernel_two, gain_one, gain_two
):
    slots = frames.shape[0]
    slot = jnp.arange(slots, dtype=jnp.int32)
    position = clip_positions(clip_lengths, group_start[0] + slot)
    lag_weights = jnp.stack([position >= 2, position >= 1, position >= 0]).astype(jnp.float32)
    scalars = jnp.stack([lax.axis_index("c").astype(jnp.int32), group_count[0]])
    orders = channel_orders()

    first_core = lax.axis_index("c") == 0
    last = group_count[0] - 2

    def sides(acts):
        return (
            jnp.where(first_core, acts[:, 3:4], acts[:, 0:1]),
            jnp.where(first_core, acts[:, 0:1], acts[:, 3:4]),
        )

    def last_two(acts):
        return lax.dynamic_slice_in_dim(acts, last, 2, 0)

    acts_one = norm_act(frames, gain_one)
    own = jnp.stack([own_half(kernel_one), own_half(kernel_two)])
    pieces = z_stage(own)
    ends = fetch(last_two(acts_one), before_in_group)
    picks = make_picks(orders)
    pieces, picks, lag_weights, scalars = lax.optimization_barrier(
        (pieces, picks, lag_weights, scalars)
    )

    opposite = fetch(pieces, small_source(2))
    after = fetch(pieces, small_source(1))
    gated, ends = lax.optimization_barrier((pieces, ends))
    parts = [pieces, after, fetch(gated, small_source(-1)), opposite]
    inner, outer = sides(jnp.concatenate([ends, acts_one], 0))
    across = fetch(outer, across_chips)
    parts, across = lax.optimization_barrier((parts, across))

    one_bundle, two_bundle = join_rows(parts, 0), join_rows(parts, 1)
    one_bundles = bulk_stage(one_bundle)
    one_own, two_own = lax.optimization_barrier((one_bundle, two_bundle))
    one_others, two_others = [fetch(one_own, sibling)], [fetch(two_own, sibling)]
    two_bundle, one_others, two_others, inner = lax.optimization_barrier(
        (two_bundle, one_others, two_others, inner)
    )
    beside = fetch(inner, sibling)
    spread = spread_halo(scalars, picks, ends, beside, across, spread_inner(picks, acts_one))
    one_bundles, one_others, two_others, spread = lax.optimization_barrier(
        (one_bundles, one_others, two_others, spread)
    )
    one_others += [fetch(b, sibling) for b in one_bundles[1:]]

    two_bundles = bulk_stage(two_bundle)
    acts_two = conv(
        scalars, lag_weights, spread, gain_two.reshape(1, C), one_bundles, one_others, finish_norm
    ).reshape(frames.shape)

    inner, outer = sides(acts_two)
    ends, corners, outer = lax.optimization_barrier((last_two(acts_two), last_two(outer), outer))
    ends = fetch(ends, before_in_group)
    across = fetch(outer, across_chips)
    corners, two_bundles = lax.optimization_barrier((corners, two_bundles))
    corners = fetch(corners, across_and_before)
    spread = spread_inner(picks, acts_two)
    ends, corners, across, spread, two_bundles = lax.optimization_barrier(
        (ends, corners, across, spread, two_bundles)
    )
    beside = fetch(jnp.concatenate([sides(ends)[0], inner], 0), sibling)
    two_others.append(fetch(two_bundles[1], sibling))
    two_last, beside = lax.optimization_barrier((two_bundles[2:], beside))
    two_others += [fetch(b, sibling) for b in two_last]
    across = jnp.concatenate([corners, across], 0)
    spread = spread_halo(scalars, picks, ends, beside, across, spread)
    result = conv(
        scalars, lag_weights, spread, frames.reshape(slots, 128, C), two_bundles, two_others,
        finish_add,
    )
    return result.reshape(frames.shape)


def solution(mesh):
    torus = Mesh(mesh.devices.reshape(NZ, NY, NX, NC), AXES)
    group, row = ("z", "y"), ("x", "c")
    return jax.shard_map(
        per_device,
        mesh=torus,
        in_specs=(
            P(group, row, None, None),
            P(),
            P(group),
            P(group),
            P(None, None, None, group, None),
            P(None, None, None, group, None),
            P(),
            P(),
        ),
        out_specs=P(group, row, None, None),
        check_vma=False,
    )
```

```python
import jax
import jax.numpy as jnp
import numpy as np
from jax import lax
from jax.experimental import pallas as pl
from jax.experimental.pallas import tpu as pltpu
from jax.sharding import Mesh
from jax.sharding import PartitionSpec as P

NZ, NY, NX, NC = 8, 4, 4, 2
AXES = ("z", "y", "x", "c")
C = 384
SHARD = 12
HALF = 14
BUNDLE = 96
ROUND = (0, 1, -1, 2)

FETCH = np.array([[0, 4], [2, -2], [1, -3], [3, -1]])


def number(z, y, x, c):
    return ((z % NZ * NY + y % NY) * NX + x % NX) * NC + c


def fetch(array, source_of):
    pairs = []
    for z in range(NZ):
        for y in range(NY):
            for x in range(NX):
                for c in range(NC):
                    source = source_of(z, y, x, c)
                    if source is not None:
                        pairs.append((number(*source), number(z, y, x, c)))
    return lax.ppermute(array, AXES, pairs)


def z_source(which):
    def source(z, y, x, c):
        odd = z % 2
        from_z = z - odd + int(FETCH[(x + 2 * odd) % NX, which])
        return (from_z, y + 2 * odd - 1, x, c) if c == 0 else (from_z, y, x, c)

    return source


def small_source(step):
    return lambda z, y, x, c: (z, y, x + step, c) if c == 0 else (z, y + step, x, c)


def bulk_source(step):
    if step == 2:
        return lambda z, y, x, c: (z + 1 if z % 2 != c else z - 1, y, x, c)
    return lambda z, y, x, c: (z, y + step, x, c) if c == 0 else (z, y, x + step, c)


def sibling(z, y, x, c):
    return (z, y, x, 1 - c)


def own_half(kernel):
    start = lax.axis_index("c") * (27 - HALF)
    taps = lax.dynamic_slice_in_dim(kernel.reshape(27, SHARD, C), start, HALF, 0)
    return taps.reshape(HALF * SHARD, C)


def z_stage(own):
    return jnp.stack([fetch(own, z_source(0)), fetch(own, z_source(1))], 1)


def join_body(*refs):
    parts, out = refs[:-1], refs[-1]
    for tap in range(HALF):
        rows = [
            part[piece, pl.ds(SHARD * tap, SHARD), :].astype(jnp.float32)
            for part in parts
            for piece in range(2)
        ]
        out[tap] = jnp.concatenate(rows, 0).astype(jnp.bfloat16)


def join_rows(parts, which):
    block = pl.BlockSpec((None, 2, HALF * SHARD, C), lambda i: (which, 0, 0, 0))
    return pl.pallas_call(
        join_body,
        grid=(1,),
        out_shape=jax.ShapeDtypeStruct((HALF, BUNDLE, C), jnp.bfloat16),
        in_specs=[block] * 4,
        out_specs=pl.BlockSpec((HALF, BUNDLE, C), lambda i: (0, 0, 0)),
        compiler_params=pltpu.CompilerParams(vmem_limit_bytes=16 * 1024 * 1024),
        cost_estimate=pl.CostEstimate(flops=0, bytes_accessed=2_000_000, transcendentals=0),
    )(*parts)


def bulk_stage(bundle):
    return [bundle] + [fetch(bundle, bulk_source(step)) for step in ROUND[1:]]


def channel_orders():
    z, y, x = (lax.axis_index(a) for a in ("z", "y", "x"))
    table = jnp.asarray(FETCH, jnp.int32)
    around = jnp.array(ROUND, jnp.int32)
    aside = jnp.array((0, 1, -1, 0), jnp.int32)
    odd = z % 2
    at_z = z + jnp.array((0, 0, 0, 1), jnp.int32) * jnp.where(odd == 1, 1, -1)
    at_x = x + around[None, :] + 2 * (at_z % 2)[:, None]
    piece_z = (at_z - at_z % 2)[:, None, None] + table[at_x % NX]
    piece_y = (y + aside + 2 * (at_z % 2) - 1)[:, None, None]
    first = piece_z % NZ * NY + piece_y % NY
    at_z = z + jnp.array((0, 0, 0, 1), jnp.int32) * jnp.where(odd == 0, 1, -1)
    piece_z = (at_z - at_z % 2)[:, None] + table[(x + aside + 2 * (at_z % 2)) % NX]
    piece_y = y + around
    second = piece_z[:, None, :] % NZ * NY + piece_y[None, :, None] % NY
    ramp = jnp.arange(SHARD, dtype=jnp.int32)
    return jnp.stack([(half.reshape(-1, 1) * SHARD + ramp).reshape(C) for half in (first, second)])


def picks_body(order, out):
    for half in range(2):
        out[half] = (
            lax.broadcasted_iota(jnp.int32, (C, C), 0) == order[half : half + 1, :]
        ).astype(jnp.bfloat16)


def make_picks(orders):
    vmem = pl.BlockSpec(memory_space=pltpu.VMEM)
    return pl.pallas_call(
        picks_body,
        out_shape=jax.ShapeDtypeStruct((2, C, C), jnp.bfloat16),
        in_specs=[vmem],
        out_specs=vmem,
        cost_estimate=pl.CostEstimate(flops=1000, bytes_accessed=1000, transcendentals=0),
    )(orders)


def spread_cells(cells, pick):
    rows = cells.shape[0]
    plain = jnp.dot(cells, pick, preferred_element_type=jnp.float32)
    col = lax.broadcasted_iota(jnp.int32, (rows, C), 0) % 32
    before = jnp.where(col == 0, 0.0, pltpu.roll(plain, 1, 0))
    after = jnp.where(col == 31, 0.0, pltpu.roll(plain, rows - 1, 0))
    return [part.astype(jnp.bfloat16) for part in (before, plain, after)]


def spread_inner_body(picks, acts, out):
    for half in range(2):
        for tap, part in enumerate(spread_cells(acts[...], picks[half])):
            out[half, 2:8, 1:5, :, C * tap : C * (tap + 1)] = part.reshape(6, 4, 32, C)


def spread_inner(picks, acts):
    vmem = pl.BlockSpec(memory_space=pltpu.VMEM)
    return pl.pallas_call(
        spread_inner_body,
        out_shape=jax.ShapeDtypeStruct((2, 8, 6, 32, 3 * C), jnp.bfloat16),
        in_specs=[vmem] * 2,
        out_specs=vmem,
        compiler_params=pltpu.CompilerParams(vmem_limit_bytes=20 * 1024 * 1024),
        cost_estimate=pl.CostEstimate(flops=1000, bytes_accessed=1000, transcendentals=0),
    )(picks, acts.reshape(-1, C))


def spread_halo_body(scalars, picks, ends, beside, across, _, out):
    core = scalars[0]
    cells = jnp.concatenate(
        [part[...].reshape(-1, C) for part in (ends, beside, across)], 0
    )
    for half in range(2):
        for tap, part in enumerate(spread_cells(cells, picks[half])):
            lanes = slice(C * tap, C * (tap + 1))
            out[half, 0:2, 1:5, :, lanes] = part[0:256].reshape(2, 4, 32, C)
            near, far = part[256:512].reshape(8, 1, 32, C), part[512:768].reshape(8, 1, 32, C)

            @pl.when(core == 0)
            def _():
                out[half, :, 0:1, :, lanes] = far
                out[half, :, 5:6, :, lanes] = near

            @pl.when(core == 1)
            def _():
                out[half, :, 0:1, :, lanes] = near
                out[half, :, 5:6, :, lanes] = far


def spread_halo(scalars, picks, ends, beside, across, spread):
    vmem = pl.BlockSpec(memory_space=pltpu.VMEM)
    return pl.pallas_call(
        spread_halo_body,
        out_shape=jax.ShapeDtypeStruct(spread.shape, spread.dtype),
        in_specs=[pl.BlockSpec(memory_space=pltpu.SMEM)] + [vmem] * 5,
        out_specs=vmem,
        input_output_aliases={5: 0},
        compiler_params=pltpu.CompilerParams(vmem_limit_bytes=20 * 1024 * 1024),
        cost_estimate=pl.CostEstimate(flops=1000, bytes_accessed=1000, transcendentals=0),
    )(scalars, picks, ends, beside, across, spread)


def conv_body(
    scalars, lag_weights, spread, tail, own0, own1, own2, own3, got0, got1, got2, got3,
    out, weights, total, sems, *, finish,
):
    frames, rows, cols = 6, 4, 32
    own, got = (own0, own1, own2, own3), (got0, got1, got2, got3)

    def copies(half, sources):
        return [
            pltpu.make_async_copy(
                sources[k], weights.at[half, :, pl.ds(BUNDLE * k, BUNDLE), :], sems.at[half, k]
            )
            for k in range(4)
        ]

    core = scalars[0]

    @pl.when(core == 0)
    def _():
        for copy in copies(0, own) + copies(1, got):
            copy.start()

    @pl.when(core == 1)
    def _():
        for copy in copies(0, got) + copies(1, own):
            copy.start()

    total[...] = jnp.zeros_like(total)

    def window(half, lag, row, long=frames, tall=rows, first=0, count=3):
        block = spread[half, lag : lag + long, row : row + tall, :, C * first : C * (first + count)]
        return block.reshape(long * tall * cols, C * count)

    def taps(half, tap, lanes, count=3):
        return weights[half, tap : tap + count, :, lanes].reshape(count * C, -1)

    def times(cells, block):
        return jnp.dot(cells, block, preferred_element_type=jnp.float32)

    def add(lag, part, lanes):
        for f in range(frames):
            total[f, :, lanes] += part[f].reshape(rows * cols, -1) * lag_weights[lag, f]

    low, high = slice(0, 256), slice(256, C)

    def two_rows(half, lags, places, first_taps):
        for lag, row, tap in zip(lags, places, first_taps):
            part = times(window(half, lag, row), taps(half, tap, low))
            add(lag, part.reshape(frames, rows, cols, 256), low)
        more_frames, more_rows = lags[1] - lags[0], places[1] - places[0]
        cells = window(half, lags[0], places[0], frames + more_frames, rows + more_rows)
        block = jnp.concatenate([taps(half, tap, high) for tap in first_taps], 1)
        part = times(cells, block).reshape(frames + more_frames, rows + more_rows, cols, 256)
        add(lags[0], part[:frames, :rows, :, :128], high)
        add(lags[1], part[more_frames:, more_rows:, :, 128:], high)

    for copy in copies(0, own):
        copy.wait()
    two_rows(0, (0, 1), (0, 0), (0, 9))
    two_rows(0, (0, 0), (1, 2), (3, 6))
    everything = slice(0, C)
    part = times(window(0, 1, 1, count=2), taps(0, 12, everything, 2))
    add(1, part.reshape(frames, rows, cols, C), everything)
    for copy in copies(1, own):
        copy.wait()
    part = times(window(1, 1, 1, first=2, count=1), taps(1, 1, everything, 1))
    add(1, part.reshape(frames, rows, cols, C), everything)
    two_rows(1, (1, 2), (2, 2), (2, 11))
    two_rows(1, (2, 2), (0, 1), (5, 8))

    finish(scalars, total, tail, out)


def finish_norm(scalars, total, tail, out):
    for f in range(6):
        data = total[f]
        scale = lax.rsqrt(jnp.mean(data * data, axis=-1, keepdims=True) + 1e-06)
        lifted = data * scale * tail[...]
        out[f] = (lifted * (1.0 / (1.0 + jnp.exp(-lifted)))).astype(jnp.bfloat16)


def finish_add(scalars, total, tail, out):
    for f in range(6):
        summed = tail[f].astype(jnp.float32) + total[f]
        out[f] = jnp.where(f < scalars[1], summed, 0.0).astype(jnp.bfloat16)


def conv(scalars, lag_weights, spread, tail, own, got, finish):
    smem = pl.BlockSpec(memory_space=pltpu.SMEM)
    vmem = pl.BlockSpec(memory_space=pltpu.VMEM)
    return pl.pallas_call(
        lambda *refs: conv_body(*refs, finish=finish),
        out_shape=jax.ShapeDtypeStruct((6, 128, C), jnp.bfloat16),
        in_specs=[smem, smem] + [vmem] * 2 + [pl.BlockSpec(memory_space=pl.ANY)] * 8,
        out_specs=vmem,
        scratch_shapes=[
            pltpu.VMEM((2, HALF, C, C), jnp.bfloat16),
            pltpu.VMEM((6, 128, C), jnp.float32),
            pltpu.SemaphoreType.DMA((2, 4)),
        ],
        compiler_params=pltpu.CompilerParams(vmem_limit_bytes=26 * 1024 * 1024),
        cost_estimate=pl.CostEstimate(flops=1000, bytes_accessed=1000, transcendentals=0),
    )(scalars, lag_weights, spread, tail, *own, *got)


def clip_positions(clip_lengths, frame_index):
    ends = jnp.cumsum(clip_lengths)
    begins = jnp.max(jnp.where(ends[None, :] <= frame_index[:, None], ends[None, :], 0), axis=1)
    return frame_index - begins


def norm_act(values, gain):
    data = values.astype(jnp.float32)
    mean_square = jnp.mean(data * data, axis=-1, keepdims=True)
    scaled = data * lax.rsqrt(mean_square + 1e-06)
    return jax.nn.silu(scaled * gain).astype(jnp.bfloat16)


def before_in_group(z, y, x, c):
    group = z * NY + y - 1
    return None if group < 0 else (group // NY, group % NY, x, c)


def across_chips(z, y, x, c):
    x = x - 1 if c == 0 else x + 1
    return (z, y, x, 1 - c) if 0 <= x < NX else None


def across_and_before(z, y, x, c):
    place = across_chips(z, y, x, c)
    return None if place is None else before_in_group(*place)


def per_device(
    frames, clip_lengths, group_start, group_count, kernel_one, kernel_two, gain_one, gain_two
):
    slots = frames.shape[0]
    slot = jnp.arange(slots, dtype=jnp.int32)
    position = clip_positions(clip_lengths, group_start[0] + slot)
    lag_weights = jnp.stack([position >= 2, position >= 1, position >= 0]).astype(jnp.float32)
    scalars = jnp.stack([lax.axis_index("c").astype(jnp.int32), group_count[0]])
    orders = channel_orders()

    first_core = lax.axis_index("c") == 0
    last = group_count[0] - 2

    def sides(acts):
        return (
            jnp.where(first_core, acts[:, 3:4], acts[:, 0:1]),
            jnp.where(first_core, acts[:, 0:1], acts[:, 3:4]),
        )

    def last_two(acts):
        return lax.dynamic_slice_in_dim(acts, last, 2, 0)

    acts_one = norm_act(frames, gain_one)
    own = jnp.stack([own_half(kernel_one), own_half(kernel_two)])
    pieces = z_stage(own)
    ends = fetch(last_two(acts_one), before_in_group)
    picks = make_picks(orders)
    pieces, picks, lag_weights, scalars = lax.optimization_barrier(
        (pieces, picks, lag_weights, scalars)
    )

    opposite = fetch(pieces, small_source(2))
    after = fetch(pieces, small_source(1))
    parts = [pieces, after, fetch(pieces, small_source(-1)), opposite]
    inner, outer = sides(jnp.concatenate([ends, acts_one], 0))
    across = fetch(outer, across_chips)
    parts, across = lax.optimization_barrier((parts, across))

    one_bundle, two_bundle = join_rows(parts, 0), join_rows(parts, 1)
    one_bundles = bulk_stage(one_bundle)
    one_own, two_own = lax.optimization_barrier((one_bundle, two_bundle))
    one_others, two_others = [fetch(one_own, sibling)], [fetch(two_own, sibling)]
    two_bundle, one_others, two_others, inner = lax.optimization_barrier(
        (two_bundle, one_others, two_others, inner)
    )
    beside = fetch(inner, sibling)
    spread = spread_halo(scalars, picks, ends, beside, across, spread_inner(picks, acts_one))
    one_bundles, one_others, two_others, spread = lax.optimization_barrier(
        (one_bundles, one_others, two_others, spread)
    )
    one_others += [fetch(b, sibling) for b in one_bundles[1:]]

    two_bundles = bulk_stage(two_bundle)
    acts_two = conv(
        scalars, lag_weights, spread, gain_two.reshape(1, C), one_bundles, one_others, finish_norm
    ).reshape(frames.shape)

    inner, outer = sides(acts_two)
    ends, corners, outer = lax.optimization_barrier((last_two(acts_two), last_two(outer), outer))
    ends = fetch(ends, before_in_group)
    across = fetch(outer, across_chips)
    corners, two_bundles = lax.optimization_barrier((corners, two_bundles))
    corners = fetch(corners, across_and_before)
    spread = spread_inner(picks, acts_two)
    ends, corners, across, spread, two_bundles = lax.optimization_barrier(
        (ends, corners, across, spread, two_bundles)
    )
    beside = fetch(jnp.concatenate([sides(ends)[0], inner], 0), sibling)
    two_others.append(fetch(two_bundles[1], sibling))
    two_last, beside = lax.optimization_barrier((two_bundles[2:], beside))
    two_others += [fetch(b, sibling) for b in two_last]
    across = jnp.concatenate([corners, across], 0)
    spread = spread_halo(scalars, picks, ends, beside, across, spread)
    result = conv(
        scalars, lag_weights, spread, frames.reshape(slots, 128, C), two_bundles, two_others,
        finish_add,
    )
    return result.reshape(frames.shape)


def solution(mesh):
    torus = Mesh(mesh.devices.reshape(NZ, NY, NX, NC), AXES)
    group, row = ("z", "y"), ("x", "c")
    return jax.shard_map(
        per_device,
        mesh=torus,
        in_specs=(
            P(group, row, None, None),
            P(),
            P(group),
            P(group),
            P(None, None, None, group, None),
            P(None, None, None, group, None),
            P(),
            P(),
        ),
        out_specs=P(group, row, None, None),
        check_vma=False,
    )
```

```python
import jax
import jax.numpy as jnp
import numpy as np
from jax import lax
from jax.experimental import pallas as pl
from jax.experimental.pallas import tpu as pltpu
from jax.sharding import Mesh
from jax.sharding import PartitionSpec as P

NZ, NY, NX, NC = 8, 4, 4, 2
AXES = ("z", "y", "x", "c")
C = 384
SHARD = 12
HALF = 14
BUNDLE = 96
ROUND = (0, 1, -1, 2)

FETCH = np.array([[0, 4], [2, -2], [1, -3], [3, -1]])


def number(z, y, x, c):
    return ((z % NZ * NY + y % NY) * NX + x % NX) * NC + c


def fetch(array, source_of):
    pairs = []
    for z in range(NZ):
        for y in range(NY):
            for x in range(NX):
                for c in range(NC):
                    source = source_of(z, y, x, c)
                    if source is not None:
                        pairs.append((number(*source), number(z, y, x, c)))
    return lax.ppermute(array, AXES, pairs)


def z_source(which):
    def source(z, y, x, c):
        odd = z % 2
        from_z = z - odd + int(FETCH[(x + 2 * odd) % NX, which])
        return (from_z, y + 2 * odd - 1, x, c) if c == 0 else (from_z, y, x, c)

    return source


def small_source(step):
    return lambda z, y, x, c: (z, y, x + step, c) if c == 0 else (z, y + step, x, c)


def bulk_source(step):
    if step == 2:
        return lambda z, y, x, c: (z + 1 if z % 2 != c else z - 1, y, x, c)
    return lambda z, y, x, c: (z, y + step, x, c) if c == 0 else (z, y, x + step, c)


def sibling(z, y, x, c):
    return (z, y, x, 1 - c)


def own_half(kernel):
    start = lax.axis_index("c") * (27 - HALF)
    taps = lax.dynamic_slice_in_dim(kernel.reshape(27, SHARD, C), start, HALF, 0)
    return taps.reshape(HALF * SHARD, C)


def z_stage(own):
    return jnp.stack([fetch(own, z_source(0)), fetch(own, z_source(1))], 1)


def join_body(*refs):
    parts, out = refs[:-1], refs[-1]
    for tap in range(HALF):
        rows = [
            part[piece, pl.ds(SHARD * tap, SHARD), :].astype(jnp.float32)
            for part in parts
            for piece in range(2)
        ]
        out[tap] = jnp.concatenate(rows, 0).astype(jnp.bfloat16)


def join_rows(parts, which):
    block = pl.BlockSpec((None, 2, HALF * SHARD, C), lambda i: (which, 0, 0, 0))
    return pl.pallas_call(
        join_body,
        grid=(1,),
        out_shape=jax.ShapeDtypeStruct((HALF, BUNDLE, C), jnp.bfloat16),
        in_specs=[block] * 4,
        out_specs=pl.BlockSpec((HALF, BUNDLE, C), lambda i: (0, 0, 0)),
        compiler_params=pltpu.CompilerParams(vmem_limit_bytes=16 * 1024 * 1024),
        cost_estimate=pl.CostEstimate(flops=0, bytes_accessed=2_000_000, transcendentals=0),
    )(*parts)


def bulk_stage(bundle):
    return [bundle] + [fetch(bundle, bulk_source(step)) for step in ROUND[1:]]


def channel_orders():
    z, y, x = (lax.axis_index(a) for a in ("z", "y", "x"))
    table = jnp.asarray(FETCH, jnp.int32)
    around = jnp.array(ROUND, jnp.int32)
    aside = jnp.array((0, 1, -1, 0), jnp.int32)
    odd = z % 2
    at_z = z + jnp.array((0, 0, 0, 1), jnp.int32) * jnp.where(odd == 1, 1, -1)
    at_x = x + around[None, :] + 2 * (at_z % 2)[:, None]
    piece_z = (at_z - at_z % 2)[:, None, None] + table[at_x % NX]
    piece_y = (y + aside + 2 * (at_z % 2) - 1)[:, None, None]
    first = piece_z % NZ * NY + piece_y % NY
    at_z = z + jnp.array((0, 0, 0, 1), jnp.int32) * jnp.where(odd == 0, 1, -1)
    piece_z = (at_z - at_z % 2)[:, None] + table[(x + aside + 2 * (at_z % 2)) % NX]
    piece_y = y + around
    second = piece_z[:, None, :] % NZ * NY + piece_y[None, :, None] % NY
    ramp = jnp.arange(SHARD, dtype=jnp.int32)
    return jnp.stack([(half.reshape(-1, 1) * SHARD + ramp).reshape(C) for half in (first, second)])


def picks_body(order, out):
    for half in range(2):
        out[:, C * half : C * (half + 1)] = (
            lax.broadcasted_iota(jnp.int32, (C, C), 0) == order[half : half + 1, :]
        ).astype(jnp.bfloat16)


def make_picks(orders):
    vmem = pl.BlockSpec(memory_space=pltpu.VMEM)
    return pl.pallas_call(
        picks_body,
        out_shape=jax.ShapeDtypeStruct((C, 2 * C), jnp.bfloat16),
        in_specs=[vmem],
        out_specs=vmem,
        cost_estimate=pl.CostEstimate(flops=1000, bytes_accessed=1000, transcendentals=0),
    )(orders)


def spread_cells(cells, picks):
    rows = cells.shape[0]
    both = jnp.dot(cells, picks, preferred_element_type=jnp.float32)
    col = lax.broadcasted_iota(jnp.int32, (rows, C), 0) % 32
    for half in range(2):
        plain = both[:, C * half : C * (half + 1)]
        before = jnp.where(col == 0, 0.0, pltpu.roll(plain, 1, 0))
        after = jnp.where(col == 31, 0.0, pltpu.roll(plain, rows - 1, 0))
        for tap, part in enumerate((before, plain, after)):
            yield half, tap, part.astype(jnp.bfloat16)


def spread_inner_body(picks, acts, out):
    for half, tap, part in spread_cells(acts[...], picks[...]):
        out[half, 2:8, 1:5, :, C * tap : C * (tap + 1)] = part.reshape(6, 4, 32, C)


def spread_inner(picks, acts):
    vmem = pl.BlockSpec(memory_space=pltpu.VMEM)
    return pl.pallas_call(
        spread_inner_body,
        out_shape=jax.ShapeDtypeStruct((2, 8, 6, 32, 3 * C), jnp.bfloat16),
        in_specs=[vmem] * 2,
        out_specs=vmem,
        compiler_params=pltpu.CompilerParams(vmem_limit_bytes=20 * 1024 * 1024),
        cost_estimate=pl.CostEstimate(flops=1000, bytes_accessed=1000, transcendentals=0),
    )(picks, acts.reshape(-1, C))


def spread_halo_body(scalars, picks, ends, beside, across, _, out):
    core = scalars[0]
    cells = jnp.concatenate(
        [part[...].reshape(-1, C) for part in (ends, beside, across)], 0
    )
    for half, tap, part in spread_cells(cells, picks[...]):
        lanes = slice(C * tap, C * (tap + 1))
        out[half, 0:2, 1:5, :, lanes] = part[0:256].reshape(2, 4, 32, C)
        near, far = part[256:512].reshape(8, 1, 32, C), part[512:768].reshape(8, 1, 32, C)

        @pl.when(core == 0)
        def _():
            out[half, :, 0:1, :, lanes] = far
            out[half, :, 5:6, :, lanes] = near

        @pl.when(core == 1)
        def _():
            out[half, :, 0:1, :, lanes] = near
            out[half, :, 5:6, :, lanes] = far


def spread_halo(scalars, picks, ends, beside, across, spread):
    vmem = pl.BlockSpec(memory_space=pltpu.VMEM)
    return pl.pallas_call(
        spread_halo_body,
        out_shape=jax.ShapeDtypeStruct(spread.shape, spread.dtype),
        in_specs=[pl.BlockSpec(memory_space=pltpu.SMEM)] + [vmem] * 5,
        out_specs=vmem,
        input_output_aliases={5: 0},
        compiler_params=pltpu.CompilerParams(vmem_limit_bytes=20 * 1024 * 1024),
        cost_estimate=pl.CostEstimate(flops=1000, bytes_accessed=1000, transcendentals=0),
    )(scalars, picks, ends, beside, across, spread)


def conv_body(
    scalars, lag_weights, spread, tail, own0, own1, own2, own3, got0, got1, got2, got3,
    out, weights, total, sems, *, finish,
):
    frames, rows, cols = 6, 4, 32
    own, got = (own0, own1, own2, own3), (got0, got1, got2, got3)

    def copies(half, sources):
        return [
            pltpu.make_async_copy(
                sources[k], weights.at[half, :, pl.ds(BUNDLE * k, BUNDLE), :], sems.at[half, k]
            )
            for k in range(4)
        ]

    core = scalars[0]

    @pl.when(core == 0)
    def _():
        for copy in copies(0, own) + copies(1, got):
            copy.start()

    @pl.when(core == 1)
    def _():
        for copy in copies(0, got) + copies(1, own):
            copy.start()

    total[...] = jnp.zeros_like(total)

    def window(half, lag, row, long=frames, tall=rows, first=0, count=3):
        block = spread[half, lag : lag + long, row : row + tall, :, C * first : C * (first + count)]
        return block.reshape(long * tall * cols, C * count)

    def taps(half, tap, lanes, count=3):
        return weights[half, tap : tap + count, :, lanes].reshape(count * C, -1)

    def times(cells, block):
        return jnp.dot(cells, block, preferred_element_type=jnp.float32)

    def add(lag, part, lanes):
        for f in range(frames):
            total[f, :, lanes] += part[f].reshape(rows * cols, -1) * lag_weights[lag, f]

    low, high = slice(0, 256), slice(256, C)

    def two_rows(half, lags, places, first_taps):
        for lag, row, tap in zip(lags, places, first_taps):
            part = times(window(half, lag, row), taps(half, tap, low))
            add(lag, part.reshape(frames, rows, cols, 256), low)
        more_frames, more_rows = lags[1] - lags[0], places[1] - places[0]
        cells = window(half, lags[0], places[0], frames + more_frames, rows + more_rows)
        block = jnp.concatenate([taps(half, tap, high) for tap in first_taps], 1)
        part = times(cells, block).reshape(frames + more_frames, rows + more_rows, cols, 256)
        add(lags[0], part[:frames, :rows, :, :128], high)
        add(lags[1], part[more_frames:, more_rows:, :, 128:], high)

    for copy in copies(0, own):
        copy.wait()
    two_rows(0, (0, 1), (0, 0), (0, 9))
    two_rows(0, (0, 0), (1, 2), (3, 6))
    everything = slice(0, C)
    part = times(window(0, 1, 1, count=2), taps(0, 12, everything, 2))
    add(1, part.reshape(frames, rows, cols, C), everything)
    for copy in copies(1, own):
        copy.wait()
    part = times(window(1, 1, 1, first=2, count=1), taps(1, 1, everything, 1))
    add(1, part.reshape(frames, rows, cols, C), everything)
    two_rows(1, (1, 2), (2, 2), (2, 11))
    two_rows(1, (2, 2), (0, 1), (5, 8))

    finish(scalars, total, tail, out)


def finish_norm(scalars, total, tail, out):
    for f in range(6):
        data = total[f]
        scale = lax.rsqrt(jnp.mean(data * data, axis=-1, keepdims=True) + 1e-06)
        lifted = data * scale * tail[...]
        out[f] = (lifted * (1.0 / (1.0 + jnp.exp(-lifted)))).astype(jnp.bfloat16)


def finish_add(scalars, total, tail, out):
    for f in range(6):
        summed = tail[f].astype(jnp.float32) + total[f]
        out[f] = jnp.where(f < scalars[1], summed, 0.0).astype(jnp.bfloat16)


def conv(scalars, lag_weights, spread, tail, own, got, finish):
    smem = pl.BlockSpec(memory_space=pltpu.SMEM)
    vmem = pl.BlockSpec(memory_space=pltpu.VMEM)
    return pl.pallas_call(
        lambda *refs: conv_body(*refs, finish=finish),
        out_shape=jax.ShapeDtypeStruct((6, 128, C), jnp.bfloat16),
        in_specs=[smem, smem] + [vmem] * 2 + [pl.BlockSpec(memory_space=pl.ANY)] * 8,
        out_specs=vmem,
        scratch_shapes=[
            pltpu.VMEM((2, HALF, C, C), jnp.bfloat16),
            pltpu.VMEM((6, 128, C), jnp.float32),
            pltpu.SemaphoreType.DMA((2, 4)),
        ],
        compiler_params=pltpu.CompilerParams(vmem_limit_bytes=26 * 1024 * 1024),
        cost_estimate=pl.CostEstimate(flops=1000, bytes_accessed=1000, transcendentals=0),
    )(scalars, lag_weights, spread, tail, *own, *got)


def clip_positions(clip_lengths, frame_index):
    ends = jnp.cumsum(clip_lengths)
    begins = jnp.max(jnp.where(ends[None, :] <= frame_index[:, None], ends[None, :], 0), axis=1)
    return frame_index - begins


def norm_act(values, gain):
    data = values.astype(jnp.float32)
    mean_square = jnp.mean(data * data, axis=-1, keepdims=True)
    scaled = data * lax.rsqrt(mean_square + 1e-06)
    return jax.nn.silu(scaled * gain).astype(jnp.bfloat16)


def before_in_group(z, y, x, c):
    group = z * NY + y - 1
    return None if group < 0 else (group // NY, group % NY, x, c)


def across_chips(z, y, x, c):
    x = x - 1 if c == 0 else x + 1
    return (z, y, x, 1 - c) if 0 <= x < NX else None


def across_and_before(z, y, x, c):
    place = across_chips(z, y, x, c)
    return None if place is None else before_in_group(*place)


def per_device(
    frames, clip_lengths, group_start, group_count, kernel_one, kernel_two, gain_one, gain_two
):
    slots = frames.shape[0]
    slot = jnp.arange(slots, dtype=jnp.int32)
    position = clip_positions(clip_lengths, group_start[0] + slot)
    lag_weights = jnp.stack([position >= 2, position >= 1, position >= 0]).astype(jnp.float32)
    scalars = jnp.stack([lax.axis_index("c").astype(jnp.int32), group_count[0]])
    orders = channel_orders()

    first_core = lax.axis_index("c") == 0
    last = group_count[0] - 2

    def sides(acts):
        return (
            jnp.where(first_core, acts[:, 3:4], acts[:, 0:1]),
            jnp.where(first_core, acts[:, 0:1], acts[:, 3:4]),
        )

    def last_two(acts):
        return lax.dynamic_slice_in_dim(acts, last, 2, 0)

    acts_one = norm_act(frames, gain_one)
    own = jnp.stack([own_half(kernel_one), own_half(kernel_two)])
    pieces = z_stage(own)
    ends = fetch(last_two(acts_one), before_in_group)
    picks = make_picks(orders)
    pieces, picks, lag_weights, scalars = lax.optimization_barrier(
        (pieces, picks, lag_weights, scalars)
    )

    opposite = fetch(pieces, small_source(2))
    after = fetch(pieces, small_source(1))
    parts = [pieces, after, fetch(pieces, small_source(-1)), opposite]
    inner, outer = sides(jnp.concatenate([ends, acts_one], 0))
    across = fetch(outer, across_chips)
    parts, across = lax.optimization_barrier((parts, across))

    one_bundle, two_bundle = join_rows(parts, 0), join_rows(parts, 1)
    one_bundles = bulk_stage(one_bundle)
    one_own, two_own = lax.optimization_barrier((one_bundle, two_bundle))
    one_others, two_others = [fetch(one_own, sibling)], [fetch(two_own, sibling)]
    two_bundle, one_others, two_others, inner = lax.optimization_barrier(
        (two_bundle, one_others, two_others, inner)
    )
    beside = fetch(inner, sibling)
    spread = spread_halo(scalars, picks, ends, beside, across, spread_inner(picks, acts_one))
    one_bundles, one_others, two_others, spread = lax.optimization_barrier(
        (one_bundles, one_others, two_others, spread)
    )
    one_others += [fetch(b, sibling) for b in one_bundles[1:]]

    two_bundles = bulk_stage(two_bundle)
    acts_two = conv(
        scalars, lag_weights, spread, gain_two.reshape(1, C), one_bundles, one_others, finish_norm
    ).reshape(frames.shape)

    inner, outer = sides(acts_two)
    ends, corners, outer = lax.optimization_barrier((last_two(acts_two), last_two(outer), outer))
    ends = fetch(ends, before_in_group)
    across = fetch(outer, across_chips)
    corners, two_bundles = lax.optimization_barrier((corners, two_bundles))
    corners = fetch(corners, across_and_before)
    spread = spread_inner(picks, acts_two)
    ends, corners, across, spread, two_bundles = lax.optimization_barrier(
        (ends, corners, across, spread, two_bundles)
    )
    beside = fetch(jnp.concatenate([sides(ends)[0], inner], 0), sibling)
    two_others.append(fetch(two_bundles[1], sibling))
    two_last, beside = lax.optimization_barrier((two_bundles[2:], beside))
    two_others += [fetch(b, sibling) for b in two_last]
    across = jnp.concatenate([corners, across], 0)
    spread = spread_halo(scalars, picks, ends, beside, across, spread)
    result = conv(
        scalars, lag_weights, spread, frames.reshape(slots, 128, C), two_bundles, two_others,
        finish_add,
    )
    return result.reshape(frames.shape)


def solution(mesh):
    torus = Mesh(mesh.devices.reshape(NZ, NY, NX, NC), AXES)
    group, row = ("z", "y"), ("x", "c")
    return jax.shard_map(
        per_device,
        mesh=torus,
        in_specs=(
            P(group, row, None, None),
            P(),
            P(group),
            P(group),
            P(None, None, None, group, None),
            P(None, None, None, group, None),
            P(),
            P(),
        ),
        out_specs=P(group, row, None, None),
        check_vma=False,
    )
```
